32 devices in a mesh: dp: 8 (over y, x, core), mp: 4 (over z).
Axes of the slice: x: 2, y: 2, z: 4, core: 2. Of those that a mesh axis runs over, the one named last changes fastest.
Arguments:
- query_stream: bfloat16 [16384, 512], P('dp'), may hold values from -6 to 6
- content_stream: bfloat16 [16384, 512], P('dp'), may hold values from -6 to 6
- encoder: bfloat16 [32768, 512], P('dp'), may hold values from -6 to 6
- dec_segments: int32 [16, 1024], P('dp'), may hold values from 0 to 3, never falling along the last dimension, each value on 1 to 512 neighbouring positions
- enc_segments: int32 [16, 2048], P('dp'), may hold values from 0 to 3, never falling along the last dimension, each value on 1 to 1024 neighbouring positions
- key_rank: int32 [16, 1024], P('dp'), may hold values from 0 to 1023
- observe_limit: int32 [16, 1024], P('dp'), may hold values from 0 to 1024
- padding: int32 [16, 1024], P('dp'), may hold values 0 or 1
- self_proj: bfloat16 [3, 512, 512], P(None, None, 'mp'), may hold values from -0.25 to 0.25
- self_bias: bfloat16 [2, 512], P(None, 'mp'), may hold values from -1.75 to 1.75
- self_out: bfloat16 [512, 512], P('mp'), may hold values from -1 to 1
- cross_proj: bfloat16 [3, 512, 512], P(None, None, 'mp'), may hold values from -0.25 to 0.25
- cross_bias: bfloat16 [2, 512], P(None, 'mp'), may hold values from -1.75 to 1.75
- cross_out: bfloat16 [512, 512], P('mp'), may hold values from -1.5 to 1.5
- ffn_in: bfloat16 [512, 2048], P(None, 'mp'), may hold values from -0.25 to 0.25
- ffn_in_bias: bfloat16 [2048], P('mp'), may hold values from -1.75 to 1.75
- ffn_out: bfloat16 [2048, 512], P('mp'), may hold values from -0.1875 to 0.1875
- out_bias: bfloat16 [3, 512], replicated, may hold values from -1.75 to 1.75
- norm_gain: bfloat16 [3, 512], replicated, may hold values from 0.099609375 to 1.8984375
- norm_bias: bfloat16 [3, 512], replicated, may hold values from -1.75 to 1.75
- cotangent: bfloat16 [16384, 512], P(('dp', 'mp')), may hold values from -6 to 6
Outputs:
- output: bfloat16 [16384, 512], P(('dp', 'mp'))
- query_grad: bfloat16 [16384, 512], P(('dp', 'mp'))
- content_grad: bfloat16 [16384, 512], P(('dp', 'mp'))
- encoder_grad: bfloat16 [32768, 512], P(('dp', 'mp'))
- self_proj_grad: float32 [3, 512, 512], P(None, None, 'mp')
- self_bias_grad: float32 [2, 512], P(None, 'mp')
- self_out_grad: float32 [512, 512], P('mp')
- cross_proj_grad: float32 [3, 512, 512], P(None, None, 'mp')
- cross_bias_grad: float32 [2, 512], P(None, 'mp')
- cross_out_grad: float32 [512, 512], P('mp')
- ffn_in_grad: float32 [512, 2048], P(None, 'mp')
- ffn_in_bias_grad: float32 [2048], P('mp')
- ffn_out_grad: float32 [2048, 512], P('mp')
- out_bias_grad: float32 [3, 512], replicated
- norm_gain_grad: float32 [3, 512], replicated
- norm_bias_grad: float32 [3, 512], replicated
The draws below stay inside these ranges and needn't reach their ends.
Inputs may be any that keep to these rules, and one draw needn't show every extreme that they name: Every sentence pair number below 4 occurs in every row of both dec_segments and enc_segments.
All inputs are finite; a program needn't handle non-finite values. No bound on the sum of `padding` on one device may be relied on, other than what follows from the above.
Results may differ from the reference program's by a relative error of at most 0.028.
The reference program's roundings to bfloat16 on the way count: a program that leaves them out, or rounds other values in their place, can miss the bound.
Values may be sent and summed in bfloat16 or wider, within the bound.
No kernel may reach another device: no remote copies, remote signals or barrier semaphores. Data moves between devices by JAX's collectives and lax.ppermute only.
A program may use at most 192 MiB of HBM per device.

```python
import math
import jax
import jax.numpy as jnp
import numpy as np
from jax import lax

D = 512
HEADS = 8
HEAD = 64
FF = 2048
SEQ_LEN = 1024
SRC_LEN = 2048
SEGS = 4
SEQS = 16
TOKENS = 16384
SOURCES = 32768


def touch_ends(values, rng, least, top_value):
    longest = values.shape.index(max(values.shape))
    spots = []
    for shift in (0, 1):
        where = [jax.random.randint(jax.random.fold_in(rng, axis), (), 0, length) for axis, length in enumerate(values.shape)]
        where[longest] = (where[longest] + shift) % values.shape[longest]
        spots.append(tuple(where))
    return values.at[spots[0]].set(least).at[spots[1]].set(top_value)


def block_scale(stream_key, extent, pieces, least, high):
    level = 1.0
    for position, shards_of in pieces:
        heights = jax.random.uniform(jax.random.fold_in(jax.random.fold_in(stream_key, 6), position), (shards_of,), jnp.float32, least / len(pieces), high / len(pieces))
        level = level * jnp.repeat(jnp.exp(heights), extent[position] // shards_of).reshape((-1,) + (1,) * (len(extent) - 1 - position))
    return level


def split_up(number_of, total, most, lean):
    portions = [(1 << 20) // math.isqrt(standing ** lean) + 1 for standing in range(2, number_of + 1)]
    surplus, counts = total - most - (number_of - 1), [1] * (number_of - 1)
    while surplus > 0:
        candidates = [i for i in range(number_of - 1) if counts[i] < most]
        whole, remaining = sum([portions[i] for i in candidates]), surplus
        for i in candidates:
            addition = min(most - counts[i], max(1, remaining * portions[i] // whole), surplus)
            counts[i] = counts[i] + addition
            surplus = surplus - addition
    return np.array([most] + counts)


def ragged_sizes(key, number_of, total, most, lean):
    if number_of == 2:
        one = jax.random.randint(key, (), max(1, total - most), min(most, total - 1) + 1)
        return jnp.stack([one, total - one])
    lengths = jnp.asarray(split_up(number_of, total, most, lean), jnp.int32)
    couples = (number_of - 1) // 2
    donor, taker = lengths[1:1 + 2 * couples:2], lengths[2:2 + 2 * couples:2]
    margin = jnp.minimum(donor - 1, most - taker)
    shifted = jax.random.randint(jax.random.fold_in(key, 1), (couples,), 0, 1 << 20) % (margin + 1)
    lengths = lengths.at[1:1 + 2 * couples:2].set(donor - shifted).at[2:2 + 2 * couples:2].set(taker + shifted)
    return lengths[jax.random.permutation(jax.random.fold_in(key, 2), number_of)]


def bell_draw(key, dims, scale, bound, split=(), kind=jnp.bfloat16):
    values = scale * jax.random.normal(key, dims, jnp.float32)
    if split:
        values = values * block_scale(key, dims, split, -0.22, 0.18)
    return jnp.clip(values, -bound, bound).astype(kind)


def setup_inputs(seed: int = 0) -> dict:
    splits = jax.random.split(jax.random.key(seed), 22)
    query_stream = bell_draw(splits[0], (TOKENS, D), 1.0, 6.0, ((0, 8),))
    content_stream = bell_draw(splits[1], (TOKENS, D), 1.0, 6.0, ((0, 8),))
    encoder = bell_draw(splits[2], (SOURCES, D), 1.0, 6.0, ((0, 8),))
    dec_segments = jax.vmap(lambda own: jnp.searchsorted(jnp.cumsum(ragged_sizes(own, SEGS, SEQ_LEN, SEQ_LEN // 2, 1)), jnp.arange(SEQ_LEN), side="right"))(jax.random.split(splits[3], SEQS)).reshape((SEQS, SEQ_LEN)).astype(jnp.int32)
    enc_segments = jax.vmap(lambda own: jnp.searchsorted(jnp.cumsum(ragged_sizes(own, SEGS, SRC_LEN, SRC_LEN // 2, 1)), jnp.arange(SRC_LEN), side="right"))(jax.random.split(splits[4], SEQS)).reshape((SEQS, SRC_LEN)).astype(jnp.int32)
    key_rank = touch_ends(jax.random.randint(splits[5], (SEQS, SEQ_LEN), 0, SEQ_LEN), jax.random.fold_in(splits[5], 1), 0, SEQ_LEN - 1).astype(jnp.int32)
    observe_limit = touch_ends(jax.random.randint(splits[6], (SEQS, SEQ_LEN), 0, SEQ_LEN + 1), jax.random.fold_in(splits[6], 1), 0, SEQ_LEN).astype(jnp.int32)
    padding = touch_ends((jax.random.randint(splits[7], (SEQS, SEQ_LEN), 0, 8) < 1).astype(jnp.int32), jax.random.fold_in(splits[7], 1), 0, 1)
    self_proj = bell_draw(splits[8], (3, D, D), D ** -0.5, 0.25, ((2, 4),))
    self_bias = bell_draw(splits[9], (2, D), 0.3, 1.75, ((1, 4),))
    self_out = bell_draw(splits[10], (D, D), (D // 16) ** -0.5, 1.0, ((0, 4),))
    cross_proj = bell_draw(splits[11], (3, D, D), D ** -0.5, 0.25, ((2, 4),))
    cross_bias = bell_draw(splits[12], (2, D), 0.3, 1.75, ((1, 4),))
    cross_out = bell_draw(splits[13], (D, D), (D // 32) ** -0.5, 1.5, ((0, 4),))
    ffn_in = bell_draw(splits[14], (D, FF), D ** -0.5, 0.25, ((1, 4),))
    ffn_in_bias = bell_draw(splits[15], (FF,), 0.3, 1.75, ((0, 4),))
    ffn_out = bell_draw(splits[16], (FF, D), (FF // 2) ** -0.5, 0.1875, ((0, 4),))
    out_bias = bell_draw(splits[17], (3, D), 0.3, 1.75)
    norm_gain = jnp.clip(1.0 + 0.18 * jax.random.normal(splits[18], (3, D), jnp.float32), 0.099609375, 1.8984375).astype(jnp.bfloat16)
    norm_bias = bell_draw(splits[19], (3, D), 0.3, 1.75)
    cotangent = bell_draw(splits[20], (TOKENS, D), 1.0, 6.0, ((0, 32),))
    return dict(query_stream=query_stream, content_stream=content_stream, encoder=encoder, dec_segments=dec_segments, enc_segments=enc_segments, key_rank=key_rank, observe_limit=observe_limit, padding=padding, self_proj=self_proj, self_bias=self_bias, self_out=self_out, cross_proj=cross_proj, cross_bias=cross_bias, cross_out=cross_out, ffn_in=ffn_in, ffn_in_bias=ffn_in_bias, ffn_out=ffn_out, out_bias=out_bias, norm_gain=norm_gain, norm_bias=norm_bias, cotangent=cotangent)


@jax.custom_vjp
def low(v):
    return lax.optimization_barrier(v.astype(jnp.bfloat16)).astype(jnp.float32)

@jax.custom_vjp
def low_back(v):
    return v

def low_keep(v):
    return (low(v), None)

def low_pass(kept, grad):
    return (grad,)

def back_keep(v):
    return (v, None)

def back_low(kept, grad):
    return (low(grad),)
low.defvjp(low_keep, low_pass)
low_back.defvjp(back_keep, back_low)
EPSILON = 1e-05
MASKED = -1000000000.0
HIGHEST = lax.Precision.HIGHEST

def both_ways(value):
    return low(low_back(value))

def matmul(left, right):
    return jnp.dot(left, right, precision=HIGHEST)

def layer_norm(summed, gain, shift):
    average = lax.optimization_barrier(jnp.mean(summed, axis=-1, keepdims=True))
    centred = summed - average
    inverse = lax.rsqrt(lax.optimization_barrier(jnp.mean(centred * centred, axis=-1, keepdims=True)) + EPSILON)
    return centred * inverse * gain + shift

def self_visible(segments, ranks, limits, padded):
    length = segments.shape[0]
    starts = jnp.concatenate([jnp.ones((1,), dtype=bool), segments[1:] != segments[:-1]])
    places = jnp.arange(length, dtype=jnp.int32)
    chosen = (ranks[None, :] < limits[:, None]) & (padded[None, :] == 0) & (places[:, None] != places[None, :])
    return (segments[:, None] == segments[None, :]) & (starts[None, :] | chosen)

def attend(queries, keys, values, visible):
    query_rows = queries.shape[0]
    key_rows = keys.shape[0]
    query_heads = queries.reshape(query_rows, HEADS, HEAD)
    key_heads = keys.reshape(key_rows, HEADS, HEAD)
    value_heads = values.reshape(key_rows, HEADS, HEAD)
    raw_scores = low_back(jnp.einsum('lhd,shd->hls', query_heads, key_heads, precision=HIGHEST))
    scores = jnp.where(visible[None], raw_scores * HEAD ** (-0.5), MASKED)
    weights = jax.nn.softmax(scores, axis=-1)
    mixed = jnp.einsum('hls,shd->lhd', low(weights), value_heads, precision=HIGHEST)
    return mixed.reshape(query_rows, HEADS * HEAD)

def self_sequence(entry):
    queries, keys, values, segments, ranks, limits, padded = entry
    return attend(queries, keys, values, self_visible(segments, ranks, limits, padded))

def cross_sequence(entry):
    queries, keys, values, segments, sources = entry
    return attend(queries, keys, values, segments[:, None] == sources[None, :])

def forward(integers, query, content, encoded, self_proj, self_bias, self_out, cross_proj, cross_bias, cross_out, ffn_in, ffn_in_bias, ffn_out, out_bias, norm_gain, norm_bias):
    dec_segments, enc_segments, key_rank, observe_limit, padding = integers
    rows = dec_segments.shape[0]
    width = query.shape[1]
    queries = both_ways(matmul(query, self_proj[0]) + self_bias[0])
    keys = both_ways(matmul(content, self_proj[1]))
    values = both_ways(matmul(content, self_proj[2]) + self_bias[1])
    mixed = lax.map(jax.checkpoint(self_sequence), (queries.reshape(rows, SEQ_LEN, width), keys.reshape(rows, SEQ_LEN, width), values.reshape(rows, SEQ_LEN, width), dec_segments, key_rank, observe_limit, padding))
    context = both_ways(mixed.reshape(-1, width))
    branch = low_back(matmul(context, self_out) + out_bias[0])
    first = layer_norm(query + branch, norm_gain[0], norm_bias[0])
    cross_queries = both_ways(matmul(low(first), cross_proj[0]) + cross_bias[0])
    cross_keys = both_ways(matmul(encoded, cross_proj[1]))
    cross_values = both_ways(matmul(encoded, cross_proj[2]) + cross_bias[1])
    cross_mixed = lax.map(jax.checkpoint(cross_sequence), (cross_queries.reshape(rows, SEQ_LEN, width), cross_keys.reshape(rows, SRC_LEN, width), cross_values.reshape(rows, SRC_LEN, width), dec_segments, enc_segments))
    cross_context = both_ways(cross_mixed.reshape(-1, width))
    cross_branch = low_back(matmul(cross_context, cross_out) + out_bias[1])
    second = layer_norm(first + cross_branch, norm_gain[1], norm_bias[1])
    pre = low_back(matmul(low(second), ffn_in) + ffn_in_bias)
    hidden = low(jax.nn.gelu(pre))
    ffn_branch = low_back(matmul(hidden, ffn_out) + out_bias[2])
    return layer_norm(second + ffn_branch, norm_gain[2], norm_bias[2])

def reference(query_stream, content_stream, encoder, dec_segments, enc_segments, key_rank, observe_limit, padding, self_proj, self_bias, self_out, cross_proj, cross_bias, cross_out, ffn_in, ffn_in_bias, ffn_out, out_bias, norm_gain, norm_bias, cotangent):
    integers = (dec_segments, enc_segments, key_rank, observe_limit, padding)
    floats = tuple((item.astype(jnp.float32) for item in (query_stream, content_stream, encoder, self_proj, self_bias, self_out, cross_proj, cross_bias, cross_out, ffn_in, ffn_in_bias, ffn_out, out_bias, norm_gain, norm_bias)))

    def run(*values_in):
        return forward(integers, *values_in)
    output, pull = jax.vjp(run, *floats)
    grads = pull(cotangent.astype(jnp.float32))
    return (output.astype(jnp.bfloat16), grads[0].astype(jnp.bfloat16), grads[1].astype(jnp.bfloat16), grads[2].astype(jnp.bfloat16), grads[3], grads[4], grads[5], grads[6], grads[7], grads[8], grads[9], grads[10], grads[11], grads[12], grads[13], grads[14])
```

```python
import functools
import math

import jax
import jax.numpy as jnp
from jax import lax
from jax.experimental import pallas as pl
from jax.experimental.pallas import tpu as pltpu
from jax.sharding import PartitionSpec as P

HEAD = 64
EPSILON = 1e-05
MASKED = -1000000000.0
LOG2E = math.log2(math.e)
D = 512
PAIR = 128
PAIRS = 4
OWN = 512
TQ = 128
TK = 256
TILES = OWN // TQ
SUB = 8
EXT = 16
BF = jnp.bfloat16
F32 = jnp.float32
VMEM_LIMIT = 56 * 1024 * 1024


def mm(left, right):
    return jnp.dot(left, right, preferred_element_type=F32)


def mm_rows(left, right):
    return lax.dot_general(left, right, (((0,), (0,)), ((), ())), preferred_element_type=F32)


def mm_cols(left, right):
    return lax.dot_general(left, right, (((1,), (1,)), ((), ())), preferred_element_type=F32)


def norm_parts(summed):
    average = jnp.mean(summed, axis=-1, keepdims=True)
    centred = summed - average
    inverse = lax.rsqrt(jnp.mean(centred * centred, axis=-1, keepdims=True) + EPSILON)
    return centred * inverse, inverse


def norm_backward(incoming, normed, inverse, gain):
    scaled = incoming * gain
    inner = (
        scaled
        - jnp.mean(scaled, axis=-1, keepdims=True)
        - normed * jnp.mean(scaled * normed, axis=-1, keepdims=True)
    )
    return inner * inverse


def col_sum(values):
    return jnp.sum(values.astype(F32), axis=0, keepdims=True)


def half_lanes(rows):
    return lax.broadcasted_iota(jnp.int32, (rows, PAIR), 1) < HEAD


def stack_heads(values):
    keep = half_lanes(values.shape[0])
    zero = jnp.zeros_like(values)
    return jnp.concatenate([jnp.where(keep, values, zero), jnp.where(keep, zero, values)], axis=0)


def pieces_of(value, first_lane, base):
    lane = lax.broadcasted_iota(jnp.int32, value.shape, 1)
    high = value.astype(BF)
    rest = value - high.astype(F32)
    middle = rest.astype(BF)
    low = (rest - middle.astype(F32)).astype(BF)
    out = jnp.where(lane == first_lane, high, base)
    out = jnp.where(lane == first_lane + 1, middle, out)
    return jnp.where(lane == first_lane + 2, low, out)


def lanes(pair):
    return slice(pair * PAIR, (pair + 1) * PAIR)


def key_range(scal, which, tile):
    base = pl.multiple_of(scal[2 + which * 2 * TILES + tile], PAIR)
    count = scal[2 + which * 2 * TILES + TILES + tile]
    return base, count


def attend_forward(scal, which, q, k, v, kaug, hot, mask, score, peak, mixed, qaug, ctx, exact):
    def tile_body(tile, carry):
        base, count = key_range(scal, which, tile)
        rows = pl.ds(pl.multiple_of(tile * TQ, TQ), TQ)
        extra = hot[rows, :]
        extra2 = jnp.concatenate([extra, extra], axis=0)
        peak[...] = jnp.full(peak.shape, -jnp.inf, F32)
        mixed[...] = jnp.zeros(mixed.shape, F32)

        def scores(step, carry):
            off = pl.multiple_of(base + step * TK, PAIR)
            here = pl.ds(pl.multiple_of(step * TK, TK), TK)
            ka = kaug[pl.ds(off, TK), :]
            if mask is not None:
                block = mask[rows, pl.ds(off, TK)]
                block = jnp.concatenate([block, block], axis=0)
            for pair in range(PAIRS):
                q2 = jnp.concatenate([stack_heads(q[rows, lanes(pair)]), extra2], axis=1)
                kk = jnp.concatenate([k[pl.ds(off, TK), lanes(pair)], ka], axis=1)
                s = mm_cols(q2, kk)
                if mask is not None:
                    s = s + block
                score[pair, :, here] = s
                top = peak[pair]
                for part in range(TK // PAIR):
                    top = jnp.maximum(top, s[:, part * PAIR : (part + 1) * PAIR])
                peak[pair] = top
            return carry

        lax.fori_loop(0, count, scores, 0)
        for pair in range(PAIRS):
            peak[pair] = jnp.broadcast_to(
                jnp.max(peak[pair], axis=1, keepdims=True), (2 * TQ, PAIR)
            )

        def weights(step, carry):
            off = pl.multiple_of(base + step * TK, PAIR)
            here = pl.ds(pl.multiple_of(step * TK, TK), TK)
            minus = jnp.full((TK, PAIR), -1.0, BF)
            for pair in range(PAIRS):
                top = jnp.concatenate([peak[pair]] * (TK // PAIR), axis=1)
                p = jnp.exp2((score[pair, :, here] - top) * LOG2E).astype(BF)
                vv = jnp.concatenate([v[pl.ds(off, TK), lanes(pair)], minus], axis=1)
                mixed[pair] += mm(p, vv)
            return carry

        lax.fori_loop(0, count, weights, 0)
        keep = half_lanes(TQ)
        for pair in range(PAIRS):
            both = mixed[pair]
            total = -both[:, PAIR:]
            normal = both[:, :PAIR] / total
            out = jnp.where(keep, normal[:TQ], normal[TQ:])
            exact[rows, lanes(pair)] = out
            ctx[rows, lanes(pair)] = out.astype(BF)
            logsum = peak[pair] + jnp.log(total)
            for head in range(2):
                part = logsum[head * TQ : (head + 1) * TQ]
                qaug[2 * pair + head, rows, :] = pieces_of(part, 4, extra)
        return carry

    lax.fori_loop(0, TILES, tile_body, 0)


def attend_backward(scal, which, q, k, v, kaug, qaug, mask_t, grad, exact, dq, dk, dv, dq_tile):
    dk[...] = jnp.zeros(dk.shape, F32)
    dv[...] = jnp.zeros(dv.shape, F32)

    def tile_body(tile, carry):
        base, count = key_range(scal, which, tile)
        start = pl.multiple_of(tile * TQ, TQ)
        rows = pl.ds(start, TQ)
        dq_tile[...] = jnp.zeros(dq_tile.shape, F32)
        keep = half_lanes(TQ)
        grads, queries, grad_aug, query_aug = [], [], [], []
        for pair in range(PAIRS):
            g = grad[rows, lanes(pair)]
            inner = g.astype(F32) * exact[rows, lanes(pair)]
            first = jnp.sum(jnp.where(keep, inner, 0.0), axis=1, keepdims=True)
            second = jnp.sum(jnp.where(keep, 0.0, inner), axis=1, keepdims=True)
            delta = jnp.broadcast_to(jnp.concatenate([first, second], axis=0), (2 * TQ, PAIR))
            aug = pieces_of(delta, 0, jnp.zeros((2 * TQ, PAIR), BF))
            g2 = stack_heads(g)
            q2 = stack_heads(q[rows, lanes(pair)])
            grads.append(g2)
            queries.append(q2)
            grad_aug.append(jnp.concatenate([g2, aug], axis=1))
            qa = jnp.concatenate([qaug[2 * pair, rows, :], qaug[2 * pair + 1, rows, :]], axis=0)
            query_aug.append(jnp.concatenate([q2, qa], axis=1))

        def keys(step, carry):
            off = pl.multiple_of(base + step * TK, PAIR)
            here = pl.ds(off, TK)
            ka = kaug[here, :]
            minus = jnp.full((TK, PAIR), -1.0, BF)
            if mask_t is not None:
                block = mask_t[here, rows]
                block = jnp.concatenate([block, block], axis=1)
            for pair in range(PAIRS):
                kp = k[here, lanes(pair)]
                s = mm_cols(jnp.concatenate([kp, ka], axis=1), query_aug[pair])
                if mask_t is not None:
                    s = s + block
                p = jnp.exp2(s * LOG2E)
                vp = jnp.concatenate([v[here, lanes(pair)], minus], axis=1)
                ds = (p * mm_cols(vp, grad_aug[pair])).astype(BF)
                dv[here, lanes(pair)] += mm(p.astype(BF), grads[pair])
                dk[here, lanes(pair)] += mm(ds, queries[pair])
                dq_tile[pair] += mm_rows(ds, kp)
            return carry

        lax.fori_loop(0, count, keys, 0)
        for pair in range(PAIRS):
            both = dq_tile[pair] * HEAD ** (-0.5)
            dq[rows, lanes(pair)] = jnp.where(keep, both[:TQ], both[TQ:]).astype(BF)
        return carry

    lax.fori_loop(0, TILES, tile_body, 0)


def load_weights(scal, mine, other, weight, sem):
    core, place = scal[0], scal[1]
    copies = []
    for side, source in ((core, mine), (1 - core, other)):
        for shift in range(4):
            spot = jnp.bitwise_xor(place, shift)
            matrix = 2 * side + spot // 2
            row = pl.multiple_of((spot % 2) * 256, 256)
            for pair in range(PAIRS):
                copies.append(
                    pltpu.make_async_copy(
                        source.at[shift, pair, pl.ds(0, 256), :],
                        weight.at[matrix, pl.ds(row, 256), lanes(pair)],
                        sem.at[len(copies)],
                    )
                )
    return copies


def self_forward_kernel(
    scal, xq, xc, mask, hot, kaug, vecs, mine, other,
    q, k, v, qaug, ctx, exact, s1, weight, bias,
    score, peak, mixed, small, sem,
):
    copies = load_weights(scal, mine, other, weight, sem)
    for pair in range(PAIRS):
        copies.append(pltpu.make_async_copy(mine.at[0, pair, pl.ds(256, EXT), :], small.at[pair], sem.at[len(copies)]))
    for copy in copies:
        copy.start()
    for copy in copies:
        copy.wait()
    for pair in range(PAIRS):
        bias[:, lanes(pair)] = small[pair].astype(F32)
    q[...] = ((mm(xq[...], weight[0]) + bias[0:1, :]).astype(BF) * BF(HEAD ** (-0.5))).astype(BF)
    for part in range(xc.shape[0] // 512):
        rows = slice(part * 512, (part + 1) * 512)
        k[rows, :] = mm(xc[rows, :], weight[1]).astype(BF)
        v[rows, :] = (mm(xc[rows, :], weight[2]) + bias[1:2, :]).astype(BF)
    attend_forward(scal, 0, q, k, v, kaug, hot, mask, score, peak, mixed, qaug, ctx, exact)
    s1[...] = xq[...].astype(F32) + mm_cols(ctx[...], weight[3]) + vecs[0:1, :]


def cross_forward_kernel(
    scal, s1, enc, hot, kaug, vecs, bias, mine, other,
    q, k, v, qaug, ctx, exact, s2, weight,
    score, peak, mixed, sem,
):
    copies = load_weights(scal, mine, other, weight, sem)
    for copy in copies:
        copy.start()
    for copy in copies:
        copy.wait()
    normed, _ = norm_parts(s1[...])
    first = normed * vecs[3:4, :] + vecs[6:7, :]
    q[...] = ((mm(first.astype(BF), weight[0]) + bias[2:3, :]).astype(BF) * BF(HEAD ** (-0.5))).astype(BF)
    for part in range(enc.shape[0] // 512):
        rows = slice(part * 512, (part + 1) * 512)
        k[rows, :] = mm(enc[rows, :], weight[1]).astype(BF)
        v[rows, :] = (mm(enc[rows, :], weight[2]) + bias[3:4, :]).astype(BF)
    attend_forward(scal, 1, q, k, v, kaug, hot, None, score, peak, mixed, qaug, ctx, exact)
    s2[...] = first + mm_cols(ctx[...], weight[3]) + vecs[1:2, :]


def gelu_parts(v):
    c = math.sqrt(2.0 / math.pi)
    square = v * v
    t = jnp.tanh(c * (v + 0.044715 * square * v))
    value = 0.5 * v * (1.0 + t)
    slope = 0.5 * (1.0 + t) + 0.5 * v * (1.0 - t * t) * (c + (3.0 * 0.044715 * c) * square)
    return value, slope


def ffn_kernel(
    scal, s2, cot, bias, vecs, mine, other,
    output, grads, back, sums,
    weight, hidden, slopes, low, sem,
):
    core, place = scal[0], scal[1]
    copies = []
    for side, source in ((core, mine), (1 - core, other)):
        for shift in range(4):
            spot = jnp.bitwise_xor(place, shift)
            row = pl.multiple_of(spot * 128, 128)
            for part in range(4):
                copies.append(
                    pltpu.make_async_copy(
                        source.at[shift, part], weight.at[side, part, pl.ds(row, 128), :],
                        sem.at[len(copies)],
                    )
                )
    for copy in copies:
        copy.start()
    for copy in copies:
        copy.wait()
    sums[...] = jnp.zeros(sums.shape, F32)
    normed2, inverse2 = norm_parts(s2[...])
    second = normed2 * vecs[4:5, :] + vecs[7:8, :]
    low[...] = second.astype(BF)
    total = second + vecs[2:3, :]
    for part in range(4):
        part_bias = jnp.concatenate([bias[4 + i : 5 + i, lanes(part)] for i in range(4)], axis=1)
        pre = mm(low[...], weight[0, part]) + part_bias
        value, slope = gelu_parts(pre)
        hidden[part] = value.astype(BF)
        slopes[part] = slope
        total = total + mm(hidden[part], weight[1, part])
    normed3, inverse3 = norm_parts(total)
    output[...] = (normed3 * vecs[5:6, :] + vecs[8:9, :]).astype(BF)
    incoming = cot[...].astype(F32)
    sums[0:1, :] = col_sum(incoming * normed3)
    sums[1:2, :] = col_sum(incoming)
    third_grad = norm_backward(incoming, normed3, inverse3, vecs[5:6, :])
    branch = third_grad.astype(BF)
    sums[2:3, :] = col_sum(branch)
    total = third_grad
    for part in range(4):
        pre_grad = (slopes[part] * mm_cols(branch, weight[1, part])).astype(BF)
        sums[8 + part : 9 + part, :] = col_sum(pre_grad)
        din = mm_rows(low[...], pre_grad).astype(BF)
        dout = mm_rows(hidden[part], branch).astype(BF)
        for spot in range(4):
            grads[0, spot, part] = din[spot * 128 : (spot + 1) * 128]
            grads[1, spot, part] = dout[spot * 128 : (spot + 1) * 128]
        total = total + mm_cols(pre_grad, weight[0, part])
    sums[3:4, :] = col_sum(total * normed2)
    sums[4:5, :] = col_sum(total)
    second_grad = norm_backward(total, normed2, inverse2, vecs[4:5, :])
    sums[5:6, :] = col_sum(second_grad.astype(BF))
    back[...] = second_grad


def store_grad(grads, matrix, value):
    low = value.astype(BF)
    for half in range(2):
        spot = (matrix % 2) * 2 + half
        for pair in range(PAIRS):
            grads[matrix // 2, spot, pair, 0:256, :] = low[half * 256 : (half + 1) * 256, lanes(pair)]


def projection_grads(grads, x, low, rows_total, matrix):
    total = None
    for part in range(rows_total // 512):
        rows = slice(part * 512, (part + 1) * 512)
        term = mm_rows(x[rows, :], low[rows, :])
        total = term if total is None else total + term
    store_grad(grads, matrix, total)


def cross_backward_kernel(
    scal, dss2, s1, weight, q, k, v, qaug, ctx, exact, enc, kaug, vecs, sums_in,
    grads, enc_grad, back, sums,
    grad_ctx, dq, dk, dv, low, dq_tile,
):
    branch = dss2[...].astype(BF)
    grad_ctx[...] = mm(branch, weight[3]).astype(BF)
    store_grad(grads, 3, mm_rows(branch, ctx[...]))
    attend_backward(scal, 1, q, k, v, kaug, qaug, None, grad_ctx, exact, dq, dk, dv, dq_tile)
    sums[...] = sums_in[...]
    normed, inverse = norm_parts(s1[...])
    first = (normed * vecs[3:4, :] + vecs[6:7, :]).astype(BF)
    sums[14:15, :] = col_sum(dq[...])
    sums[15:16, :] = col_sum(dv[...].astype(BF))
    store_grad(grads, 0, mm_rows(first, dq[...]))
    for part in range(enc.shape[0] // 512):
        rows = slice(part * 512, (part + 1) * 512)
        low[0, rows, :] = dk[rows, :].astype(BF)
        low[1, rows, :] = dv[rows, :].astype(BF)
        enc_grad[rows, :] = (
            mm_cols(low[0, rows, :], weight[1]) + mm_cols(low[1, rows, :], weight[2])
        ).astype(BF)
    projection_grads(grads, enc, low.at[0], enc.shape[0], 1)
    projection_grads(grads, enc, low.at[1], enc.shape[0], 2)
    total = dss2[...] + mm_cols(dq[...], weight[0])
    sums[6:7, :] = col_sum(total * normed)
    sums[7:8, :] = col_sum(total)
    first_grad = norm_backward(total, normed, inverse, vecs[3:4, :])
    sums[12:13, :] = col_sum(first_grad.astype(BF))
    back[...] = first_grad


def self_backward_kernel(
    scal, fsg, weight, q, k, v, qaug, ctx, exact, xq, xc, mask_t, kaug, sums,
    grads, query_grad, content_grad,
    grad_ctx, dq, dk, dv, low, dq_tile,
):
    branch = fsg[...].astype(BF)
    grad_ctx[...] = mm(branch, weight[3]).astype(BF)
    store_grad(grads, 3, mm_rows(branch, ctx[...]))
    attend_backward(scal, 0, q, k, v, kaug, qaug, mask_t, grad_ctx, exact, dq, dk, dv, dq_tile)
    store_grad(grads, 0, mm_rows(xq[...], dq[...]))
    for part in range(xc.shape[0] // 512):
        rows = slice(part * 512, (part + 1) * 512)
        low[0, rows, :] = dk[rows, :].astype(BF)
        low[1, rows, :] = dv[rows, :].astype(BF)
        content_grad[rows, :] = (
            mm_cols(low[0, rows, :], weight[1]) + mm_cols(low[1, rows, :], weight[2])
        ).astype(BF)
    projection_grads(grads, xc, low.at[0], xc.shape[0], 1)
    projection_grads(grads, xc, low.at[1], xc.shape[0], 2)
    query_grad[...] = (fsg[...] + mm_cols(dq[...], weight[0])).astype(BF)
    bias_q = col_sum(dq[...])
    bias_v = col_sum(low[1].astype(F32))
    order = (0, 1, 2, 3, 4, 5, 6, 7, 12)
    for core in range(2):
        for spot in range(4):
            for pair in range(PAIRS):
                number = core * 4 + spot
                rows = []
                if number == 0:
                    rows = [bias_q[:, lanes(pair)], bias_v[:, lanes(pair)]]
                    rows += [sums[14:15, lanes(pair)], sums[15:16, lanes(pair)]]
                    rows += [sums[8 + pair : 9 + pair, lanes(i)] for i in range(4)]
                elif number <= 3:
                    for index in order[(number - 1) * 3 : number * 3]:
                        rows += [sums[index : index + 1, lanes(i)] for i in range(4)]
                rows += [jnp.zeros((EXT - len(rows), PAIR), F32)]
                grads[core, spot, pair, 256 : 256 + EXT, :] = jnp.concatenate(rows, axis=0).astype(BF)


def call(kernel, outs, scratch, inputs, hbm_inputs=(), flops=0):
    specs = [pl.BlockSpec(memory_space=pltpu.SMEM)]
    specs += [
        pl.BlockSpec(memory_space=pl.ANY if index in hbm_inputs else pltpu.VMEM)
        for index in range(1, len(inputs))
    ]
    return pl.pallas_call(
        kernel,
        out_shape=[jax.ShapeDtypeStruct(shape, dtype) for shape, dtype in outs],
        in_specs=specs,
        out_specs=[pl.BlockSpec(memory_space=pltpu.VMEM)] * len(outs),
        scratch_shapes=scratch,
        compiler_params=pltpu.CompilerParams(vmem_limit_bytes=VMEM_LIMIT),
        cost_estimate=pl.CostEstimate(flops=flops, bytes_accessed=8 << 20, transcendentals=0),
    )(*inputs)


def body(
    query_stream, content_stream, encoder, dec_segments, enc_segments, key_rank, observe_limit,
    padding, self_proj, self_bias, self_out, cross_proj, cross_bias, cross_out, ffn_in,
    ffn_in_bias, ffn_out, out_bias, norm_gain, norm_bias, cotangent,
):
    members = lax.axis_size("mp")
    groups = lax.axis_size("dp")
    position = lax.axis_index("mp")
    group = lax.axis_index("dp")
    core = group % 2
    place = (group // 2) % 4
    sequences, length = dec_segments.shape
    sources = enc_segments.shape[1]
    per_row = members // sequences
    row = position // per_row
    part = position % per_row

    def swap(value, axis, mask):
        size = members if axis == "mp" else groups
        return lax.ppermute(value, axis, [(i, i ^ mask) for i in range(size)])

    def gather(shard):
        width = shard.shape[1:]
        own = lax.dynamic_index_in_dim(shard, core * 4 + place, 0, keepdims=False)
        line = jnp.stack([own] + [swap(own, "mp", shift) for shift in range(1, 4)])
        plane = jnp.stack([line] + [swap(line, "dp", 2 * shift) for shift in range(1, 4)])
        return plane, swap(plane, "dp", 1)

    small = jnp.concatenate(
        [self_bias, cross_bias, ffn_in_bias.reshape(4, PAIR), jnp.zeros((8, PAIR), BF)], axis=0
    )
    group1 = jnp.concatenate([self_proj, self_out.T[None]], axis=0).reshape(SUB, 256, PAIR)
    group1 = jnp.concatenate([group1, jnp.broadcast_to(small[None], (SUB, EXT, PAIR))], axis=1)
    group2 = jnp.concatenate([cross_proj, cross_out.T[None]], axis=0).reshape(SUB, 256, PAIR)
    group3 = jnp.concatenate([ffn_in, ffn_out], axis=0).reshape(SUB, 128, D)
    mine1, other1 = gather(group1)
    mine2, other2 = gather(group2)
    mine3, other3 = gather(group3)

    vecs = jnp.concatenate([out_bias, norm_gain, norm_bias, jnp.zeros((7, D), BF)], axis=0).astype(F32)
    seg_dec = lax.dynamic_index_in_dim(dec_segments, row, 0, keepdims=False)
    seg_enc = lax.dynamic_index_in_dim(enc_segments, row, 0, keepdims=False)
    ranks = lax.dynamic_index_in_dim(key_rank, row, 0, keepdims=False)
    limits = lax.dynamic_index_in_dim(observe_limit, row, 0, keepdims=False)
    padded = lax.dynamic_index_in_dim(padding, row, 0, keepdims=False)
    xq = lax.dynamic_slice_in_dim(query_stream, position * OWN, OWN, 0)
    xc = lax.dynamic_slice_in_dim(content_stream, row * length, length, 0)
    enc = lax.dynamic_slice_in_dim(encoder, row * sources, sources, 0)

    starts = jnp.concatenate([jnp.ones((1,), dtype=bool), seg_dec[1:] != seg_dec[:-1]])
    rank_eff = jnp.where(starts, -1, jnp.where(padded == 0, ranks, length))
    own = lambda values: lax.dynamic_slice_in_dim(values, part * OWN, OWN, 0)
    places = jnp.arange(length, dtype=jnp.int32)
    seg_own, limit_own, place_own = own(seg_dec), own(limits), own(places)

    def visible(seg_q, limit_q, place_q, seg_k, rank_k, place_k, start_k):
        return (seg_q == seg_k) & (start_k | ((rank_k < limit_q) & (place_q != place_k)))

    mask = jnp.where(
        visible(
            seg_own[:, None], limit_own[:, None], place_own[:, None],
            seg_dec[None, :], rank_eff[None, :], places[None, :], starts[None, :],
        ),
        0.0, MASKED,
    ).astype(F32)
    mask_t = jnp.where(
        visible(
            seg_own[None, :], limit_own[None, :], place_own[None, :],
            seg_dec[:, None], rank_eff[:, None], places[:, None], starts[:, None],
        ),
        0.0, MASKED,
    ).astype(F32)
    lane = jnp.arange(PAIR, dtype=jnp.int32)[None, :]
    hot = (seg_own[:, None] == lane).astype(BF)

    def key_aug(segments):
        different = (lane < 4) & (segments[:, None] != lane)
        minus = (lane >= 4) & (lane < 7)
        return jnp.where(different, MASKED, jnp.where(minus, -1.0, 0.0)).astype(BF)

    kaug_dec, kaug_enc = key_aug(seg_dec), key_aug(seg_enc)

    def ranges(seg_k):
        low_seg, high_seg = seg_own[::TQ], seg_own[TQ - 1 :: TQ]
        begin = jnp.sum((seg_k[None, :] < low_seg[:, None]).astype(jnp.int32), axis=1)
        end = jnp.sum((seg_k[None, :] <= high_seg[:, None]).astype(jnp.int32), axis=1)
        base = begin // PAIR * PAIR
        count = (end - base + TK - 1) // TK
        base = jnp.minimum(base, seg_k.shape[0] - count * TK)
        return [base, count]

    scal = jnp.concatenate(
        [core[None], place[None]] + ranges(seg_dec) + ranges(seg_enc)
    ).astype(jnp.int32)

    def attention_outs(keys):
        return [
            ((OWN, D), BF), ((keys, D), BF), ((keys, D), BF), ((2 * PAIRS, OWN, PAIR), BF),
            ((OWN, D), BF), ((OWN, D), F32), ((OWN, D), F32), ((4, D, D), BF),
        ]

    def attention_scratch(keys):
        return [
            pltpu.VMEM((PAIRS, 2 * TQ, keys), F32), pltpu.VMEM((PAIRS, 2 * TQ, PAIR), F32),
            pltpu.VMEM((PAIRS, 2 * TQ, 2 * PAIR), F32),
        ]

    def backward_scratch(keys):
        return [
            pltpu.VMEM((OWN, D), BF), pltpu.VMEM((OWN, D), BF), pltpu.VMEM((keys, D), F32),
            pltpu.VMEM((keys, D), F32), pltpu.VMEM((2, keys, D), BF),
            pltpu.VMEM((PAIRS, 2 * TQ, PAIR), F32),
        ]

    q1, k1, v1, qaug1, ctx1, exact1, s1, weight1, bias = call(
        self_forward_kernel,
        attention_outs(length) + [((EXT, D), F32)],
        attention_scratch(length)
        + [pltpu.VMEM((PAIRS, EXT, PAIR), BF), pltpu.SemaphoreType.DMA((36,))],
        (scal, xq, xc, mask, hot, kaug_dec, vecs, mine1, other1),
        (7, 8), 5 * 10**9,
    )
    q2, k2, v2, qaug2, ctx2, exact2, s2, weight2 = call(
        cross_forward_kernel,
        attention_outs(sources),
        attention_scratch(sources) + [pltpu.SemaphoreType.DMA((32,))],
        (scal, s1, enc, hot, kaug_enc, vecs, bias, mine2, other2),
        (7, 8), 8 * 10**9,
    )
    output, grads3, dss2, sums = call(
        ffn_kernel,
        [((OWN, D), BF), ((2, 4, 4, 128, D), BF), ((OWN, D), F32), ((EXT, D), F32)],
        [
            pltpu.VMEM((2, 4, D, D), BF), pltpu.VMEM((4, OWN, D), BF), pltpu.VMEM((4, OWN, D), F32),
            pltpu.VMEM((OWN, D), BF), pltpu.SemaphoreType.DMA((32,)),
        ],
        (scal, s2, cotangent, bias, vecs, mine3, other3),
        (5, 6), 8 * 10**9,
    )
    grads2, enc_part, fsg, sums = call(
        cross_backward_kernel,
        [((2, 4, 4, 256, PAIR), BF), ((sources, D), BF), ((OWN, D), F32), ((EXT, D), F32)],
        backward_scratch(sources),
        (scal, dss2, s1, weight2, q2, k2, v2, qaug2, ctx2, exact2, enc, kaug_enc, vecs, sums),
        (), 15 * 10**9,
    )
    grads1, query_grad, content_part = call(
        self_backward_kernel,
        [((2, 4, 4, 256 + EXT, PAIR), BF), ((OWN, D), BF), ((length, D), BF)],
        backward_scratch(length),
        (scal, fsg, weight1, q1, k1, v1, qaug1, ctx1, exact1, xq, xc, mask_t, kaug_dec, sums),
        (), 10 * 10**9,
    )

    def row_exchange(partial):
        rows = partial.shape[0] // per_row
        blocks = partial.reshape(per_row, rows, D)
        total = lax.dynamic_index_in_dim(blocks, part, 0, keepdims=False).astype(F32)
        for shift in range(1, per_row):
            theirs = lax.dynamic_index_in_dim(blocks, part ^ shift, 0, keepdims=False)
            total = total + swap(theirs, "mp", shift).astype(F32)
        return total.astype(BF)

    def pick(values, index):
        return lax.dynamic_index_in_dim(values, index, 0, keepdims=False)

    def reduce(grads):
        half = pick(grads, core).astype(F32) + swap(pick(grads, 1 - core), "dp", 1).astype(F32)
        half = half.astype(BF)
        quarter = pick(half, place).astype(F32)
        for shift in range(1, 4):
            quarter = quarter + swap(pick(half, place ^ shift), "dp", 2 * shift).astype(F32)
        quarter = quarter.astype(BF)
        piece = quarter[0].astype(F32)
        for shift in range(1, 4):
            piece = piece + swap(quarter[shift], "mp", shift).astype(F32)
        bit = 8
        while bit < groups:
            piece = piece + swap(piece, "dp", bit)
            bit *= 2
        piece = piece.astype(BF)
        line = jnp.stack([piece] + [swap(piece, "dp", 2 * shift) for shift in range(1, 4)])
        line = jnp.stack([pick(line, place ^ shift) for shift in range(4)])
        both = swap(line, "dp", 1)
        return jnp.concatenate(
            [jnp.where(core == 0, line, both), jnp.where(core == 0, both, line)], axis=0
        ).astype(F32)

    encoder_grad = row_exchange(enc_part)
    content_grad = row_exchange(content_part)
    ffn = reduce(grads3).reshape(2, D, D)
    cross = reduce(grads2).reshape(4, D, PAIR)
    own = reduce(grads1)
    ext = own[:4, 256:]
    own = own[:, :256].reshape(4, D, PAIR)
    wide = ext[1:4, :12].reshape(9, D)
    return (
        output,
        query_grad,
        content_grad,
        encoder_grad,
        own[:3],
        ext[0, 0:2],
        own[3].T,
        cross[:3],
        ext[0, 2:4],
        cross[3].T,
        ffn[0],
        ext[0, 4:8].reshape(D),
        ffn[1],
        jnp.stack([wide[8], wide[5], wide[2]]),
        jnp.stack([wide[6], wide[3], wide[0]]),
        jnp.stack([wide[7], wide[4], wide[1]]),
    )


def solution(mesh):
    return jax.shard_map(
        body,
        mesh=mesh,
        in_specs=(
            P("dp", None), P("dp", None), P("dp", None), P("dp", None), P("dp", None),
            P("dp", None), P("dp", None), P("dp", None), P(None, None, "mp"), P(None, "mp"),
            P("mp", None), P(None, None, "mp"), P(None, "mp"), P("mp", None), P(None, "mp"),
            P("mp"), P("mp", None), P(), P(), P(), P(("dp", "mp"), None),
        ),
        out_specs=(
            P(("dp", "mp"), None), P(("dp", "mp"), None), P(("dp", "mp"), None),
            P(("dp", "mp"), None), P(None, None, "mp"), P(None, "mp"), P("mp", None),
            P(None, None, "mp"), P(None, "mp"), P("mp", None), P(None, "mp"), P("mp"),
            P("mp", None), P(), P(), P(),
        ),
        check_vma=False,
    )
```

```python
import math

import jax
import jax.numpy as jnp
from jax import lax
from jax.experimental import pallas as pl
from jax.experimental.pallas import tpu as pltpu
from jax.sharding import PartitionSpec as P

HEAD = 64
EPSILON = 1e-05
MASKED = -1000000000.0
LOG2E = math.log2(math.e)
D = 512
PAIR = 128
PAIRS = 4
OWN = 512
TQ = 128
ROW_TILES = 8
TK = 256
TILES = OWN // TQ
SUB = 8
EXT = 16
BF = jnp.bfloat16
F32 = jnp.float32
VMEM_LIMIT = 56 * 1024 * 1024


def mm(left, right):
    return jnp.dot(left, right, preferred_element_type=F32)


def mm_rows(left, right):
    return lax.dot_general(left, right, (((0,), (0,)), ((), ())), preferred_element_type=F32)


def mm_cols(left, right):
    return lax.dot_general(left, right, (((1,), (1,)), ((), ())), preferred_element_type=F32)


def norm_parts(summed):
    average = jnp.mean(summed, axis=-1, keepdims=True)
    centred = summed - average
    inverse = lax.rsqrt(jnp.mean(centred * centred, axis=-1, keepdims=True) + EPSILON)
    return centred * inverse, inverse


def norm_backward(incoming, normed, inverse, gain):
    scaled = incoming * gain
    inner = (
        scaled
        - jnp.mean(scaled, axis=-1, keepdims=True)
        - normed * jnp.mean(scaled * normed, axis=-1, keepdims=True)
    )
    return inner * inverse


def col_sum(values):
    return jnp.sum(values.astype(F32), axis=0, keepdims=True)


def half_lanes(rows):
    return lax.broadcasted_iota(jnp.int32, (rows, PAIR), 1) < HEAD


def stack_heads(values):
    keep = half_lanes(values.shape[0])
    zero = jnp.zeros_like(values)
    return jnp.concatenate([jnp.where(keep, values, zero), jnp.where(keep, zero, values)], axis=0)


def pieces_of(value, first_lane, base):
    lane = lax.broadcasted_iota(jnp.int32, value.shape, 1)
    high = value.astype(BF)
    rest = value - high.astype(F32)
    middle = rest.astype(BF)
    low = (rest - middle.astype(F32)).astype(BF)
    out = jnp.where(lane == first_lane, high, base)
    out = jnp.where(lane == first_lane + 1, middle, out)
    return jnp.where(lane == first_lane + 2, low, out)


def lanes(pair):
    return slice(pair * PAIR, (pair + 1) * PAIR)


def key_range(scal, which, tile):
    base = pl.multiple_of(scal[2 + which * 2 * TILES + tile], PAIR)
    count = scal[2 + which * 2 * TILES + TILES + tile]
    return base, count


def over_keys(count, block):
    done = 0
    for wide in (4, 2, 1):
        whole = (count - done) // wide

        def step(index, carry, done=done, wide=wide):
            block((done + index * wide) * TK, wide * TK)
            return carry

        lax.fori_loop(0, whole, step, 0)
        done = done + whole * wide


def attend_forward(scal, which, q, k, v, kaug, hot, mask, score, peak, mixed, qaug, ctx, exact):
    def tile_body(tile, carry):
        base, count = key_range(scal, which, tile)
        rows = pl.ds(pl.multiple_of(tile * TQ, TQ), TQ)
        extra = hot[rows, :]
        extra2 = jnp.concatenate([extra, extra], axis=0)
        peak[...] = jnp.full(peak.shape, -jnp.inf, F32)
        mixed[...] = jnp.zeros(mixed.shape, F32)

        def scores(begin, size):
            off = pl.multiple_of(base + begin, PAIR)
            here = pl.ds(pl.multiple_of(begin, TK), size)
            ka = kaug[pl.ds(off, size), :]
            if mask is not None:
                block = mask[rows, pl.ds(off, size)]
                block = jnp.concatenate([block, block], axis=0)
            for pair in range(PAIRS):
                q2 = jnp.concatenate([stack_heads(q[rows, lanes(pair)]), extra2], axis=1)
                kk = jnp.concatenate([k[pl.ds(off, size), lanes(pair)], ka], axis=1)
                s = mm_cols(q2, kk)
                if mask is not None:
                    s = s + block
                score[pair, :, here] = s
                top = peak[pair]
                for part in range(size // PAIR):
                    top = jnp.maximum(top, s[:, part * PAIR : (part + 1) * PAIR])
                peak[pair] = top

        over_keys(count, scores)
        for pair in range(PAIRS):
            peak[pair] = jnp.broadcast_to(
                jnp.max(peak[pair], axis=1, keepdims=True), (2 * TQ, PAIR)
            )

        def weights(begin, size):
            off = pl.multiple_of(base + begin, PAIR)
            here = pl.ds(pl.multiple_of(begin, TK), size)
            minus = jnp.full((size, PAIR), -1.0, BF)
            for pair in range(PAIRS):
                top = jnp.concatenate([peak[pair]] * (size // PAIR), axis=1)
                p = jnp.exp2((score[pair, :, here] - top) * LOG2E).astype(BF)
                vv = jnp.concatenate([v[pl.ds(off, size), lanes(pair)], minus], axis=1)
                mixed[pair] += mm(p, vv)

        over_keys(count, weights)
        keep = half_lanes(TQ)
        for pair in range(PAIRS):
            both = mixed[pair]
            total = -both[:, PAIR:]
            normal = both[:, :PAIR] / total
            out = jnp.where(keep, normal[:TQ], normal[TQ:])
            exact[rows, lanes(pair)] = out
            ctx[rows, lanes(pair)] = out.astype(BF)
            logsum = peak[pair] + jnp.log(total)
            for head in range(2):
                part = logsum[head * TQ : (head + 1) * TQ]
                qaug[2 * pair + head, rows, :] = pieces_of(part, 4, extra)
        return carry

    lax.fori_loop(0, TILES, tile_body, 0)


def attend_backward(scal, which, q, k, v, kaug, qaug, mask_t, grad, exact, dq, dk, dv, dq_tile):
    def tile_body(tile, carry):
        base, count = key_range(scal, which, tile)
        start = pl.multiple_of(tile * TQ, TQ)
        rows = pl.ds(start, TQ)
        dq_tile[...] = jnp.zeros(dq_tile.shape, F32)
        keep = half_lanes(TQ)
        grads, queries, grad_aug, query_aug = [], [], [], []
        for pair in range(PAIRS):
            g = grad[rows, lanes(pair)]
            inner = g.astype(F32) * exact[rows, lanes(pair)]
            first = jnp.sum(jnp.where(keep, inner, 0.0), axis=1, keepdims=True)
            second = jnp.sum(jnp.where(keep, 0.0, inner), axis=1, keepdims=True)
            delta = jnp.broadcast_to(jnp.concatenate([first, second], axis=0), (2 * TQ, PAIR))
            aug = pieces_of(delta, 0, jnp.zeros((2 * TQ, PAIR), BF))
            g2 = stack_heads(g)
            q2 = stack_heads(q[rows, lanes(pair)])
            grads.append(g2)
            queries.append(q2)
            grad_aug.append(jnp.concatenate([g2, aug], axis=1))
            qa = jnp.concatenate([qaug[2 * pair, rows, :], qaug[2 * pair + 1, rows, :]], axis=0)
            query_aug.append(jnp.concatenate([q2, qa], axis=1))

        def keys(begin, size):
            off = pl.multiple_of(base + begin, PAIR)
            here = pl.ds(off, size)
            ka = kaug[here, :]
            minus = jnp.full((size, PAIR), -1.0, BF)
            if mask_t is not None:
                block = mask_t[here, rows]
                block = jnp.concatenate([block, block], axis=1)
            for pair in range(PAIRS):
                kp = k[here, lanes(pair)]
                s = mm_cols(jnp.concatenate([kp, ka], axis=1), query_aug[pair])
                if mask_t is not None:
                    s = s + block
                p = jnp.exp2(s * LOG2E)
                vp = jnp.concatenate([v[here, lanes(pair)], minus], axis=1)
                ds = (p * mm_cols(vp, grad_aug[pair])).astype(BF)
                dv[here, lanes(pair)] += mm(p.astype(BF), grads[pair])
                dk[here, lanes(pair)] += mm(ds, queries[pair])
                dq_tile[pair] += mm_rows(ds, kp)

        over_keys(count, keys)
        for pair in range(PAIRS):
            both = dq_tile[pair] * HEAD ** (-0.5)
            dq[rows, lanes(pair)] = jnp.where(keep, both[:TQ], both[TQ:]).astype(BF)
        return carry

    lax.fori_loop(0, TILES, tile_body, 0)


def mesh_place():
    group = lax.axis_index("dp")
    return group % 2, (group // 2) % 4, lax.axis_index("mp")


def run_copies(copies):
    for copy in copies:
        copy.start()
    for copy in copies:
        copy.wait()


def load_weights(proj, out, mine, other, weight, sem):
    core, place, _ = mesh_place()
    copies = []
    for matrix in range(3):
        copies.append(
            pltpu.make_async_copy(
                proj.at[matrix], weight.at[matrix, :, lanes(0)], sem.at[len(copies)]
            )
        )
    for side, source in ((core, mine), (1 - core, other)):
        for shift in range(4):
            spot = jnp.bitwise_xor(place, shift)
            matrix = 2 * side + spot // 2
            row = pl.multiple_of((spot % 2) * 256, 256)
            for pair in range(1, PAIRS):
                copies.append(
                    pltpu.make_async_copy(
                        source.at[shift, pair - 1, pl.ds(0, 256), :],
                        weight.at[matrix, pl.ds(row, 256), lanes(pair)],
                        sem.at[len(copies)],
                    )
                )
    weight[3, :, lanes(0)] = out[...].astype(F32).T.astype(BF)
    return copies


def put(source, target, sem):
    copy = pltpu.make_async_copy(source, target, sem)
    copy.start()
    return copy


def own_tiles(source, target, sem, first):
    _, _, position = mesh_place()
    copies = []
    for tile in range(TILES):
        row = pl.multiple_of((position // 2 * ROW_TILES + 2 * tile + position % 2) * TQ, TQ)
        copies.append(
            pltpu.make_async_copy(
                source.at[pl.ds(row, TQ), :], target.at[tile * TQ : (tile + 1) * TQ, :],
                sem.at[first + tile],
            )
        )
    return copies


def send_grads(buffer, mine, theirs, sem):
    core, place, _ = mesh_place()
    chunk = buffer.shape[1] // SUB
    copies = []
    for side, target in ((core, mine), (1 - core, theirs)):
        for shift in range(4):
            row = pl.multiple_of((4 * side + jnp.bitwise_xor(place, shift)) * chunk, 16)
            copies.append(
                pltpu.make_async_copy(
                    buffer.at[:, pl.ds(row, chunk), :], target.at[shift], sem.at[len(copies)]
                )
            )
    run_copies(copies)


def send_rows(buffer, keep, theirs, sem):
    part = lax.axis_index("mp") % 2
    rows = buffer.shape[0] // 2
    copies = []
    for side, target in ((part, keep), (1 - part, theirs)):
        row = pl.multiple_of(side * rows, 16)
        copies.append(
            pltpu.make_async_copy(buffer.at[pl.ds(row, rows), :], target, sem.at[len(copies)])
        )
    run_copies(copies)


def pack_kernel(
    self_proj, self_out, cross_proj, cross_out, ffn_in, ffn_out, self_bias, cross_bias, ffn_bias, cot,
    own, own3, cot_send, small,
):
    core, place, position = mesh_place()
    for index in range(2):
        row = pl.multiple_of((1 - position % 2 + 2 * index) * TQ, TQ)
        cot_send[index * TQ : (index + 1) * TQ, :] = cot[pl.ds(row, TQ), :]
    chunk = 4 * core + place
    matrix, half = chunk // 2, chunk % 2
    for proj, out, base in ((self_proj, self_out, 0), (cross_proj, cross_out, 256 + EXT)):

        @pl.when(matrix < 3)
        def _(proj=proj, base=base):
            own[base : base + 256, :] = proj[matrix, pl.ds(pl.multiple_of(half * 256, 256), 256), :]

        @pl.when(matrix == 3)
        def _(out=out, base=base):
            block = out[:, pl.ds(pl.multiple_of(half * 256, 256), 256)]
            own[base : base + 256, :] = block.astype(F32).T.astype(BF)

    rows = [self_bias[...].astype(F32), cross_bias[...].astype(F32)]
    rows += [ffn_bias[:, lanes(block)].astype(F32) for block in range(4)]
    rows += [jnp.zeros((8, PAIR), F32)]
    small[...] = jnp.concatenate(rows, axis=0).astype(BF)
    own[256 : 256 + EXT, :] = small[...]
    rows = own3.shape[0]
    row = lax.axis_index("dp") * rows

    @pl.when(row < D)
    def _():
        own3[...] = ffn_in[pl.ds(pl.multiple_of(row, rows), rows), :]

    @pl.when(row >= D)
    def _():
        own3[...] = ffn_out[pl.ds(pl.multiple_of(row - D, rows), rows), :]


def prep_kernel(
    dec, enc, ranks, limits, padded, out_bias, gain, shift,
    scal, mask, mask_t, hot, kaug_dec, kaug_enc, vecs, table,
):
    _, _, position = mesh_place()
    row, part = position // 2, position % 2
    length, sources = dec.shape[1], enc.shape[1]
    seg = dec[pl.ds(row, 1), :]
    seg_enc = enc[pl.ds(row, 1), :]
    place = lax.broadcasted_iota(jnp.int32, (1, length), 1)
    begins = (place == 0) | (seg != pltpu.roll(seg, 1, 1))
    rank = jnp.where(padded[pl.ds(row, 1), :] == 0, ranks[pl.ds(row, 1), :], length)
    table[...] = jnp.zeros(table.shape, F32)
    table[0:1, :] = seg.astype(F32)
    table[1:2, :] = rank.astype(F32)
    table[2:3, :] = begins.astype(F32)
    table[3:4, :] = limits[pl.ds(row, 1), :].astype(F32)
    table[4:5, :] = place.astype(F32)
    own = jnp.concatenate(
        [
            table[:, pl.ds(pl.multiple_of((2 * tile + part) * TQ, TQ), TQ)]
            for tile in range(TILES)
        ],
        axis=1,
    )
    own_t = own.T
    every = table[...]
    every_t = every.T

    def visible(seg_q, limit_q, place_q, seg_k, rank_k, start_k, place_k):
        chosen = (rank_k < limit_q) & (place_q != place_k)
        return jnp.where((seg_q == seg_k) & ((start_k > 0.5) | chosen), 0.0, MASKED)

    mask[...] = visible(
        own_t[:, 0:1], own_t[:, 3:4], own_t[:, 4:5],
        every[0:1], every[1:2], every[2:3], every[4:5],
    )
    mask_t[...] = visible(
        own[0:1], own[3:4], own[4:5],
        every_t[:, 0:1], every_t[:, 1:2], every_t[:, 2:3], every_t[:, 4:5],
    )

    def key_aug(column):
        lane = lax.broadcasted_iota(jnp.int32, (column.shape[0], PAIR), 1)
        different = (lane < 4) & (column != lane.astype(F32))
        minus = (lane >= 4) & (lane < 7)
        return jnp.where(different, MASKED, jnp.where(minus, -1.0, 0.0)).astype(BF)

    kaug_dec[...] = key_aug(every_t[:, 0:1])
    seg_enc_f = jnp.broadcast_to(seg_enc.astype(F32), (8, sources))
    kaug_enc[...] = key_aug(seg_enc_f.T[:, 0:1])
    lane = lax.broadcasted_iota(jnp.int32, (OWN, PAIR), 1)
    hot[...] = (own_t[:, 0:1] == lane.astype(F32)).astype(F32).astype(BF)
    vecs[...] = jnp.zeros(vecs.shape, F32)
    for index, source in enumerate((out_bias, gain, shift)):
        vecs[3 * index : 3 * index + 3, :] = source[...].astype(F32)
    scal[0] = 0
    scal[1] = 0
    for which, keys in ((0, every[0:1]), (1, seg_enc_f[0:1])):
        size = keys.shape[1]
        for tile in range(TILES):
            block = own[0:1, tile * TQ : (tile + 1) * TQ]
            low, high = jnp.min(block), jnp.max(block)
            begin = jnp.sum((keys < low).astype(F32)).astype(jnp.int32)
            end = jnp.sum((keys <= high).astype(F32)).astype(jnp.int32)
            base = begin // PAIR * PAIR
            count = (end - base + TK - 1) // TK
            scal[2 + which * 2 * TILES + tile] = jnp.minimum(base, size - count * TK)
            scal[2 + which * 2 * TILES + TILES + tile] = count


def fetch(source, target, start, sem):
    return pltpu.make_async_copy(
        source.at[pl.ds(pl.multiple_of(start, target.shape[0]), target.shape[0]), :], target, sem
    )


def project(x, weight, bias, target):
    for part in range(x.shape[0] // 512):
        rows = slice(part * 512, (part + 1) * 512)
        value = mm(x[rows, :], weight)
        target[rows, :] = (value if bias is None else value + bias).astype(BF)


def self_forward_kernel(
    scal, query, content, mask_in, hot, kaug, vecs, small, proj, out, mine, other,
    q, k_out, v_out, qaug, ctx, exact, s1, weight_out, bias,
    score, peak, mixed, got, xq, xc, k, v, weight, mask, sem, sem_out,
):
    _, _, position = mesh_place()
    rows = xc.shape[0]
    copies = own_tiles(query, xq, sem, 32)
    copies.append(
        pltpu.make_async_copy(
            content.at[pl.ds(pl.multiple_of(position // 2 * rows, rows), rows), :], xc, sem.at[36]
        )
    )
    for pair in range(1, PAIRS):
        copies.append(
            pltpu.make_async_copy(
                mine.at[0, pair - 1, pl.ds(256, EXT), :], got.at[pair - 1], sem.at[36 + pair]
            )
        )
    late = pltpu.make_async_copy(mask_in, mask, sem.at[40])
    for copy in copies:
        copy.start()
    moves = load_weights(proj, out, mine, other, weight, sem)
    for copy in moves:
        copy.start()
    late.start()
    for copy in copies + moves:
        copy.wait()
    outs = [put(weight, weight_out, sem_out.at[0])]
    bias[:, lanes(0)] = small[...].astype(F32)
    for pair in range(1, PAIRS):
        bias[:, lanes(pair)] = got[pair - 1].astype(F32)
    q[...] = ((mm(xq[...], weight[0]) + bias[0:1, :]).astype(BF) * BF(HEAD ** (-0.5))).astype(BF)
    project(xc, weight[1], None, k)
    outs.append(put(k, k_out, sem_out.at[1]))
    project(xc, weight[2], bias[1:2, :], v)
    outs.append(put(v, v_out, sem_out.at[2]))
    late.wait()
    attend_forward(scal, 0, q, k, v, kaug, hot, mask, score, peak, mixed, qaug, ctx, exact)
    s1[...] = xq[...].astype(F32) + mm_cols(ctx[...], weight[3]) + vecs[0:1, :]
    for copy in outs:
        copy.wait()


def cross_forward_kernel(
    scal, s1, encoder, hot, kaug, vecs, bias, proj, out, mine, other,
    q, k_out, v_out, qaug, ctx, exact, s2, weight_out,
    score, peak, mixed, enc, k, v, weight, sem, sem_out,
):
    _, _, position = mesh_place()
    moves = load_weights(proj, out, mine, other, weight, sem)
    rows = enc.shape[0]
    late = pltpu.make_async_copy(
        encoder.at[pl.ds(pl.multiple_of(position // 2 * rows, rows), rows), :], enc, sem.at[32]
    )
    for copy in moves:
        copy.start()
    late.start()
    normed, _ = norm_parts(s1[...])
    first = normed * vecs[3:4, :] + vecs[6:7, :]
    for copy in moves:
        copy.wait()
    outs = [put(weight, weight_out, sem_out.at[0])]
    q[...] = (
        (mm(first.astype(BF), weight[0]) + bias[2:3, :]).astype(BF) * BF(HEAD ** (-0.5))
    ).astype(BF)
    late.wait()
    project(enc, weight[1], None, k)
    outs.append(put(k, k_out, sem_out.at[1]))
    project(enc, weight[2], bias[3:4, :], v)
    outs.append(put(v, v_out, sem_out.at[2]))
    attend_forward(scal, 1, q, k, v, kaug, hot, None, score, peak, mixed, qaug, ctx, exact)
    s2[...] = first + mm_cols(ctx[...], weight[3]) + vecs[1:2, :]
    for copy in outs:
        copy.wait()


def gelu_parts(v):
    c = math.sqrt(2.0 / math.pi)
    square = v * v
    t = jnp.tanh(c * (v + 0.044715 * square * v))
    value = 0.5 * v * (1.0 + t)
    slope = 0.5 * (1.0 + t) + 0.5 * v * (1.0 - t * t) * (c + (3.0 * 0.044715 * c) * square)
    return value, slope


def ffn_kernel(
    s2, cot_own, cot_got, bias, vecs, gathered,
    output, mine, theirs, back, sums, output_send,
    weight, hidden, slopes, low, grads, cot, sem, sem_cot,
):
    _, _, position = mesh_place()
    half = position % 2
    late = []
    for index in range(2):
        row = pl.multiple_of((half + 2 * index) * TQ, TQ)
        target = pl.multiple_of((2 * half + index) * TQ, TQ)
        late.append(
            put(cot_own.at[pl.ds(row, TQ), :], cot.at[pl.ds(target, TQ), :], sem_cot.at[index])
        )
    target = pl.multiple_of((1 - half) * 2 * TQ, 2 * TQ)
    late.append(put(cot_got, cot.at[pl.ds(target, 2 * TQ), :], sem_cot.at[2]))
    copies = []
    for part in range(4):
        for side in range(2):
            row = pl.multiple_of(jnp.bitwise_xor(position, part) * 2 * D + side * D, D)
            copies.append(
                pltpu.make_async_copy(
                    gathered.at[pl.ds(row, D), :], weight.at[side, part], sem.at[len(copies)]
                )
            )
    for copy in copies:
        copy.start()
    sums[...] = jnp.zeros(sums.shape, F32)
    normed2, inverse2 = norm_parts(s2[...])
    second = normed2 * vecs[4:5, :] + vecs[7:8, :]
    low[...] = second.astype(BF)
    total = second + vecs[2:3, :]
    for part in range(4):
        part_bias = jnp.concatenate([bias[4 + i : 5 + i, lanes(part)] for i in range(4)], axis=1)
        copies[2 * part].wait()
        copies[2 * part + 1].wait()
        pre = mm(low[...], weight[0, part]) + part_bias
        value, slope = gelu_parts(pre)
        hidden[part] = value.astype(BF)
        slopes[part] = slope
        total = total + mm(hidden[part], weight[1, part])
    normed3, inverse3 = norm_parts(total)
    output[...] = (normed3 * vecs[5:6, :] + vecs[8:9, :]).astype(BF)
    for copy in late:
        copy.wait()
    row = pl.multiple_of((1 - half) * 2 * TQ, 2 * TQ)
    output_send[...] = output[pl.ds(row, 2 * TQ), :]
    incoming = cot[...].astype(F32)
    sums[0:1, :] = col_sum(incoming * normed3)
    sums[1:2, :] = col_sum(incoming)
    third_grad = norm_backward(incoming, normed3, inverse3, vecs[5:6, :])
    branch = third_grad.astype(BF)
    sums[2:3, :] = col_sum(branch)
    total = third_grad
    for part in range(4):
        pre_grad = (slopes[part] * mm_cols(branch, weight[1, part])).astype(BF)
        sums[8 + part : 9 + part, :] = col_sum(pre_grad)
        grads[part, 0:D, :] = mm_rows(low[...], pre_grad).astype(BF)
        grads[part, D : 2 * D, :] = mm_rows(hidden[part], branch).astype(BF)
        total = total + mm_cols(pre_grad, weight[0, part])
    sums[3:4, :] = col_sum(total * normed2)
    sums[4:5, :] = col_sum(total)
    second_grad = norm_backward(total, normed2, inverse2, vecs[4:5, :])
    sums[5:6, :] = col_sum(second_grad.astype(BF))
    back[...] = second_grad
    send_grads(grads, mine, theirs, sem)


def store_grad(grads, matrix, value):
    low = value.astype(BF)
    for pair in range(PAIRS):
        grads[pair, matrix * D : (matrix + 1) * D, :] = low[:, lanes(pair)]


def projection_grads(grads, x, low, matrix):
    total = None
    for part in range(x.shape[0] // 512):
        rows = slice(part * 512, (part + 1) * 512)
        term = mm_rows(x[rows, :], low[rows, :])
        total = term if total is None else total + term
    store_grad(grads, matrix, total)


def input_grads(dk, dv, weight, out):
    for part in range(dk.shape[0] // 512):
        rows = slice(part * 512, (part + 1) * 512)
        out[rows, :] = (
            mm_cols(dk[rows, :], weight[1]) + mm_cols(dv[rows, :], weight[2])
        ).astype(BF)


def load_all(sources, targets, sem):
    copies = [
        pltpu.make_async_copy(source, target, sem.at[index])
        for index, (source, target) in enumerate(zip(sources, targets))
    ]
    for copy in copies:
        copy.start()
    return copies


def store_low(dk, dv, dk_low, dv_low, low, sem):
    copies = []
    for index, (value, target) in enumerate(((dk, dk_low), (dv, dv_low))):
        for part in range(value.shape[0] // 512):
            rows = slice(part * 512, (part + 1) * 512)
            low[index, rows, :] = value[rows, :].astype(BF)
            copies.append(put(low.at[index, rows, :], target.at[rows, :], sem.at[len(copies)]))
    return copies


def cross_attention_grad_kernel(
    scal, dss2, weight_in, q_in, k_in, v_in, qaug_in, exact_in, kaug_in,
    dq, dk_low, dv_low, keep, send,
    grad_ctx, weight, enc_grad, dk, dv, dq_tile, low, q, k, v, qaug, exact, kaug, sem,
):
    first = put(weight_in, weight, sem.at[7])
    copies = load_all(
        (q_in, qaug_in, exact_in, kaug_in, k_in, v_in), (q, qaug, exact, kaug, k, v), sem
    )
    dk[...] = jnp.zeros(dk.shape, F32)
    dv[...] = jnp.zeros(dv.shape, F32)
    first.wait()
    grad_ctx[...] = mm(dss2[...].astype(BF), weight[3]).astype(BF)
    for copy in copies:
        copy.wait()
    attend_backward(scal, 1, q, k, v, kaug, qaug, None, grad_ctx, exact, dq, dk, dv, dq_tile)
    copies = store_low(dk, dv, dk_low, dv_low, low, sem)
    input_grads(low.at[0], low.at[1], weight, enc_grad)
    for copy in copies:
        copy.wait()
    send_rows(enc_grad, keep, send, sem)


def cross_projection_grad_kernel(
    dss2, s1, weight, self_weight, ctx, self_ctx, dq, dk, dv, encoder, vecs, sums_in,
    mine, theirs, back, grad_ctx, sums,
    grads, enc, sem,
):
    _, _, position = mesh_place()
    copy = fetch(encoder, enc, position // 2 * enc.shape[0], sem.at[0])
    copy.start()
    sums[...] = sums_in[...]
    normed, inverse = norm_parts(s1[...])
    first = (normed * vecs[3:4, :] + vecs[6:7, :]).astype(BF)
    total = dss2[...] + mm_cols(dq[...], weight[0])
    sums[6:7, :] = col_sum(total * normed)
    sums[7:8, :] = col_sum(total)
    first_grad = norm_backward(total, normed, inverse, vecs[3:4, :])
    branch = first_grad.astype(BF)
    sums[12:13, :] = col_sum(branch)
    back[...] = first_grad
    grad_ctx[...] = mm(branch, self_weight[3]).astype(BF)
    store_grad(grads, 4, mm_rows(branch, self_ctx[...]))
    store_grad(grads, 3, mm_rows(dss2[...].astype(BF), ctx[...]))
    sums[14:15, :] = col_sum(dq[...])
    sums[15:16, :] = col_sum(dv[...])
    store_grad(grads, 0, mm_rows(first, dq[...]))
    copy.wait()
    projection_grads(grads, enc, dk, 1)
    projection_grads(grads, enc, dv, 2)
    send_grads(grads, mine, theirs, sem)


def self_attention_grad_kernel(
    scal, grad_ctx, q_in, k_in, v_in, qaug_in, exact_in, mask_in, kaug_in,
    dq, dk_low, dv_low,
    dk, dv, dq_tile, low, q, k, v, qaug, exact, mask_t, kaug, sem,
):
    copies = load_all(
        (q_in, qaug_in, exact_in, kaug_in, k_in, v_in, mask_in),
        (q, qaug, exact, kaug, k, v, mask_t),
        sem,
    )
    dk[...] = jnp.zeros(dk.shape, F32)
    dv[...] = jnp.zeros(dv.shape, F32)
    for copy in copies:
        copy.wait()
    attend_backward(scal, 0, q, k, v, kaug, qaug, mask_t, grad_ctx, exact, dq, dk, dv, dq_tile)
    for copy in store_low(dk, dv, dk_low, dv_low, low, sem):
        copy.wait()


def self_projection_grad_kernel(
    fsg, weight, dq, dk, dv, query, content, sums,
    mine, theirs, keep, send, query_grad,
    grads, content_grad, xq, xc, sem,
):
    _, _, position = mesh_place()
    half = position % 2
    rows = xc.shape[0]
    copies = own_tiles(query, xq, sem, 0)
    copies.append(
        pltpu.make_async_copy(
            content.at[pl.ds(pl.multiple_of(position // 2 * rows, rows), rows), :], xc, sem.at[4]
        )
    )
    run_copies(copies)
    store_grad(grads, 0, mm_rows(xq[...], dq[...]))
    projection_grads(grads, xc, dk, 1)
    projection_grads(grads, xc, dv, 2)
    bias_q = col_sum(dq[...])
    bias_v = col_sum(dv[...])
    for pair in range(PAIRS):
        parts = [bias_q[:, lanes(pair)], bias_v[:, lanes(pair)]]
        parts += [sums[14:15, lanes(pair)], sums[15:16, lanes(pair)]]
        parts += [sums[8 + pair : 9 + pair, lanes(i)] for i in range(4)]
        for index in (0, 1, 2, 3, 4, 5, 6, 7, 12):
            parts += [sums[index : index + 1, lanes(i)] for i in range(4)]
        parts += [jnp.zeros((SUB * EXT - len(parts), PAIR), F32)]
        grads[pair, 3 * D : 3 * D + SUB * EXT, :] = jnp.concatenate(parts, axis=0).astype(BF)
    send_grads(grads, mine, theirs, sem)
    input_grads(dk, dv, weight, content_grad)
    query_grad[...] = (fsg[...] + mm_cols(dq[...], weight[0])).astype(BF)
    mid = rows // 2
    keep[...] = content_grad[pl.ds(pl.multiple_of(half * mid, mid), mid), :]
    send[0:mid, :] = content_grad[pl.ds(pl.multiple_of((1 - half) * mid, mid), mid), :]
    row = pl.multiple_of((1 - half) * 2 * TQ, 2 * TQ)
    send[mid:, :] = query_grad[pl.ds(row, 2 * TQ), :]


def add_split_kernel(mine, theirs, *outs):
    for index, out in enumerate(outs):
        out[...] = (mine[index].astype(F32) + theirs[index].astype(F32)).astype(BF)


def sum_split_kernel(own, first, second, third, *outs):
    for index, out in enumerate(outs):
        out[...] = (
            (own[index].astype(F32) + first[index].astype(F32))
            + (second[index].astype(F32) + third[index].astype(F32))
        ).astype(BF)


def sum_merge_kernel(a0, a1, a2, a3, b0, b1, b2, b3, *outs):
    rows = a0.shape[1]
    for index, out in enumerate(outs):
        for group, spot in (((a0, a1, a2, a3), slice(0, rows)), ((b0, b1, b2, b3), slice(rows, None))):
            own, first, second, third = [part[index].astype(F32) for part in group]
            out[spot, :] = ((own + first) + (second + third)).astype(BF)


def sum_kernel(own, first, second, third, out):
    out[...] = (
        (own[...].astype(F32) + first[...].astype(F32))
        + (second[...].astype(F32) + third[...].astype(F32))
    ).astype(out.dtype)


def finish_kernel(
    ffn, ffn_other, line, other, output_own, output_got, query_own, keep, got,
    self_proj, self_bias, self_out, cross_proj, cross_bias, cross_out, ffn_in, ffn_bias, ffn_out,
    out_bias, gain, moved, output, query, content, wide_ffn, flat, flat_self,
):
    core, place, position = mesh_place()
    half = position % 2
    mid = keep.shape[0]
    for own, theirs, skip, target in (
        (output_own, output_got, 0, output), (query_own, got, mid, query)
    ):
        for index in range(2):
            row = pl.multiple_of((2 * half + index) * TQ, TQ)
            place_own = pl.multiple_of((half + 2 * index) * TQ, TQ)
            place_got = pl.multiple_of((1 - half + 2 * index) * TQ, TQ)
            first = skip + index * TQ
            target[pl.ds(place_own, TQ), :] = own[pl.ds(row, TQ), :]
            target[pl.ds(place_got, TQ), :] = theirs[first : first + TQ, :]
    content[...] = (keep[...].astype(F32) + got[0:mid, :].astype(F32)).astype(BF)
    cross_rows, self_rows = flat.shape[0] // SUB, flat_self.shape[0] // SUB
    for side, source, dense in ((core, line, ffn), (1 - core, other, ffn_other)):
        for shift in range(4):
            spot = 4 * side + jnp.bitwise_xor(place, shift)
            row = pl.multiple_of(spot * 128, 128)
            wide_ffn[pl.ds(row, 128), :] = dense[shift].astype(F32)
            row = pl.multiple_of(spot * cross_rows, 8)
            flat[pl.ds(row, cross_rows), :] = source[shift, 0:cross_rows, :].astype(F32)
            row = pl.multiple_of(spot * self_rows, 8)
            flat_self[pl.ds(row, self_rows), :] = source[shift, cross_rows:, :].astype(F32)
    ffn_in[...] = wide_ffn[0:D, :]
    ffn_out[...] = wide_ffn[D:, :]
    for matrix in range(3):
        cross_proj[matrix] = flat[matrix * D : (matrix + 1) * D, :]
        self_proj[matrix] = flat_self[matrix * D : (matrix + 1) * D, :]
    cross_out[...] = flat[3 * D : 4 * D, :].T
    self_out[...] = flat[4 * D : 5 * D, :].T
    start = 3 * D
    self_bias[...] = flat_self[start : start + 2, :]
    cross_bias[...] = flat_self[start + 2 : start + 4, :]
    for block in range(4):
        ffn_bias[:, lanes(block)] = flat_self[start + 4 + block : start + 5 + block, :]
    for target, order in ((out_bias, (8, 5, 2)), (gain, (6, 3, 0)), (moved, (7, 4, 1))):
        for index, number in enumerate(order):
            for block in range(4):
                row = start + 8 + number * 4 + block
                target[index : index + 1, lanes(block)] = flat_self[row : row + 1, :]


def call(kernel, outs, inputs, scratch=(), smem_in=(), any_in=(), any_out=(), smem_out=(), long=False):
    def space(index, smem, hbm):
        return pltpu.SMEM if index in smem else pl.ANY if index in hbm else pltpu.VMEM

    return pl.pallas_call(
        kernel,
        out_shape=[jax.ShapeDtypeStruct(shape, dtype) for shape, dtype in outs],
        in_specs=[
            pl.BlockSpec(memory_space=space(index, smem_in, any_in)) for index in range(len(inputs))
        ],
        out_specs=[
            pl.BlockSpec(memory_space=space(index, smem_out, any_out)) for index in range(len(outs))
        ],
        scratch_shapes=list(scratch),
        compiler_params=pltpu.CompilerParams(vmem_limit_bytes=VMEM_LIMIT),
        cost_estimate=pl.CostEstimate(
            flops=10**13 if long else 10**6, bytes_accessed=1 << (30 if long else 14),
            transcendentals=0,
        ),
    )(*inputs)


def after(value, *others):
    flat, tree = jax.tree.flatten(value)
    tied = lax.optimization_barrier(tuple(flat) + tuple(others))
    return jax.tree.unflatten(tree, tied[: len(flat)])


def body(
    query_stream, content_stream, encoder, dec_segments, enc_segments, key_rank, observe_limit,
    padding, self_proj, self_bias, self_out, cross_proj, cross_bias, cross_out, ffn_in,
    ffn_in_bias, ffn_out, out_bias, norm_gain, norm_bias, cotangent,
):
    members = lax.axis_size("mp")
    groups = lax.axis_size("dp")
    length = dec_segments.shape[1]
    sources = enc_segments.shape[1]
    DMA = pltpu.SemaphoreType.DMA

    def swap(value, axis, mask):
        size = members if axis == "mp" else groups
        return lax.ppermute(value, axis, [(i, i ^ mask) for i in range(size)])

    def along(values):
        return [swap(value, "mp", shift + 1) for shift, value in enumerate(values)]

    def across(values):
        return [swap(value, "dp", 2 * shift + 2) for shift, value in enumerate(values)]

    own12, own3, cot_send, small = call(
        pack_kernel,
        [
            ((512 + EXT, PAIR), BF), ((2 * D // groups, D), BF), ((2 * TQ, D), BF),
            ((EXT, PAIR), BF),
        ],
        (
            self_proj, self_out, cross_proj, cross_out, ffn_in, ffn_out, self_bias, cross_bias,
            ffn_in_bias.reshape(1, D), cotangent,
        ),
    )
    gathered = lax.all_gather(own3, ("mp", "dp"), axis=0, tiled=True)
    line12 = along([own12] * 3)
    scal, mask, mask_t, hot, kaug_dec, kaug_enc, vecs = call(
        prep_kernel,
        [
            ((2 + 4 * TILES,), jnp.int32), ((OWN, length), F32), ((length, OWN), F32),
            ((OWN, PAIR), BF), ((length, PAIR), BF), ((sources, PAIR), BF), ((EXT, D), F32),
        ],
        (
            dec_segments, enc_segments, key_rank, observe_limit, padding, out_bias, norm_gain,
            norm_bias,
        ),
        [pltpu.VMEM((8, length), F32)],
        smem_out=(0,),
    )
    line12, hot = after((line12, hot))
    line1 = jnp.stack([value[: 256 + EXT] for value in line12])
    line2 = jnp.stack([value[256 + EXT :] for value in line12])
    plane1 = jnp.stack([line1] + across([line1] * 3))
    other1 = swap(plane1, "dp", 1)
    cot_got = swap(after(cot_send, line1), "mp", 1)
    plane2 = across([after(line2, plane1)] * 3)

    def attention_outs(keys):
        return [
            ((OWN, D), BF), ((keys, D), BF), ((keys, D), BF), ((2 * PAIRS, OWN, PAIR), BF),
            ((OWN, D), BF), ((OWN, D), F32), ((OWN, D), F32), ((4, D, D), BF),
        ]

    def attention_scratch(keys):
        return [
            pltpu.VMEM((PAIRS, 2 * TQ, keys), F32), pltpu.VMEM((PAIRS, 2 * TQ, PAIR), F32),
            pltpu.VMEM((PAIRS, 2 * TQ, 2 * PAIR), F32),
        ]

    def backward_scratch(keys, masked=False):
        shapes = [
            pltpu.VMEM((keys, D), F32), pltpu.VMEM((keys, D), F32),
            pltpu.VMEM((PAIRS, 2 * TQ, PAIR), F32), pltpu.VMEM((2, keys, D), BF),
            pltpu.VMEM((OWN, D), BF), pltpu.VMEM((keys, D), BF), pltpu.VMEM((keys, D), BF),
            pltpu.VMEM((2 * PAIRS, OWN, PAIR), BF), pltpu.VMEM((OWN, D), F32),
        ]
        if masked:
            shapes.append(pltpu.VMEM((keys, OWN), F32))
        return shapes + [pltpu.VMEM((keys, PAIR), BF), DMA((8,))]

    q1, k1, v1, qaug1, ctx1, exact1, s1, weight1, bias = call(
        self_forward_kernel,
        attention_outs(length) + [((EXT, D), F32)],
        (
            scal, query_stream, content_stream, mask, hot, kaug_dec, vecs, small, self_proj,
            self_out, plane1, other1,
        ),
        attention_scratch(length)
        + [
            pltpu.VMEM((PAIRS - 1, EXT, PAIR), BF), pltpu.VMEM((OWN, D), BF),
            pltpu.VMEM((length, D), BF), pltpu.VMEM((length, D), BF), pltpu.VMEM((length, D), BF),
            pltpu.VMEM((4, D, D), BF), pltpu.VMEM((OWN, length), F32), DMA((41,)), DMA((3,)),
        ],
        smem_in=(0,), any_in=(1, 2, 3, 8, 10, 11), any_out=(1, 2, 7),
    )
    plane2, s1 = after((plane2, s1))
    plane2 = jnp.stack([line2] + plane2)
    other2 = swap(plane2, "dp", 1)
    q2, k2, v2, qaug2, ctx2, exact2, s2, weight2 = call(
        cross_forward_kernel,
        attention_outs(sources),
        (
            scal, s1, encoder, hot, kaug_enc, vecs, bias, cross_proj, cross_out, plane2, other2,
        ),
        attention_scratch(sources)
        + [
            pltpu.VMEM((sources, D), BF), pltpu.VMEM((sources, D), BF), pltpu.VMEM((sources, D), BF),
            pltpu.VMEM((4, D, D), BF), DMA((33,)), DMA((3,)),
        ],
        smem_in=(0,), any_in=(2, 7, 9, 10), any_out=(1, 2, 7),
    )
    gathered, s2 = after((gathered, s2))

    def group_outs(rows, width):
        return [((4, 4, rows // SUB, width), BF)] * 2

    output_own, mine3, theirs3, dss2, sums, output_send = call(
        ffn_kernel,
        [((OWN, D), BF)]
        + group_outs(2 * D, D)
        + [((OWN, D), F32), ((EXT, D), F32), ((2 * TQ, D), BF)],
        (s2, cotangent, cot_got, bias, vecs, gathered),
        [
            pltpu.VMEM((2, 4, D, D), BF), pltpu.VMEM((4, OWN, D), BF), pltpu.VMEM((4, OWN, D), F32),
            pltpu.VMEM((OWN, D), BF), pltpu.VMEM((4, 2 * D, D), BF),
            pltpu.VMEM((OWN, D), BF), DMA((8,)), DMA((3,)),
        ],
        any_in=(1, 2, 5), any_out=(1, 2),
    )

    def add_split(mine, theirs):
        shape = mine.shape[1:]
        return call(add_split_kernel, [(shape, BF)] * 4, (mine, theirs))

    def sum_split(parts):
        shape = parts[0].shape[1:]
        return call(sum_split_kernel, [(shape, BF)] * 4, tuple(parts))

    def sum_parts(parts):
        piece = call(sum_kernel, [(parts[0].shape, F32 if groups > SUB else BF)], tuple(parts))[0]
        bit = SUB
        while bit < groups:
            piece = piece + swap(piece, "dp", bit)
            bit *= 2
        return piece.astype(BF)

    theirs3 = swap(theirs3, "dp", 1)
    dq2, dk2, dv2, enc_keep, enc_send = call(
        cross_attention_grad_kernel,
        [((OWN, D), BF), ((sources, D), BF), ((sources, D), BF)] + [((sources // 2, D), BF)] * 2,
        (scal, dss2, weight2, q2, k2, v2, qaug2, exact2, kaug_enc),
        [pltpu.VMEM((OWN, D), BF), pltpu.VMEM((4, D, D), BF), pltpu.VMEM((sources, D), BF)]
        + backward_scratch(sources),
        smem_in=(0,), any_in=(2, 3, 4, 5, 6, 7, 8), any_out=(1, 2, 3, 4), long=True,
    )
    theirs3, dq2 = after((theirs3, dq2))
    parts3 = add_split(mine3, theirs3)
    dq2 = after(dq2, parts3[0])
    moved3 = across(parts3[1:])
    enc_theirs = swap(enc_send, "mp", 1)
    output_got = swap(output_send, "mp", 1)
    mine2, theirs2, fsg, grad_ctx1, sums = call(
        cross_projection_grad_kernel,
        group_outs(5 * D, PAIR) + [((OWN, D), F32), ((OWN, D), BF), ((EXT, D), F32)],
        (dss2, s1, weight2, weight1, ctx2, ctx1, dq2, dk2, dv2, encoder, vecs, sums),
        [pltpu.VMEM((PAIRS, 5 * D, PAIR), BF), pltpu.VMEM((sources, D), BF), DMA((8,))],
        any_in=(9,), any_out=(0, 1), long=True,
    )
    output_got, grad_ctx1 = after((output_got, grad_ctx1))
    theirs2 = swap(theirs2, "dp", 1)
    dq1, dk1, dv1 = call(
        self_attention_grad_kernel,
        [((OWN, D), BF), ((length, D), BF), ((length, D), BF)],
        (scal, grad_ctx1, q1, k1, v1, qaug1, exact1, mask_t, kaug_dec),
        backward_scratch(length, True),
        smem_in=(0,), any_in=(2, 3, 4, 5, 6, 7, 8), any_out=(1, 2), long=True,
    )
    moved3, theirs2, enc_theirs, dq1 = after((moved3, theirs2, enc_theirs, dq1))
    slots3 = sum_split([parts3[0]] + moved3)
    parts2 = add_split(mine2, theirs2)
    dq1 = after(dq1, slots3[0], parts2[0])
    moved_slots3 = along(slots3[1:])
    moved2 = across(parts2[1:])
    mine1, theirs1, content_keep, rows_send, query_own = call(
        self_projection_grad_kernel,
        group_outs(3 * D + SUB * EXT, PAIR)
        + [((length // 2, D), BF), ((length // 2 + 2 * TQ, D), BF), ((OWN, D), BF)],
        (fsg, weight1, dq1, dk1, dv1, query_stream, content_stream, sums),
        [
            pltpu.VMEM((PAIRS, 3 * D + SUB * EXT, PAIR), BF), pltpu.VMEM((length, D), BF),
            pltpu.VMEM((OWN, D), BF), pltpu.VMEM((length, D), BF), DMA((8,)),
        ],
        any_in=(5, 6), any_out=(0, 1), long=True,
    )
    theirs1 = swap(theirs1, "dp", 1)
    rows_got = swap(rows_send, "mp", 1)
    parts1 = add_split(mine1, theirs1)
    moved_slots3, moved2, parts1 = after((moved_slots3, moved2, parts1))
    moved1 = across(parts1[1:])
    piece3 = sum_parts([slots3[0]] + moved_slots3)
    piece3, moved1 = after((piece3, moved1))
    slots = call(
        sum_merge_kernel,
        [((parts2[0].shape[1] + parts1[0].shape[1], PAIR), BF)] * 4,
        (parts2[0], *moved2, parts1[0], *moved1),
    )
    moved_slots = along(slots[1:])
    ffn_line = across([piece3] * 3)
    piece = sum_parts([slots[0]] + moved_slots)
    line = across([piece] * 3)
    ffn_line, line = after((ffn_line, line))
    ffn_line = jnp.stack([piece3] + ffn_line)
    ffn_other = swap(ffn_line, "dp", 1)
    line = jnp.stack([piece] + line)
    other = swap(line, "dp", 1)

    def join(keep, theirs):
        return (keep.astype(F32) + theirs.astype(F32)).astype(BF)

    encoder_grad = join(enc_keep, enc_theirs)
    (
        self_proj_grad, self_bias_grad, self_out_grad, cross_proj_grad, cross_bias_grad,
        cross_out_grad, ffn_in_grad, ffn_bias_grad, ffn_out_grad, out_bias_grad,
        gain_grad, shift_grad, output, query_grad, content_grad,
    ) = call(
        finish_kernel,
        [
            ((3, D, PAIR), F32), ((2, PAIR), F32), ((PAIR, D), F32), ((3, D, PAIR), F32),
            ((2, PAIR), F32), ((PAIR, D), F32), ((D, D), F32), ((1, D), F32), ((D, D), F32),
            ((3, D), F32), ((3, D), F32), ((3, D), F32), ((OWN, D), BF), ((OWN, D), BF), ((length // 2, D), BF),
        ],
        (
            ffn_line, ffn_other, line, other, output_own, output_got, query_own, content_keep,
            rows_got,
        ),
        [
            pltpu.VMEM((2 * D, D), F32), pltpu.VMEM((5 * D, PAIR), F32),
            pltpu.VMEM((3 * D + SUB * EXT, PAIR), F32),
        ],
    )
    return (
        output,
        query_grad,
        content_grad,
        encoder_grad,
        self_proj_grad,
        self_bias_grad,
        self_out_grad,
        cross_proj_grad,
        cross_bias_grad,
        cross_out_grad,
        ffn_in_grad,
        ffn_bias_grad.reshape(D),
        ffn_out_grad,
        out_bias_grad,
        gain_grad,
        shift_grad,
    )


def solution(mesh):
    return jax.shard_map(
        body,
        mesh=mesh,
        in_specs=(
            P("dp", None), P("dp", None), P("dp", None), P("dp", None), P("dp", None),
            P("dp", None), P("dp", None), P("dp", None), P(None, None, "mp"), P(None, "mp"),
            P("mp", None), P(None, None, "mp"), P(None, "mp"), P("mp", None), P(None, "mp"),
            P("mp"), P("mp", None), P(), P(), P(), P(("dp", "mp"), None),
        ),
        out_specs=(
            P(("dp", "mp"), None), P(("dp", "mp"), None), P(("dp", "mp"), None),
            P(("dp", "mp"), None), P(None, None, "mp"), P(None, "mp"), P("mp", None),
            P(None, None, "mp"), P(None, "mp"), P("mp", None), P(None, "mp"), P("mp"),
            P("mp", None), P(), P(), P(),
        ),
        check_vma=False,
    )
```

```python
import math

import jax
import jax.numpy as jnp
from jax import lax
from jax.experimental import pallas as pl
from jax.experimental.pallas import tpu as pltpu
from jax.sharding import PartitionSpec as P

HEAD = 64
EPSILON = 1e-05
MASKED = -1000000000.0
LOG2E = math.log2(math.e)
D = 512
PAIR = 128
PAIRS = 4
OWN = 512
TQ = 128
ROW_TILES = 8
TK = 256
TILES = OWN // TQ
SUB = 8
EXT = 16
BF = jnp.bfloat16
F32 = jnp.float32
VMEM_LIMIT = 56 * 1024 * 1024


def mm(left, right):
    return jnp.dot(left, right, preferred_element_type=F32)


def mm_rows(left, right):
    return lax.dot_general(left, right, (((0,), (0,)), ((), ())), preferred_element_type=F32)


def mm_cols(left, right):
    return lax.dot_general(left, right, (((1,), (1,)), ((), ())), preferred_element_type=F32)


def norm_parts(summed):
    average = jnp.mean(summed, axis=-1, keepdims=True)
    centred = summed - average
    inverse = lax.rsqrt(jnp.mean(centred * centred, axis=-1, keepdims=True) + EPSILON)
    return centred * inverse, inverse


def norm_backward(incoming, normed, inverse, gain):
    scaled = incoming * gain
    inner = (
        scaled
        - jnp.mean(scaled, axis=-1, keepdims=True)
        - normed * jnp.mean(scaled * normed, axis=-1, keepdims=True)
    )
    return inner * inverse


def col_sum(values):
    return jnp.sum(values.astype(F32), axis=0, keepdims=True)


def half_lanes(rows):
    return lax.broadcasted_iota(jnp.int32, (rows, PAIR), 1) < HEAD


def stack_heads(values):
    keep = half_lanes(values.shape[0])
    zero = jnp.zeros_like(values)
    return jnp.concatenate([jnp.where(keep, values, zero), jnp.where(keep, zero, values)], axis=0)


def pieces_of(value, first_lane, base):
    lane = lax.broadcasted_iota(jnp.int32, value.shape, 1)
    high = value.astype(BF)
    rest = value - high.astype(F32)
    middle = rest.astype(BF)
    low = (rest - middle.astype(F32)).astype(BF)
    out = jnp.where(lane == first_lane, high, base)
    out = jnp.where(lane == first_lane + 1, middle, out)
    return jnp.where(lane == first_lane + 2, low, out)


def lanes(pair):
    return slice(pair * PAIR, (pair + 1) * PAIR)


def key_range(scal, which, tile):
    base = pl.multiple_of(scal[2 + which * 2 * TILES + tile], PAIR)
    count = scal[2 + which * 2 * TILES + TILES + tile]
    return base, count


def over_keys(count, block):
    done = 0
    for wide in (4, 2, 1):
        whole = (count - done) // wide

        def step(index, carry, done=done, wide=wide):
            block((done + index * wide) * TK, wide * TK)
            return carry

        lax.fori_loop(0, whole, step, 0)
        done = done + whole * wide


def attend_forward(scal, which, q, k, v, kaug, hot, mask, score, peak, mixed, qaug, ctx, exact):
    def tile_body(tile, carry):
        base, count = key_range(scal, which, tile)
        rows = pl.ds(pl.multiple_of(tile * TQ, TQ), TQ)
        extra = hot[rows, :]
        extra2 = jnp.concatenate([extra, extra], axis=0)
        peak[...] = jnp.full(peak.shape, -jnp.inf, F32)
        mixed[...] = jnp.zeros(mixed.shape, F32)

        def scores(begin, size):
            off = pl.multiple_of(base + begin, PAIR)
            here = pl.ds(pl.multiple_of(begin, TK), size)
            ka = kaug[pl.ds(off, size), :]
            if mask is not None:
                block = mask[rows, pl.ds(off, size)]
                block = jnp.concatenate([block, block], axis=0)
            for pair in range(PAIRS):
                q2 = jnp.concatenate([stack_heads(q[rows, lanes(pair)]), extra2], axis=1)
                kk = jnp.concatenate([k[pl.ds(off, size), lanes(pair)], ka], axis=1)
                s = mm_cols(q2, kk)
                if mask is not None:
                    s = s + block
                score[pair, :, here] = s
                top = peak[pair]
                for part in range(size // PAIR):
                    top = jnp.maximum(top, s[:, part * PAIR : (part + 1) * PAIR])
                peak[pair] = top

        over_keys(count, scores)
        for pair in range(PAIRS):
            peak[pair] = jnp.broadcast_to(
                jnp.max(peak[pair], axis=1, keepdims=True), (2 * TQ, PAIR)
            )

        def weights(begin, size):
            off = pl.multiple_of(base + begin, PAIR)
            here = pl.ds(pl.multiple_of(begin, TK), size)
            minus = jnp.full((size, PAIR), -1.0, BF)
            for pair in range(PAIRS):
                top = jnp.concatenate([peak[pair]] * (size // PAIR), axis=1)
                p = jnp.exp2((score[pair, :, here] - top) * LOG2E).astype(BF)
                vv = jnp.concatenate([v[pl.ds(off, size), lanes(pair)], minus], axis=1)
                mixed[pair] += mm(p, vv)

        over_keys(count, weights)
        keep = half_lanes(TQ)
        for pair in range(PAIRS):
            both = mixed[pair]
            total = -both[:, PAIR:]
            normal = both[:, :PAIR] / total
            out = jnp.where(keep, normal[:TQ], normal[TQ:])
            exact[rows, lanes(pair)] = out
            ctx[rows, lanes(pair)] = out.astype(BF)
            logsum = peak[pair] + jnp.log(total)
            for head in range(2):
                part = logsum[head * TQ : (head + 1) * TQ]
                qaug[2 * pair + head, rows, :] = pieces_of(part, 4, extra)
        return carry

    lax.fori_loop(0, TILES, tile_body, 0)


def attend_backward(scal, which, q, k, v, kaug, qaug, mask_t, grad, exact, dq, dk, dv, dq_tile):
    def tile_body(tile, carry):
        base, count = key_range(scal, which, tile)
        start = pl.multiple_of(tile * TQ, TQ)
        rows = pl.ds(start, TQ)
        dq_tile[...] = jnp.zeros(dq_tile.shape, F32)
        keep = half_lanes(TQ)
        grads, queries, grad_aug, query_aug = [], [], [], []
        for pair in range(PAIRS):
            g = grad[rows, lanes(pair)]
            inner = g.astype(F32) * exact[rows, lanes(pair)]
            first = jnp.sum(jnp.where(keep, inner, 0.0), axis=1, keepdims=True)
            second = jnp.sum(jnp.where(keep, 0.0, inner), axis=1, keepdims=True)
            delta = jnp.broadcast_to(jnp.concatenate([first, second], axis=0), (2 * TQ, PAIR))
            aug = pieces_of(delta, 0, jnp.zeros((2 * TQ, PAIR), BF))
            g2 = stack_heads(g)
            q2 = stack_heads(q[rows, lanes(pair)])
            grads.append(g2)
            queries.append(q2)
            grad_aug.append(jnp.concatenate([g2, aug], axis=1))
            qa = jnp.concatenate([qaug[2 * pair, rows, :], qaug[2 * pair + 1, rows, :]], axis=0)
            query_aug.append(jnp.concatenate([q2, qa], axis=1))

        def keys(begin, size):
            off = pl.multiple_of(base + begin, PAIR)
            here = pl.ds(off, size)
            ka = kaug[here, :]
            minus = jnp.full((size, PAIR), -1.0, BF)
            if mask_t is not None:
                block = mask_t[here, rows]
                block = jnp.concatenate([block, block], axis=1)
            for pair in range(PAIRS):
                kp = k[here, lanes(pair)]
                s = mm_cols(jnp.concatenate([kp, ka], axis=1), query_aug[pair])
                if mask_t is not None:
                    s = s + block
                p = jnp.exp2(s * LOG2E)
                vp = jnp.concatenate([v[here, lanes(pair)], minus], axis=1)
                ds = (p * mm_cols(vp, grad_aug[pair])).astype(BF)
                dv[here, lanes(pair)] += mm(p.astype(BF), grads[pair])
                dk[here, lanes(pair)] += mm(ds, queries[pair])
                dq_tile[pair] += mm_rows(ds, kp)

        over_keys(count, keys)
        for pair in range(PAIRS):
            both = dq_tile[pair] * HEAD ** (-0.5)
            dq[rows, lanes(pair)] = jnp.where(keep, both[:TQ], both[TQ:]).astype(BF)
        return carry

    lax.fori_loop(0, TILES, tile_body, 0)


def mesh_place():
    group = lax.axis_index("dp")
    return group % 2, (group // 2) % 4, lax.axis_index("mp")


def run_copies(copies):
    for copy in copies:
        copy.start()
    for copy in copies:
        copy.wait()


def load_weights(proj, out, mine, other, weight, sem):
    core, place, _ = mesh_place()
    copies = []
    for matrix in range(3):
        copies.append(
            pltpu.make_async_copy(
                proj.at[matrix], weight.at[matrix, :, lanes(0)], sem.at[len(copies)]
            )
        )
    for side, source in ((core, mine), (1 - core, other)):
        for shift in range(4):
            spot = jnp.bitwise_xor(place, shift)
            matrix = 2 * side + spot // 2
            row = pl.multiple_of((spot % 2) * 256, 256)
            for pair in range(1, PAIRS):
                copies.append(
                    pltpu.make_async_copy(
                        source.at[shift, pair - 1, pl.ds(0, 256), :],
                        weight.at[matrix, pl.ds(row, 256), lanes(pair)],
                        sem.at[len(copies)],
                    )
                )
    weight[3, :, lanes(0)] = out[...].astype(F32).T.astype(BF)
    return copies


def put(source, target, sem):
    copy = pltpu.make_async_copy(source, target, sem)
    copy.start()
    return copy


def own_tiles(source, target, sem, first):
    _, _, position = mesh_place()
    copies = []
    for tile in range(TILES):
        row = pl.multiple_of((position // 2 * ROW_TILES + 2 * tile + position % 2) * TQ, TQ)
        copies.append(
            pltpu.make_async_copy(
                source.at[pl.ds(row, TQ), :], target.at[tile * TQ : (tile + 1) * TQ, :],
                sem.at[first + tile],
            )
        )
    return copies


def grad_copies(buffer, mine, theirs, sem):
    core, place, _ = mesh_place()
    chunk = buffer.shape[1] // SUB
    copies = []
    for side, target in ((core, mine), (1 - core, theirs)):
        for shift in range(4):
            row = pl.multiple_of((4 * side + jnp.bitwise_xor(place, shift)) * chunk, 16)
            copies.append(
                pltpu.make_async_copy(
                    buffer.at[:, pl.ds(row, chunk), :], target.at[shift], sem.at[len(copies)]
                )
            )
    return copies


def send_grads(buffer, mine, theirs, sem):
    run_copies(grad_copies(buffer, mine, theirs, sem))


def send_rows(buffer, keep, theirs, sem):
    part = lax.axis_index("mp") % 2
    rows = buffer.shape[0] // 2
    copies = []
    for side, target in ((part, keep), (1 - part, theirs)):
        row = pl.multiple_of(side * rows, 16)
        copies.append(
            pltpu.make_async_copy(buffer.at[pl.ds(row, rows), :], target, sem.at[len(copies)])
        )
    run_copies(copies)


def pack_kernel(
    self_proj, self_out, cross_proj, cross_out, ffn_in, ffn_out, self_bias, cross_bias, ffn_bias, cot,
    own, own3, cot_send, small,
):
    core, place, position = mesh_place()
    for index in range(2):
        row = pl.multiple_of((1 - position % 2 + 2 * index) * TQ, TQ)
        cot_send[index * TQ : (index + 1) * TQ, :] = cot[pl.ds(row, TQ), :]
    chunk = 4 * core + place
    matrix, half = chunk // 2, chunk % 2
    for proj, out, base in ((self_proj, self_out, 0), (cross_proj, cross_out, 256 + EXT)):

        @pl.when(matrix < 3)
        def _(proj=proj, base=base):
            own[base : base + 256, :] = proj[matrix, pl.ds(pl.multiple_of(half * 256, 256), 256), :]

        @pl.when(matrix == 3)
        def _(out=out, base=base):
            block = out[:, pl.ds(pl.multiple_of(half * 256, 256), 256)]
            own[base : base + 256, :] = block.astype(F32).T.astype(BF)

    rows = [self_bias[...].astype(F32), cross_bias[...].astype(F32)]
    rows += [ffn_bias[:, lanes(block)].astype(F32) for block in range(4)]
    rows += [jnp.zeros((8, PAIR), F32)]
    small[...] = jnp.concatenate(rows, axis=0).astype(BF)
    own[256 : 256 + EXT, :] = small[...]
    rows = own3.shape[0]
    row = chunk * rows

    @pl.when(row < D)
    def _():
        own3[...] = ffn_in[pl.ds(pl.multiple_of(row, rows), rows), :]

    @pl.when(row >= D)
    def _():
        own3[...] = ffn_out[pl.ds(pl.multiple_of(row - D, rows), rows), :]


def prep_kernel(
    dec, enc, ranks, limits, padded, out_bias, gain, shift,
    scal, mask, mask_t, hot, kaug_dec, kaug_enc, vecs, table,
):
    _, _, position = mesh_place()
    row, part = position // 2, position % 2
    length, sources = dec.shape[1], enc.shape[1]
    seg = dec[pl.ds(row, 1), :]
    seg_enc = enc[pl.ds(row, 1), :]
    place = lax.broadcasted_iota(jnp.int32, (1, length), 1)
    begins = (place == 0) | (seg != pltpu.roll(seg, 1, 1))
    rank = jnp.where(padded[pl.ds(row, 1), :] == 0, ranks[pl.ds(row, 1), :], length)
    table[...] = jnp.zeros(table.shape, F32)
    table[0:1, :] = seg.astype(F32)
    table[1:2, :] = rank.astype(F32)
    table[2:3, :] = begins.astype(F32)
    table[3:4, :] = limits[pl.ds(row, 1), :].astype(F32)
    table[4:5, :] = place.astype(F32)
    own = jnp.concatenate(
        [
            table[:, pl.ds(pl.multiple_of((2 * tile + part) * TQ, TQ), TQ)]
            for tile in range(TILES)
        ],
        axis=1,
    )
    own_t = own.T
    every = table[...]
    every_t = every.T

    def visible(seg_q, limit_q, place_q, seg_k, rank_k, start_k, place_k):
        chosen = (rank_k < limit_q) & (place_q != place_k)
        return jnp.where((seg_q == seg_k) & ((start_k > 0.5) | chosen), 0.0, MASKED)

    mask[...] = visible(
        own_t[:, 0:1], own_t[:, 3:4], own_t[:, 4:5],
        every[0:1], every[1:2], every[2:3], every[4:5],
    )
    mask_t[...] = visible(
        own[0:1], own[3:4], own[4:5],
        every_t[:, 0:1], every_t[:, 1:2], every_t[:, 2:3], every_t[:, 4:5],
    )

    def key_aug(column):
        lane = lax.broadcasted_iota(jnp.int32, (column.shape[0], PAIR), 1)
        different = (lane < 4) & (column != lane.astype(F32))
        minus = (lane >= 4) & (lane < 7)
        return jnp.where(different, MASKED, jnp.where(minus, -1.0, 0.0)).astype(BF)

    kaug_dec[...] = key_aug(every_t[:, 0:1])
    seg_enc_f = jnp.broadcast_to(seg_enc.astype(F32), (8, sources))
    kaug_enc[...] = key_aug(seg_enc_f.T[:, 0:1])
    lane = lax.broadcasted_iota(jnp.int32, (OWN, PAIR), 1)
    hot[...] = (own_t[:, 0:1] == lane.astype(F32)).astype(F32).astype(BF)
    vecs[...] = jnp.zeros(vecs.shape, F32)
    for index, source in enumerate((out_bias, gain, shift)):
        vecs[3 * index : 3 * index + 3, :] = source[...].astype(F32)
    scal[0] = 0
    scal[1] = 0
    for which, keys in ((0, every[0:1]), (1, seg_enc_f[0:1])):
        size = keys.shape[1]
        for tile in range(TILES):
            block = own[0:1, tile * TQ : (tile + 1) * TQ]
            low, high = jnp.min(block), jnp.max(block)
            begin = jnp.sum((keys < low).astype(F32)).astype(jnp.int32)
            end = jnp.sum((keys <= high).astype(F32)).astype(jnp.int32)
            base = begin // PAIR * PAIR
            count = (end - base + TK - 1) // TK
            scal[2 + which * 2 * TILES + tile] = jnp.minimum(base, size - count * TK)
            scal[2 + which * 2 * TILES + TILES + tile] = count


def fetch(source, target, start, sem):
    return pltpu.make_async_copy(
        source.at[pl.ds(pl.multiple_of(start, target.shape[0]), target.shape[0]), :], target, sem
    )


def project(x, weight, bias, target):
    step = min(x.shape[0], 1024)
    for part in range(x.shape[0] // step):
        rows = slice(part * step, (part + 1) * step)
        value = mm(x[rows, :], weight)
        target[rows, :] = (value if bias is None else value + bias).astype(BF)


def self_forward_kernel(
    scal, query, content, mask_in, hot, kaug, vecs, small, proj, out, mine, other,
    q, k_out, v_out, qaug, ctx, exact, s1, weight_out, bias,
    score, peak, mixed, got, xq, xc, k, v, weight, mask, sem, sem_out,
):
    _, _, position = mesh_place()
    rows = xc.shape[0]
    copies = own_tiles(query, xq, sem, 32)
    copies.append(
        pltpu.make_async_copy(
            content.at[pl.ds(pl.multiple_of(position // 2 * rows, rows), rows), :], xc, sem.at[36]
        )
    )
    for pair in range(1, PAIRS):
        copies.append(
            pltpu.make_async_copy(
                mine.at[0, pair - 1, pl.ds(256, EXT), :], got.at[pair - 1], sem.at[36 + pair]
            )
        )
    late = pltpu.make_async_copy(mask_in, mask, sem.at[40])
    for copy in copies:
        copy.start()
    moves = load_weights(proj, out, mine, other, weight, sem)
    for copy in moves:
        copy.start()
    late.start()
    for copy in copies + moves:
        copy.wait()
    outs = [put(weight, weight_out, sem_out.at[0])]
    bias[:, lanes(0)] = small[...].astype(F32)
    for pair in range(1, PAIRS):
        bias[:, lanes(pair)] = got[pair - 1].astype(F32)
    q[...] = ((mm(xq[...], weight[0]) + bias[0:1, :]).astype(BF) * BF(HEAD ** (-0.5))).astype(BF)
    project(xc, weight[1], None, k)
    outs.append(put(k, k_out, sem_out.at[1]))
    project(xc, weight[2], bias[1:2, :], v)
    outs.append(put(v, v_out, sem_out.at[2]))
    late.wait()
    attend_forward(scal, 0, q, k, v, kaug, hot, mask, score, peak, mixed, qaug, ctx, exact)
    s1[...] = xq[...].astype(F32) + mm_cols(ctx[...], weight[3]) + vecs[0:1, :]
    for copy in outs:
        copy.wait()


def cross_forward_kernel(
    scal, s1, encoder, hot, kaug, vecs, bias, proj, out, mine, other,
    q, k_out, v_out, qaug, ctx, exact, s2, weight_out,
    score, peak, mixed, enc, k, v, weight, sem, sem_out,
):
    _, _, position = mesh_place()
    moves = load_weights(proj, out, mine, other, weight, sem)
    rows = enc.shape[0]
    late = pltpu.make_async_copy(
        encoder.at[pl.ds(pl.multiple_of(position // 2 * rows, rows), rows), :], enc, sem.at[32]
    )
    for copy in moves:
        copy.start()
    late.start()
    normed, _ = norm_parts(s1[...])
    first = normed * vecs[3:4, :] + vecs[6:7, :]
    for copy in moves:
        copy.wait()
    outs = [put(weight, weight_out, sem_out.at[0])]
    q[...] = (
        (mm(first.astype(BF), weight[0]) + bias[2:3, :]).astype(BF) * BF(HEAD ** (-0.5))
    ).astype(BF)
    late.wait()
    project(enc, weight[1], None, k)
    outs.append(put(k, k_out, sem_out.at[1]))
    project(enc, weight[2], bias[3:4, :], v)
    outs.append(put(v, v_out, sem_out.at[2]))
    attend_forward(scal, 1, q, k, v, kaug, hot, None, score, peak, mixed, qaug, ctx, exact)
    s2[...] = first + mm_cols(ctx[...], weight[3]) + vecs[1:2, :]
    for copy in outs:
        copy.wait()


def gelu_parts(v):
    c = math.sqrt(2.0 / math.pi)
    square = v * v
    t = jnp.tanh(c * (v + 0.044715 * square * v))
    value = 0.5 * v * (1.0 + t)
    slope = 0.5 * (1.0 + t) + 0.5 * v * (1.0 - t * t) * (c + (3.0 * 0.044715 * c) * square)
    return value, slope


def ffn_kernel(
    s2, cot_own, cot_got, bias, vecs, ffn_in, ffn_out, first_core, second_core,
    output, mine, theirs, back, sums, output_send,
    weight, hidden, slopes, low, grads, cot, sem, sem_cot,
):
    core, place, position = mesh_place()
    half = position % 2
    late = []
    for index in range(2):
        row = pl.multiple_of((half + 2 * index) * TQ, TQ)
        target = pl.multiple_of((2 * half + index) * TQ, TQ)
        late.append(
            put(cot_own.at[pl.ds(row, TQ), :], cot.at[pl.ds(target, TQ), :], sem_cot.at[index])
        )
    target = pl.multiple_of((1 - half) * 2 * TQ, 2 * TQ)
    late.append(put(cot_got, cot.at[pl.ds(target, 2 * TQ), :], sem_cot.at[2]))
    copies = [[] for _ in range(4)]
    for side, source in enumerate((ffn_in, ffn_out)):
        copies[0].append(put(source, weight.at[side, 0], sem.at[side]))
    for part in range(1, 4):
        for side, source in ((core, first_core), (1 - core, second_core)):
            for shift in range(4):
                row = pl.multiple_of(jnp.bitwise_xor(place, shift) * 128, 128)
                number = 2 + sum(len(group) for group in copies[1:])
                copies[part].append(
                    put(
                        source.at[shift, part - 1], weight.at[side, part, pl.ds(row, 128), :],
                        sem.at[number],
                    )
                )
    sums[...] = jnp.zeros(sums.shape, F32)
    normed2, inverse2 = norm_parts(s2[...])
    second = normed2 * vecs[4:5, :] + vecs[7:8, :]
    low[...] = second.astype(BF)
    total = second + vecs[2:3, :]
    for part in range(4):
        block = slice(part * D, (part + 1) * D)
        part_bias = jnp.concatenate([bias[4 + i : 5 + i, lanes(part)] for i in range(4)], axis=1)
        for copy in copies[part]:
            copy.wait()
        pre = mm(low[...], weight[0, part]) + part_bias
        value, slope = gelu_parts(pre)
        hidden[:, block] = value.astype(BF)
        slopes[:, block] = slope
        total = total + mm(hidden[:, block], weight[1, part])
    normed3, inverse3 = norm_parts(total)
    output[...] = (normed3 * vecs[5:6, :] + vecs[8:9, :]).astype(BF)
    for copy in late:
        copy.wait()
    row = pl.multiple_of((1 - half) * 2 * TQ, 2 * TQ)
    output_send[...] = output[pl.ds(row, 2 * TQ), :]
    incoming = cot[...].astype(F32)
    sums[0:1, :] = col_sum(incoming * normed3)
    sums[1:2, :] = col_sum(incoming)
    third_grad = norm_backward(incoming, normed3, inverse3, vecs[5:6, :])
    branch = third_grad.astype(BF)
    sums[2:3, :] = col_sum(branch)
    total = third_grad
    for part in range(4):
        block = slice(part * D, (part + 1) * D)
        pre_grad = (slopes[:, block] * mm_cols(branch, weight[1, part])).astype(BF)
        sums[8 + part : 9 + part, :] = col_sum(pre_grad)
        grads[part, 0:D, :] = mm_rows(low[...], pre_grad).astype(BF)
        grads[part, D : 2 * D, :] = mm_rows(hidden[:, block], branch).astype(BF)
        if part == 3:
            moves = grad_copies(grads, mine, theirs, sem)
            for copy in moves:
                copy.start()
        total = total + mm_cols(pre_grad, weight[0, part])
    sums[3:4, :] = col_sum(total * normed2)
    sums[4:5, :] = col_sum(total)
    second_grad = norm_backward(total, normed2, inverse2, vecs[4:5, :])
    sums[5:6, :] = col_sum(second_grad.astype(BF))
    back[...] = second_grad
    for copy in moves:
        copy.wait()


def store_grad(grads, matrix, value):
    low = value.astype(BF)
    for pair in range(PAIRS):
        grads[pair, matrix * D : (matrix + 1) * D, :] = low[:, lanes(pair)]


def projection_grads(grads, x, low, matrix):
    store_grad(grads, matrix, mm_rows(x[...], low[...]))


def input_grads(dk, dv, weight, out):
    step = min(dk.shape[0], 1024)
    for part in range(dk.shape[0] // step):
        rows = slice(part * step, (part + 1) * step)
        out[rows, :] = (
            mm_cols(dk[rows, :], weight[1]) + mm_cols(dv[rows, :], weight[2])
        ).astype(BF)


def load_all(sources, targets, sem):
    copies = [
        pltpu.make_async_copy(source, target, sem.at[index])
        for index, (source, target) in enumerate(zip(sources, targets))
    ]
    for copy in copies:
        copy.start()
    return copies


def store_low(dk, dv, dk_low, dv_low, low, sem):
    copies = []
    for index, (value, target) in enumerate(((dk, dk_low), (dv, dv_low))):
        for part in range(value.shape[0] // 512):
            rows = slice(part * 512, (part + 1) * 512)
            low[index, rows, :] = value[rows, :].astype(BF)
            copies.append(put(low.at[index, rows, :], target.at[rows, :], sem.at[len(copies)]))
    return copies


def cross_attention_grad_kernel(
    scal, dss2, weight_in, q_in, k_in, v_in, qaug_in, exact_in, kaug_in,
    dq, dk_low, dv_low, keep, send,
    grad_ctx, weight, enc_grad, dk, dv, dq_tile, low, q, k, v, qaug, exact, kaug, sem,
):
    first = put(weight_in, weight, sem.at[7])
    copies = load_all(
        (q_in, qaug_in, exact_in, kaug_in, k_in, v_in), (q, qaug, exact, kaug, k, v), sem
    )
    dk[...] = jnp.zeros(dk.shape, F32)
    dv[...] = jnp.zeros(dv.shape, F32)
    first.wait()
    grad_ctx[...] = mm(dss2[...].astype(BF), weight[3]).astype(BF)
    for copy in copies:
        copy.wait()
    attend_backward(scal, 1, q, k, v, kaug, qaug, None, grad_ctx, exact, dq, dk, dv, dq_tile)
    copies = store_low(dk, dv, dk_low, dv_low, low, sem)
    input_grads(low.at[0], low.at[1], weight, enc_grad)
    for copy in copies:
        copy.wait()
    send_rows(enc_grad, keep, send, sem)


def cross_projection_grad_kernel(
    dss2, s1, weight_in, self_weight, ctx, self_ctx, dq, dk_in, dv_in, encoder, vecs, sums_in,
    mine, theirs, back, grad_ctx, sums,
    grads, enc, weight, dk, dv, sem,
):
    _, _, position = mesh_place()
    rows = enc.shape[0]
    start = pl.multiple_of(position // 2 * rows, rows)
    early = [
        put(weight_in.at[0], weight.at[0], sem.at[0]),
        put(self_weight.at[3], weight.at[1], sem.at[1]),
    ]
    late = [
        put(encoder.at[pl.ds(start, rows), :], enc, sem.at[2]),
        put(dk_in, dk, sem.at[3]),
        put(dv_in, dv, sem.at[4]),
    ]
    sums[...] = sums_in[...]
    normed, inverse = norm_parts(s1[...])
    first = (normed * vecs[3:4, :] + vecs[6:7, :]).astype(BF)
    store_grad(grads, 0, mm_rows(first, dq[...]))
    store_grad(grads, 3, mm_rows(dss2[...].astype(BF), ctx[...]))
    for copy in early:
        copy.wait()
    total = dss2[...] + mm_cols(dq[...], weight[0])
    sums[6:7, :] = col_sum(total * normed)
    sums[7:8, :] = col_sum(total)
    first_grad = norm_backward(total, normed, inverse, vecs[3:4, :])
    branch = first_grad.astype(BF)
    sums[12:13, :] = col_sum(branch)
    back[...] = first_grad
    grad_ctx[...] = mm(branch, weight[1]).astype(BF)
    store_grad(grads, 4, mm_rows(branch, self_ctx[...]))
    sums[14:15, :] = col_sum(dq[...])
    for copy in late:
        copy.wait()
    projection_grads(grads, enc, dk, 1)
    projection_grads(grads, enc, dv, 2)
    sums[15:16, :] = col_sum(dv[...])
    send_grads(grads, mine, theirs, sem)


def self_attention_grad_kernel(
    scal, grad_ctx, q_in, k_in, v_in, qaug_in, exact_in, mask_in, kaug_in,
    dq, dk_low, dv_low,
    dk, dv, dq_tile, low, q, k, v, qaug, exact, mask_t, kaug, sem,
):
    copies = load_all(
        (q_in, qaug_in, exact_in, kaug_in, k_in, v_in, mask_in),
        (q, qaug, exact, kaug, k, v, mask_t),
        sem,
    )
    dk[...] = jnp.zeros(dk.shape, F32)
    dv[...] = jnp.zeros(dv.shape, F32)
    for copy in copies:
        copy.wait()
    attend_backward(scal, 0, q, k, v, kaug, qaug, mask_t, grad_ctx, exact, dq, dk, dv, dq_tile)
    for copy in store_low(dk, dv, dk_low, dv_low, low, sem):
        copy.wait()


def self_projection_grad_kernel(
    fsg, weight_in, dq, dk, dv, query, content, sums,
    mine, theirs, keep, send, query_grad,
    grads, content_grad, xq, xc, weight, sem, sem_late,
):
    _, _, position = mesh_place()
    half = position % 2
    rows = xc.shape[0]
    copies = own_tiles(query, xq, sem, 0)
    for copy in copies:
        copy.start()
    place = pl.multiple_of(position // 2 * rows, rows)
    content_copy = put(content.at[pl.ds(place, rows), :], xc, sem_late.at[0])
    weight_copy = put(weight_in, weight, sem_late.at[1])
    for copy in copies:
        copy.wait()
    store_grad(grads, 0, mm_rows(xq[...], dq[...]))
    content_copy.wait()
    projection_grads(grads, xc, dk, 1)
    projection_grads(grads, xc, dv, 2)
    bias_q = col_sum(dq[...])
    bias_v = col_sum(dv[...])
    for pair in range(PAIRS):
        parts = [bias_q[:, lanes(pair)], bias_v[:, lanes(pair)]]
        parts += [sums[14:15, lanes(pair)], sums[15:16, lanes(pair)]]
        parts += [sums[8 + pair : 9 + pair, lanes(i)] for i in range(4)]
        for index in (0, 1, 2, 3, 4, 5, 6, 7, 12):
            parts += [sums[index : index + 1, lanes(i)] for i in range(4)]
        parts += [jnp.zeros((SUB * EXT - len(parts), PAIR), F32)]
        grads[pair, 3 * D : 3 * D + SUB * EXT, :] = jnp.concatenate(parts, axis=0).astype(BF)
    moves = grad_copies(grads, mine, theirs, sem)
    for copy in moves:
        copy.start()
    weight_copy.wait()
    input_grads(dk, dv, weight, content_grad)
    query_grad[...] = (fsg[...] + mm_cols(dq[...], weight[0])).astype(BF)
    mid = rows // 2
    keep[...] = content_grad[pl.ds(pl.multiple_of(half * mid, mid), mid), :]
    send[0:mid, :] = content_grad[pl.ds(pl.multiple_of((1 - half) * mid, mid), mid), :]
    row = pl.multiple_of((1 - half) * 2 * TQ, 2 * TQ)
    send[mid:, :] = query_grad[pl.ds(row, 2 * TQ), :]
    for copy in moves:
        copy.wait()


def add_split_kernel(mine, theirs, *outs):
    for index, out in enumerate(outs):
        out[...] = (mine[index].astype(F32) + theirs[index].astype(F32)).astype(BF)


def sum_split_kernel(own, first, second, third, *outs):
    for index, out in enumerate(outs):
        out[...] = (
            (own[index].astype(F32) + first[index].astype(F32))
            + (second[index].astype(F32) + third[index].astype(F32))
        ).astype(BF)


def sum_merge_kernel(a0, a1, a2, a3, b0, b1, b2, b3, *outs):
    rows = a0.shape[1]
    for index, out in enumerate(outs):
        for group, spot in (((a0, a1, a2, a3), slice(0, rows)), ((b0, b1, b2, b3), slice(rows, None))):
            own, first, second, third = [part[index].astype(F32) for part in group]
            out[spot, :] = ((own + first) + (second + third)).astype(BF)


def sum_kernel(own, first, second, third, out):
    out[...] = (
        (own[...].astype(F32) + first[...].astype(F32))
        + (second[...].astype(F32) + third[...].astype(F32))
    ).astype(out.dtype)


def finish_ffn_kernel(line, other, ffn_in, ffn_out, wide):
    core, place, _ = mesh_place()
    for side, source in ((core, line), (1 - core, other)):
        for shift in range(4):
            row = pl.multiple_of((4 * side + jnp.bitwise_xor(place, shift)) * 128, 128)
            wide[pl.ds(row, 128), :] = source[shift].astype(F32)
    ffn_in[...] = wide[0:D, :]
    ffn_out[...] = wide[D:, :]


def finish_rows_kernel(output_own, output_got, query_own, keep, got, output, query, content):
    _, _, position = mesh_place()
    half = position % 2
    mid = keep.shape[0]
    for own, theirs, skip, target in (
        (output_own, output_got, 0, output), (query_own, got, mid, query)
    ):
        for index in range(2):
            row = pl.multiple_of((2 * half + index) * TQ, TQ)
            place_own = pl.multiple_of((half + 2 * index) * TQ, TQ)
            place_got = pl.multiple_of((1 - half + 2 * index) * TQ, TQ)
            first = skip + index * TQ
            target[pl.ds(place_own, TQ), :] = own[pl.ds(row, TQ), :]
            target[pl.ds(place_got, TQ), :] = theirs[first : first + TQ, :]
    content[...] = (keep[...].astype(F32) + got[0:mid, :].astype(F32)).astype(BF)


def finish_kernel(
    line, other,
    self_proj, self_bias, self_out, cross_proj, cross_bias, cross_out, ffn_bias,
    out_bias, gain, moved, flat, flat_self,
):
    core, place, _ = mesh_place()
    cross_rows, self_rows = flat.shape[0] // SUB, flat_self.shape[0] // SUB
    for side, source in ((core, line), (1 - core, other)):
        for shift in range(4):
            spot = 4 * side + jnp.bitwise_xor(place, shift)
            row = pl.multiple_of(spot * cross_rows, 8)
            flat[pl.ds(row, cross_rows), :] = source[shift, 0:cross_rows, :].astype(F32)
            row = pl.multiple_of(spot * self_rows, 8)
            flat_self[pl.ds(row, self_rows), :] = source[shift, cross_rows:, :].astype(F32)
    for matrix in range(3):
        cross_proj[matrix] = flat[matrix * D : (matrix + 1) * D, :]
        self_proj[matrix] = flat_self[matrix * D : (matrix + 1) * D, :]
    cross_out[...] = flat[3 * D : 4 * D, :].T
    self_out[...] = flat[4 * D : 5 * D, :].T
    start = 3 * D
    self_bias[...] = flat_self[start : start + 2, :]
    cross_bias[...] = flat_self[start + 2 : start + 4, :]
    for block in range(4):
        ffn_bias[:, lanes(block)] = flat_self[start + 4 + block : start + 5 + block, :]
    for target, order in ((out_bias, (8, 5, 2)), (gain, (6, 3, 0)), (moved, (7, 4, 1))):
        for index, number in enumerate(order):
            for block in range(4):
                row = start + 8 + number * 4 + block
                target[index : index + 1, lanes(block)] = flat_self[row : row + 1, :]


def call(kernel, outs, inputs, scratch=(), smem_in=(), any_in=(), any_out=(), smem_out=(), long=False):
    def space(index, smem, hbm):
        return pltpu.SMEM if index in smem else pl.ANY if index in hbm else pltpu.VMEM

    return pl.pallas_call(
        kernel,
        out_shape=[jax.ShapeDtypeStruct(shape, dtype) for shape, dtype in outs],
        in_specs=[
            pl.BlockSpec(memory_space=space(index, smem_in, any_in)) for index in range(len(inputs))
        ],
        out_specs=[
            pl.BlockSpec(memory_space=space(index, smem_out, any_out)) for index in range(len(outs))
        ],
        scratch_shapes=list(scratch),
        compiler_params=pltpu.CompilerParams(vmem_limit_bytes=VMEM_LIMIT),
        cost_estimate=pl.CostEstimate(
            flops=10**13 if long else 10**6, bytes_accessed=1 << (30 if long else 14),
            transcendentals=0,
        ),
    )(*inputs)


def after(value, *others):
    flat, tree = jax.tree.flatten(value)
    tied = lax.optimization_barrier(tuple(flat) + tuple(others))
    return jax.tree.unflatten(tree, tied[: len(flat)])


def body(
    query_stream, content_stream, encoder, dec_segments, enc_segments, key_rank, observe_limit,
    padding, self_proj, self_bias, self_out, cross_proj, cross_bias, cross_out, ffn_in,
    ffn_in_bias, ffn_out, out_bias, norm_gain, norm_bias, cotangent,
):
    members = lax.axis_size("mp")
    groups = lax.axis_size("dp")
    length = dec_segments.shape[1]
    sources = enc_segments.shape[1]
    DMA = pltpu.SemaphoreType.DMA

    def swap(value, axis, mask):
        size = members if axis == "mp" else groups
        return lax.ppermute(value, axis, [(i, i ^ mask) for i in range(size)])

    def along(values):
        return [swap(value, "mp", shift + 1) for shift, value in enumerate(values)]

    def across(values):
        return [swap(value, "dp", 2 * shift + 2) for shift, value in enumerate(values)]

    own12, own3, cot_send, small = call(
        pack_kernel,
        [
            ((512 + EXT, PAIR), BF), ((2 * D // SUB, D), BF), ((2 * TQ, D), BF),
            ((EXT, PAIR), BF),
        ],
        (
            self_proj, self_out, cross_proj, cross_out, ffn_in, ffn_out, self_bias, cross_bias,
            ffn_in_bias.reshape(1, D), cotangent,
        ),
    )
    line12 = along([own12] * 3)
    scal, mask, mask_t, hot, kaug_dec, kaug_enc, vecs = call(
        prep_kernel,
        [
            ((2 + 4 * TILES,), jnp.int32), ((OWN, length), F32), ((length, OWN), F32),
            ((OWN, PAIR), BF), ((length, PAIR), BF), ((sources, PAIR), BF), ((EXT, D), F32),
        ],
        (
            dec_segments, enc_segments, key_rank, observe_limit, padding, out_bias, norm_gain,
            norm_bias,
        ),
        [pltpu.VMEM((8, length), F32)],
        smem_out=(0,),
    )
    line12, hot = after((line12, hot))
    line1 = jnp.stack([value[: 256 + EXT] for value in line12])
    line2 = jnp.stack([value[256 + EXT :] for value in line12])
    plane1, line3 = after((across([line1] * 3), along([after(own3, line1)] * 3)))
    plane1 = jnp.stack([line1] + plane1)
    line3 = jnp.stack(line3)
    other1 = swap(plane1, "dp", 1)
    cot_got = swap(after(cot_send, line1), "mp", 1)
    plane2 = across([after(line2, plane1)] * 3)

    def attention_outs(keys):
        return [
            ((OWN, D), BF), ((keys, D), BF), ((keys, D), BF), ((2 * PAIRS, OWN, PAIR), BF),
            ((OWN, D), BF), ((OWN, D), F32), ((OWN, D), F32), ((4, D, D), BF),
        ]

    def attention_scratch(keys):
        return [
            pltpu.VMEM((PAIRS, 2 * TQ, keys), F32), pltpu.VMEM((PAIRS, 2 * TQ, PAIR), F32),
            pltpu.VMEM((PAIRS, 2 * TQ, 2 * PAIR), F32),
        ]

    def backward_scratch(keys, masked=False):
        shapes = [
            pltpu.VMEM((keys, D), F32), pltpu.VMEM((keys, D), F32),
            pltpu.VMEM((PAIRS, 2 * TQ, PAIR), F32), pltpu.VMEM((2, keys, D), BF),
            pltpu.VMEM((OWN, D), BF), pltpu.VMEM((keys, D), BF), pltpu.VMEM((keys, D), BF),
            pltpu.VMEM((2 * PAIRS, OWN, PAIR), BF), pltpu.VMEM((OWN, D), F32),
        ]
        if masked:
            shapes.append(pltpu.VMEM((keys, OWN), F32))
        return shapes + [pltpu.VMEM((keys, PAIR), BF), DMA((8,))]

    q1, k1, v1, qaug1, ctx1, exact1, s1, weight1, bias = call(
        self_forward_kernel,
        attention_outs(length) + [((EXT, D), F32)],
        (
            scal, query_stream, content_stream, mask, hot, kaug_dec, vecs, small, self_proj,
            self_out, plane1, other1,
        ),
        attention_scratch(length)
        + [
            pltpu.VMEM((PAIRS - 1, EXT, PAIR), BF), pltpu.VMEM((OWN, D), BF),
            pltpu.VMEM((length, D), BF), pltpu.VMEM((length, D), BF), pltpu.VMEM((length, D), BF),
            pltpu.VMEM((4, D, D), BF), pltpu.VMEM((OWN, length), F32), DMA((41,)), DMA((3,)),
        ],
        smem_in=(0,), any_in=(1, 2, 3, 8, 10, 11), any_out=(1, 2, 7),
    )
    plane2, s1, cot_got = after((plane2, s1, cot_got))
    plane2 = jnp.stack([line2] + plane2)
    plane3 = across([after(line3, plane2)] * 3)
    other2 = swap(plane2, "dp", 1)
    q2, k2, v2, qaug2, ctx2, exact2, s2, weight2 = call(
        cross_forward_kernel,
        attention_outs(sources),
        (
            scal, s1, encoder, hot, kaug_enc, vecs, bias, cross_proj, cross_out, plane2, other2,
        ),
        attention_scratch(sources)
        + [
            pltpu.VMEM((sources, D), BF), pltpu.VMEM((sources, D), BF), pltpu.VMEM((sources, D), BF),
            pltpu.VMEM((4, D, D), BF), DMA((33,)), DMA((3,)),
        ],
        smem_in=(0,), any_in=(2, 7, 9, 10), any_out=(1, 2, 7),
    )
    plane3, s2 = after((plane3, s2))
    plane3 = jnp.stack([line3] + plane3)
    other3 = swap(plane3, "dp", 1)

    def group_outs(rows, width):
        return [((4, 4, rows // SUB, width), BF)] * 2

    output_own, mine3, theirs3, dss2, sums, output_send = call(
        ffn_kernel,
        [((OWN, D), BF)]
        + group_outs(2 * D, D)
        + [((OWN, D), F32), ((EXT, D), F32), ((2 * TQ, D), BF)],
        (s2, cotangent, cot_got, bias, vecs, ffn_in, ffn_out, plane3, other3),
        [
            pltpu.VMEM((2, 4, D, D), BF), pltpu.VMEM((OWN, 4 * D), BF),
            pltpu.VMEM((OWN, 4 * D), F32), pltpu.VMEM((OWN, D), BF), pltpu.VMEM((4, 2 * D, D), BF),
            pltpu.VMEM((OWN, D), BF), DMA((26,)), DMA((3,)),
        ],
        any_in=(1, 2, 5, 6, 7, 8), any_out=(1, 2),
    )

    def add_split(mine, theirs):
        shape = mine.shape[1:]
        return call(add_split_kernel, [(shape, BF)] * 4, (mine, theirs))

    def sum_split(parts):
        shape = parts[0].shape[1:]
        return call(sum_split_kernel, [(shape, BF)] * 4, tuple(parts))

    def sum_parts(parts):
        piece = call(sum_kernel, [(parts[0].shape, F32 if groups > SUB else BF)], tuple(parts))[0]
        bit = SUB
        while bit < groups:
            piece = piece + swap(piece, "dp", bit)
            bit *= 2
        return piece.astype(BF)

    theirs3 = swap(theirs3, "dp", 1)
    dq2, dk2, dv2, enc_keep, enc_send = call(
        cross_attention_grad_kernel,
        [((OWN, D), BF), ((sources, D), BF), ((sources, D), BF)] + [((sources // 2, D), BF)] * 2,
        (scal, dss2, weight2, q2, k2, v2, qaug2, exact2, kaug_enc),
        [pltpu.VMEM((OWN, D), BF), pltpu.VMEM((4, D, D), BF), pltpu.VMEM((sources, D), BF)]
        + backward_scratch(sources),
        smem_in=(0,), any_in=(2, 3, 4, 5, 6, 7, 8), any_out=(1, 2, 3, 4), long=True,
    )
    output_got = swap(output_send, "mp", 1)
    theirs3, dq2, output_got = after((theirs3, dq2, output_got))
    parts3 = add_split(mine3, theirs3)
    dq2 = after(dq2, parts3[0])
    moved3 = across(parts3[1:])
    enc_theirs = swap(enc_send, "mp", 1)
    mine2, theirs2, fsg, grad_ctx1, sums = call(
        cross_projection_grad_kernel,
        group_outs(5 * D, PAIR) + [((OWN, D), F32), ((OWN, D), BF), ((EXT, D), F32)],
        (dss2, s1, weight2, weight1, ctx2, ctx1, dq2, dk2, dv2, encoder, vecs, sums),
        [
            pltpu.VMEM((PAIRS, 5 * D, PAIR), BF), pltpu.VMEM((sources, D), BF),
            pltpu.VMEM((2, D, D), BF), pltpu.VMEM((sources, D), BF), pltpu.VMEM((sources, D), BF),
            DMA((8,)),
        ],
        any_in=(2, 3, 7, 8, 9), any_out=(0, 1), long=True,
    )
    theirs2 = swap(theirs2, "dp", 1)
    dq1, dk1, dv1 = call(
        self_attention_grad_kernel,
        [((OWN, D), BF), ((length, D), BF), ((length, D), BF)],
        (scal, grad_ctx1, q1, k1, v1, qaug1, exact1, mask_t, kaug_dec),
        backward_scratch(length, True),
        smem_in=(0,), any_in=(2, 3, 4, 5, 6, 7, 8), any_out=(1, 2), long=True,
    )
    moved3, theirs2, enc_theirs, dq1 = after((moved3, theirs2, enc_theirs, dq1))
    slots3 = sum_split([parts3[0]] + moved3)
    parts2 = add_split(mine2, theirs2)
    dq1 = after(dq1, slots3[0], parts2[0])
    moved_slots3 = along(slots3[1:])
    moved2 = across(parts2[1:])
    mine1, theirs1, content_keep, rows_send, query_own = call(
        self_projection_grad_kernel,
        group_outs(3 * D + SUB * EXT, PAIR)
        + [((length // 2, D), BF), ((length // 2 + 2 * TQ, D), BF), ((OWN, D), BF)],
        (fsg, weight1, dq1, dk1, dv1, query_stream, content_stream, sums),
        [
            pltpu.VMEM((PAIRS, 3 * D + SUB * EXT, PAIR), BF), pltpu.VMEM((length, D), BF),
            pltpu.VMEM((OWN, D), BF), pltpu.VMEM((length, D), BF), pltpu.VMEM((4, D, D), BF),
            DMA((8,)), DMA((2,)),
        ],
        any_in=(1, 5, 6), any_out=(0, 1), long=True,
    )
    theirs1, moved_slots3, moved2 = after((theirs1, moved_slots3, moved2))
    theirs1 = swap(theirs1, "dp", 1)
    rows_got = swap(rows_send, "mp", 1)
    parts1 = add_split(mine1, theirs1)
    moved1 = across(parts1[1:])
    piece3 = sum_parts([slots3[0]] + moved_slots3)
    encoder_grad = (enc_keep.astype(F32) + enc_theirs.astype(F32)).astype(BF)
    piece3, moved1, encoder_grad = after((piece3, moved1, encoder_grad))
    slots = call(
        sum_merge_kernel,
        [((parts2[0].shape[1] + parts1[0].shape[1], PAIR), BF)] * 4,
        (parts2[0], *moved2, parts1[0], *moved1),
    )
    ffn_line = across([piece3] * 3)
    moved_slots, rows_got, ffn_line = after((along(slots[1:]), rows_got, ffn_line))
    piece = sum_parts([slots[0]] + moved_slots)
    ffn_line = jnp.stack([piece3] + ffn_line)
    ffn_other = swap(ffn_line, "dp", 1)
    output, query_grad, content_grad = call(
        finish_rows_kernel,
        [((OWN, D), BF), ((OWN, D), BF), ((length // 2, D), BF)],
        (output_own, output_got, query_own, content_keep, rows_got),
    )
    line, ffn_other, content_grad = after((across([piece] * 3), ffn_other, content_grad))
    line = jnp.stack([piece] + line)
    other = swap(line, "dp", 1)
    ffn_in_grad, ffn_out_grad = call(
        finish_ffn_kernel,
        [((D, D), F32), ((D, D), F32)],
        (ffn_line, ffn_other),
        [pltpu.VMEM((2 * D, D), F32)],
    )

    (
        self_proj_grad, self_bias_grad, self_out_grad, cross_proj_grad, cross_bias_grad,
        cross_out_grad, ffn_bias_grad, out_bias_grad,
        gain_grad, shift_grad,
    ) = call(
        finish_kernel,
        [
            ((3, D, PAIR), F32), ((2, PAIR), F32), ((PAIR, D), F32), ((3, D, PAIR), F32),
            ((2, PAIR), F32), ((PAIR, D), F32), ((1, D), F32),
            ((3, D), F32), ((3, D), F32), ((3, D), F32),
        ],
        (line, other),
        [
            pltpu.VMEM((5 * D, PAIR), F32), pltpu.VMEM((3 * D + SUB * EXT, PAIR), F32),
        ],
    )
    return (
        output,
        query_grad,
        content_grad,
        encoder_grad,
        self_proj_grad,
        self_bias_grad,
        self_out_grad,
        cross_proj_grad,
        cross_bias_grad,
        cross_out_grad,
        ffn_in_grad,
        ffn_bias_grad.reshape(D),
        ffn_out_grad,
        out_bias_grad,
        gain_grad,
        shift_grad,
    )


def solution(mesh):
    return jax.shard_map(
        body,
        mesh=mesh,
        in_specs=(
            P("dp", None), P("dp", None), P("dp", None), P("dp", None), P("dp", None),
            P("dp", None), P("dp", None), P("dp", None), P(None, None, "mp"), P(None, "mp"),
            P("mp", None), P(None, None, "mp"), P(None, "mp"), P("mp", None), P(None, "mp"),
            P("mp"), P("mp", None), P(), P(), P(), P(("dp", "mp"), None),
        ),
        out_specs=(
            P(("dp", "mp"), None), P(("dp", "mp"), None), P(("dp", "mp"), None),
            P(("dp", "mp"), None), P(None, None, "mp"), P(None, "mp"), P("mp", None),
            P(None, None, "mp"), P(None, "mp"), P("mp", None), P(None, "mp"), P("mp"),
            P("mp", None), P(), P(), P(),
        ),
        check_vma=False,
    )
```

```python
import math

import jax
import jax.numpy as jnp
from jax import lax
from jax.experimental import pallas as pl
from jax.experimental.pallas import tpu as pltpu
from jax.sharding import PartitionSpec as P

HEAD = 64
EPSILON = 1e-05
MASKED = -1000000000.0
LOG2E = math.log2(math.e)
D = 512
PAIR = 128
PAIRS = 4
OWN = 512
TQ = 128
ROW_TILES = 8
TK = 256
TILES = OWN // TQ
SUB = 8
EXT = 16
BF = jnp.bfloat16
F32 = jnp.float32
VMEM_LIMIT = 56 * 1024 * 1024


def mm(left, right):
    return jnp.dot(left, right, preferred_element_type=F32)


def mm_rows(left, right):
    return lax.dot_general(left, right, (((0,), (0,)), ((), ())), preferred_element_type=F32)


def mm_cols(left, right):
    return lax.dot_general(left, right, (((1,), (1,)), ((), ())), preferred_element_type=F32)


def norm_parts(summed):
    average = jnp.mean(summed, axis=-1, keepdims=True)
    centred = summed - average
    inverse = lax.rsqrt(jnp.mean(centred * centred, axis=-1, keepdims=True) + EPSILON)
    return centred * inverse, inverse


def norm_backward(incoming, normed, inverse, gain):
    scaled = incoming * gain
    inner = (
        scaled
        - jnp.mean(scaled, axis=-1, keepdims=True)
        - normed * jnp.mean(scaled * normed, axis=-1, keepdims=True)
    )
    return inner * inverse


def col_sum(values):
    return jnp.sum(values.astype(F32), axis=0, keepdims=True)


def half_lanes(rows):
    return lax.broadcasted_iota(jnp.int32, (rows, PAIR), 1) < HEAD


def stack_heads(values):
    keep = half_lanes(values.shape[0])
    zero = jnp.zeros_like(values)
    return jnp.concatenate([jnp.where(keep, values, zero), jnp.where(keep, zero, values)], axis=0)


def pieces_of(value, first_lane, base):
    lane = lax.broadcasted_iota(jnp.int32, value.shape, 1)
    high = value.astype(BF)
    rest = value - high.astype(F32)
    middle = rest.astype(BF)
    low = (rest - middle.astype(F32)).astype(BF)
    out = jnp.where(lane == first_lane, high, base)
    out = jnp.where(lane == first_lane + 1, middle, out)
    return jnp.where(lane == first_lane + 2, low, out)


def lanes(pair):
    return slice(pair * PAIR, (pair + 1) * PAIR)


def key_range(scal, which, tile):
    base = pl.multiple_of(scal[2 + which * 2 * TILES + tile], PAIR)
    count = scal[2 + which * 2 * TILES + TILES + tile]
    return base, count


def over_keys(count, block):
    done = 0
    for wide in (4, 2, 1):
        whole = (count - done) // wide

        def step(index, carry, done=done, wide=wide):
            block((done + index * wide) * TK, wide * TK)
            return carry

        lax.fori_loop(0, whole, step, 0)
        done = done + whole * wide


def attend_forward(scal, which, q, k, v, kaug, hot, mask, score, peak, mixed, qaug, ctx, exact):
    def tile_body(tile, carry):
        base, count = key_range(scal, which, tile)
        rows = pl.ds(pl.multiple_of(tile * TQ, TQ), TQ)
        extra = hot[rows, :]
        extra2 = jnp.concatenate([extra, extra], axis=0)
        peak[...] = jnp.full(peak.shape, -jnp.inf, F32)
        mixed[...] = jnp.zeros(mixed.shape, F32)

        def scores(begin, size):
            off = pl.multiple_of(base + begin, PAIR)
            here = pl.ds(pl.multiple_of(begin, TK), size)
            ka = kaug[pl.ds(off, size), :]
            if mask is not None:
                block = mask[rows, pl.ds(off, size)]
                block = jnp.concatenate([block, block], axis=0)
            for pair in range(PAIRS):
                q2 = jnp.concatenate([stack_heads(q[rows, lanes(pair)]), extra2], axis=1)
                kk = jnp.concatenate([k[pl.ds(off, size), lanes(pair)], ka], axis=1)
                s = mm_cols(q2, kk)
                if mask is not None:
                    s = s + block
                score[pair, :, here] = s
                top = peak[pair]
                for part in range(size // PAIR):
                    top = jnp.maximum(top, s[:, part * PAIR : (part + 1) * PAIR])
                peak[pair] = top

        over_keys(count, scores)
        for pair in range(PAIRS):
            peak[pair] = jnp.broadcast_to(
                jnp.max(peak[pair], axis=1, keepdims=True), (2 * TQ, PAIR)
            )

        def weights(begin, size):
            off = pl.multiple_of(base + begin, PAIR)
            here = pl.ds(pl.multiple_of(begin, TK), size)
            minus = jnp.full((size, PAIR), -1.0, BF)
            for pair in range(PAIRS):
                top = jnp.concatenate([peak[pair]] * (size // PAIR), axis=1)
                p = jnp.exp2((score[pair, :, here] - top) * LOG2E).astype(BF)
                vv = jnp.concatenate([v[pl.ds(off, size), lanes(pair)], minus], axis=1)
                mixed[pair] += mm(p, vv)

        over_keys(count, weights)
        keep = half_lanes(TQ)
        for pair in range(PAIRS):
            both = mixed[pair]
            total = -both[:, PAIR:]
            normal = both[:, :PAIR] / total
            out = jnp.where(keep, normal[:TQ], normal[TQ:])
            exact[rows, lanes(pair)] = out
            ctx[rows, lanes(pair)] = out.astype(BF)
            logsum = peak[pair] + jnp.log(total)
            for head in range(2):
                part = logsum[head * TQ : (head + 1) * TQ]
                qaug[2 * pair + head, rows, :] = pieces_of(part, 4, extra)
        return carry

    lax.fori_loop(0, TILES, tile_body, 0)


def attend_backward(scal, which, q, k, v, kaug, qaug, mask_t, grad, exact, dq, dk, dv, dq_tile):
    def tile_body(tile, carry):
        base, count = key_range(scal, which, tile)
        start = pl.multiple_of(tile * TQ, TQ)
        rows = pl.ds(start, TQ)
        dq_tile[...] = jnp.zeros(dq_tile.shape, F32)
        keep = half_lanes(TQ)
        grads, queries, grad_aug, query_aug = [], [], [], []
        for pair in range(PAIRS):
            g = grad[rows, lanes(pair)]
            inner = g.astype(F32) * exact[rows, lanes(pair)]
            first = jnp.sum(jnp.where(keep, inner, 0.0), axis=1, keepdims=True)
            second = jnp.sum(jnp.where(keep, 0.0, inner), axis=1, keepdims=True)
            delta = jnp.broadcast_to(jnp.concatenate([first, second], axis=0), (2 * TQ, PAIR))
            aug = pieces_of(delta, 0, jnp.zeros((2 * TQ, PAIR), BF))
            g2 = stack_heads(g)
            q2 = stack_heads(q[rows, lanes(pair)])
            grads.append(g2)
            queries.append(q2)
            grad_aug.append(jnp.concatenate([g2, aug], axis=1))
            qa = jnp.concatenate([qaug[2 * pair, rows, :], qaug[2 * pair + 1, rows, :]], axis=0)
            query_aug.append(jnp.concatenate([q2, qa], axis=1))

        def keys(begin, size):
            off = pl.multiple_of(base + begin, PAIR)
            here = pl.ds(off, size)
            ka = kaug[here, :]
            minus = jnp.full((size, PAIR), -1.0, BF)
            if mask_t is not None:
                block = mask_t[here, rows]
                block = jnp.concatenate([block, block], axis=1)

            def raw(pair):
                kp = k[here, lanes(pair)]
                vp = jnp.concatenate([v[here, lanes(pair)], minus], axis=1)
                s = mm_cols(jnp.concatenate([kp, ka], axis=1), query_aug[pair])
                return kp, s, mm_cols(vp, grad_aug[pair])

            ready = raw(0)
            for pair in range(PAIRS):
                kp, s, dp = ready
                if pair + 1 < PAIRS:
                    ready = raw(pair + 1)
                if mask_t is not None:
                    s = s + block
                p = jnp.exp2(s * LOG2E)
                ds = (p * dp).astype(BF)
                dv[here, lanes(pair)] += mm(p.astype(BF), grads[pair])
                dk[here, lanes(pair)] += mm(ds, queries[pair])
                dq_tile[pair] += mm_rows(ds, kp)

        over_keys(count, keys)
        for pair in range(PAIRS):
            both = dq_tile[pair] * HEAD ** (-0.5)
            dq[rows, lanes(pair)] = jnp.where(keep, both[:TQ], both[TQ:]).astype(BF)
        return carry

    lax.fori_loop(0, TILES, tile_body, 0)


def mesh_place():
    group = lax.axis_index("dp")
    return group % 2, (group // 2) % 4, lax.axis_index("mp")


def run_copies(copies):
    for copy in copies:
        copy.start()
    for copy in copies:
        copy.wait()


def load_weights(proj, out, mine, other, weight, sem):
    core, place, _ = mesh_place()
    copies = []
    for matrix in range(3):
        copies.append(
            pltpu.make_async_copy(
                proj.at[matrix], weight.at[matrix, :, lanes(0)], sem.at[len(copies)]
            )
        )
    for side, source in ((core, mine), (1 - core, other)):
        for shift in range(4):
            spot = jnp.bitwise_xor(place, shift)
            matrix = 2 * side + spot // 2
            row = pl.multiple_of((spot % 2) * 256, 256)
            for pair in range(1, PAIRS):
                copies.append(
                    pltpu.make_async_copy(
                        source.at[shift, pair - 1, pl.ds(0, 256), :],
                        weight.at[matrix, pl.ds(row, 256), lanes(pair)],
                        sem.at[len(copies)],
                    )
                )
    weight[3, :, lanes(0)] = out[...].astype(F32).T.astype(BF)
    return copies


def put(source, target, sem):
    copy = pltpu.make_async_copy(source, target, sem)
    copy.start()
    return copy


def own_tiles(source, target, sem, first):
    _, _, position = mesh_place()
    copies = []
    for tile in range(TILES):
        row = pl.multiple_of((position // 2 * ROW_TILES + 2 * tile + position % 2) * TQ, TQ)
        copies.append(
            pltpu.make_async_copy(
                source.at[pl.ds(row, TQ), :], target.at[tile * TQ : (tile + 1) * TQ, :],
                sem.at[first + tile],
            )
        )
    return copies


def grad_copies(buffer, mine, theirs, sem):
    core, place, _ = mesh_place()
    chunk = buffer.shape[1] // SUB
    copies = []
    for side, target in ((core, mine), (1 - core, theirs)):
        for shift in range(4):
            row = pl.multiple_of((4 * side + jnp.bitwise_xor(place, shift)) * chunk, 16)
            copies.append(
                pltpu.make_async_copy(
                    buffer.at[:, pl.ds(row, chunk), :], target.at[shift], sem.at[len(copies)]
                )
            )
    return copies


def send_grads(buffer, mine, theirs, sem):
    run_copies(grad_copies(buffer, mine, theirs, sem))


def send_rows(buffer, keep, theirs, sem):
    part = lax.axis_index("mp") % 2
    rows = buffer.shape[0] // 2
    copies = []
    for side, target in ((part, keep), (1 - part, theirs)):
        row = pl.multiple_of(side * rows, 16)
        copies.append(
            pltpu.make_async_copy(buffer.at[pl.ds(row, rows), :], target, sem.at[len(copies)])
        )
    run_copies(copies)


def pack_kernel(
    self_proj, self_out, cross_proj, cross_out, ffn_in, ffn_out, self_bias, cross_bias, ffn_bias, cot,
    own, own3, cot_send, small,
):
    core, place, position = mesh_place()
    for index in range(2):
        row = pl.multiple_of((1 - position % 2 + 2 * index) * TQ, TQ)
        cot_send[index * TQ : (index + 1) * TQ, :] = cot[pl.ds(row, TQ), :]
    chunk = 4 * core + place
    matrix, half = chunk // 2, chunk % 2
    for proj, out, base in ((self_proj, self_out, 0), (cross_proj, cross_out, 256 + EXT)):

        @pl.when(matrix < 3)
        def _(proj=proj, base=base):
            own[base : base + 256, :] = proj[matrix, pl.ds(pl.multiple_of(half * 256, 256), 256), :]

        @pl.when(matrix == 3)
        def _(out=out, base=base):
            block = out[:, pl.ds(pl.multiple_of(half * 256, 256), 256)]
            own[base : base + 256, :] = block.astype(F32).T.astype(BF)

    rows = [self_bias[...].astype(F32), cross_bias[...].astype(F32)]
    rows += [ffn_bias[:, lanes(block)].astype(F32) for block in range(4)]
    rows += [jnp.zeros((8, PAIR), F32)]
    small[...] = jnp.concatenate(rows, axis=0).astype(BF)
    own[256 : 256 + EXT, :] = small[...]
    rows = own3.shape[0]
    row = chunk * rows

    @pl.when(row < D)
    def _():
        own3[...] = ffn_in[pl.ds(pl.multiple_of(row, rows), rows), :]

    @pl.when(row >= D)
    def _():
        own3[...] = ffn_out[pl.ds(pl.multiple_of(row - D, rows), rows), :]


def prep_kernel(
    dec, enc, ranks, limits, padded, out_bias, gain, shift,
    scal, mask, mask_t, hot, kaug_dec, kaug_enc, vecs, table,
):
    _, _, position = mesh_place()
    row, part = position // 2, position % 2
    length, sources = dec.shape[1], enc.shape[1]
    seg = dec[pl.ds(row, 1), :]
    seg_enc = enc[pl.ds(row, 1), :]
    place = lax.broadcasted_iota(jnp.int32, (1, length), 1)
    begins = (place == 0) | (seg != pltpu.roll(seg, 1, 1))
    rank = jnp.where(padded[pl.ds(row, 1), :] == 0, ranks[pl.ds(row, 1), :], length)
    table[...] = jnp.zeros(table.shape, F32)
    table[0:1, :] = seg.astype(F32)
    table[1:2, :] = rank.astype(F32)
    table[2:3, :] = begins.astype(F32)
    table[3:4, :] = limits[pl.ds(row, 1), :].astype(F32)
    table[4:5, :] = place.astype(F32)
    own = jnp.concatenate(
        [
            table[:, pl.ds(pl.multiple_of((2 * tile + part) * TQ, TQ), TQ)]
            for tile in range(TILES)
        ],
        axis=1,
    )
    own_t = own.T
    every = table[...]
    every_t = every.T

    def visible(seg_q, limit_q, place_q, seg_k, rank_k, start_k, place_k):
        chosen = (rank_k < limit_q) & (place_q != place_k)
        return jnp.where((seg_q == seg_k) & ((start_k > 0.5) | chosen), 0.0, MASKED)

    mask[...] = visible(
        own_t[:, 0:1], own_t[:, 3:4], own_t[:, 4:5],
        every[0:1], every[1:2], every[2:3], every[4:5],
    )
    mask_t[...] = visible(
        own[0:1], own[3:4], own[4:5],
        every_t[:, 0:1], every_t[:, 1:2], every_t[:, 2:3], every_t[:, 4:5],
    )

    def key_aug(column):
        lane = lax.broadcasted_iota(jnp.int32, (column.shape[0], PAIR), 1)
        different = (lane < 4) & (column != lane.astype(F32))
        minus = (lane >= 4) & (lane < 7)
        return jnp.where(different, MASKED, jnp.where(minus, -1.0, 0.0)).astype(BF)

    kaug_dec[...] = key_aug(every_t[:, 0:1])
    seg_enc_f = jnp.broadcast_to(seg_enc.astype(F32), (8, sources))
    kaug_enc[...] = key_aug(seg_enc_f.T[:, 0:1])
    lane = lax.broadcasted_iota(jnp.int32, (OWN, PAIR), 1)
    hot[...] = (own_t[:, 0:1] == lane.astype(F32)).astype(F32).astype(BF)
    vecs[...] = jnp.zeros(vecs.shape, F32)
    for index, source in enumerate((out_bias, gain, shift)):
        vecs[3 * index : 3 * index + 3, :] = source[...].astype(F32)
    scal[0] = 0
    scal[1] = 0
    for which, keys in ((0, every[0:1]), (1, seg_enc_f[0:1])):
        size = keys.shape[1]
        for tile in range(TILES):
            block = own[0:1, tile * TQ : (tile + 1) * TQ]
            low, high = jnp.min(block), jnp.max(block)
            begin = jnp.sum((keys < low).astype(F32)).astype(jnp.int32)
            end = jnp.sum((keys <= high).astype(F32)).astype(jnp.int32)
            base = begin // PAIR * PAIR
            count = (end - base + TK - 1) // TK
            scal[2 + which * 2 * TILES + tile] = jnp.minimum(base, size - count * TK)
            scal[2 + which * 2 * TILES + TILES + tile] = count


def fetch(source, target, start, sem):
    return pltpu.make_async_copy(
        source.at[pl.ds(pl.multiple_of(start, target.shape[0]), target.shape[0]), :], target, sem
    )


def project(x, weight, bias, target):
    step = min(x.shape[0], 1024)
    for part in range(x.shape[0] // step):
        rows = slice(part * step, (part + 1) * step)
        value = mm(x[rows, :], weight)
        target[rows, :] = (value if bias is None else value + bias).astype(BF)


def self_forward_kernel(
    scal, query, content, mask_in, hot, kaug, vecs, small, proj, out, mine, other,
    q, k_out, v_out, qaug, ctx, exact, s1, weight_out, bias,
    score, peak, mixed, got, xq, xc, k, v, weight, mask, sem, sem_out,
):
    _, _, position = mesh_place()
    rows = xc.shape[0]
    copies = own_tiles(query, xq, sem, 32)
    copies.append(
        pltpu.make_async_copy(
            content.at[pl.ds(pl.multiple_of(position // 2 * rows, rows), rows), :], xc, sem.at[36]
        )
    )
    for pair in range(1, PAIRS):
        copies.append(
            pltpu.make_async_copy(
                mine.at[0, pair - 1, pl.ds(256, EXT), :], got.at[pair - 1], sem.at[36 + pair]
            )
        )
    late = pltpu.make_async_copy(mask_in, mask, sem.at[40])
    for copy in copies:
        copy.start()
    moves = load_weights(proj, out, mine, other, weight, sem)
    for copy in moves:
        copy.start()
    late.start()
    for copy in copies + moves:
        copy.wait()
    outs = [put(weight, weight_out, sem_out.at[0])]
    bias[:, lanes(0)] = small[...].astype(F32)
    for pair in range(1, PAIRS):
        bias[:, lanes(pair)] = got[pair - 1].astype(F32)
    q[...] = ((mm(xq[...], weight[0]) + bias[0:1, :]).astype(BF) * BF(HEAD ** (-0.5))).astype(BF)
    project(xc, weight[1], None, k)
    outs.append(put(k, k_out, sem_out.at[1]))
    project(xc, weight[2], bias[1:2, :], v)
    outs.append(put(v, v_out, sem_out.at[2]))
    late.wait()
    attend_forward(scal, 0, q, k, v, kaug, hot, mask, score, peak, mixed, qaug, ctx, exact)
    s1[...] = xq[...].astype(F32) + mm_cols(ctx[...], weight[3]) + vecs[0:1, :]
    for copy in outs:
        copy.wait()


def cross_forward_kernel(
    scal, s1, encoder, hot, kaug, vecs, bias, proj, out, mine, other,
    q, k_out, v_out, qaug, ctx, exact, s2, weight_out,
    score, peak, mixed, enc, k, v, weight, sem, sem_out,
):
    _, _, position = mesh_place()
    moves = load_weights(proj, out, mine, other, weight, sem)
    rows = enc.shape[0]
    late = pltpu.make_async_copy(
        encoder.at[pl.ds(pl.multiple_of(position // 2 * rows, rows), rows), :], enc, sem.at[32]
    )
    for copy in moves:
        copy.start()
    late.start()
    normed, _ = norm_parts(s1[...])
    first = normed * vecs[3:4, :] + vecs[6:7, :]
    for copy in moves:
        copy.wait()
    outs = [put(weight, weight_out, sem_out.at[0])]
    q[...] = (
        (mm(first.astype(BF), weight[0]) + bias[2:3, :]).astype(BF) * BF(HEAD ** (-0.5))
    ).astype(BF)
    late.wait()
    project(enc, weight[1], None, k)
    outs.append(put(k, k_out, sem_out.at[1]))
    project(enc, weight[2], bias[3:4, :], v)
    outs.append(put(v, v_out, sem_out.at[2]))
    attend_forward(scal, 1, q, k, v, kaug, hot, None, score, peak, mixed, qaug, ctx, exact)
    s2[...] = first + mm_cols(ctx[...], weight[3]) + vecs[1:2, :]
    for copy in outs:
        copy.wait()


def gelu_parts(v):
    c = math.sqrt(2.0 / math.pi)
    square = v * v
    t = jnp.tanh(c * (v + 0.044715 * square * v))
    value = 0.5 * v * (1.0 + t)
    slope = 0.5 * (1.0 + t) + 0.5 * v * (1.0 - t * t) * (c + (3.0 * 0.044715 * c) * square)
    return value, slope


def ffn_kernel(
    s2, cot_own, cot_got, bias, vecs, ffn_in, ffn_out, first_core, second_core,
    output, mine, theirs, back, sums, output_send,
    weight, hidden, slopes, low, grads, cot, sem, sem_cot,
):
    core, place, position = mesh_place()
    half = position % 2
    late = []
    for index in range(2):
        row = pl.multiple_of((half + 2 * index) * TQ, TQ)
        target = pl.multiple_of((2 * half + index) * TQ, TQ)
        late.append(
            put(cot_own.at[pl.ds(row, TQ), :], cot.at[pl.ds(target, TQ), :], sem_cot.at[index])
        )
    target = pl.multiple_of((1 - half) * 2 * TQ, 2 * TQ)
    late.append(put(cot_got, cot.at[pl.ds(target, 2 * TQ), :], sem_cot.at[2]))
    copies = [[] for _ in range(4)]
    for side, source in enumerate((ffn_in, ffn_out)):
        copies[0].append(put(source, weight.at[side, 0], sem.at[side]))
    for part in range(1, 4):
        for side, source in ((core, first_core), (1 - core, second_core)):
            for shift in range(4):
                row = pl.multiple_of(jnp.bitwise_xor(place, shift) * 128, 128)
                number = 2 + sum(len(group) for group in copies[1:])
                copies[part].append(
                    put(
                        source.at[shift, part - 1], weight.at[side, part, pl.ds(row, 128), :],
                        sem.at[number],
                    )
                )
    sums[...] = jnp.zeros(sums.shape, F32)
    normed2, inverse2 = norm_parts(s2[...])
    second = normed2 * vecs[4:5, :] + vecs[7:8, :]
    low[...] = second.astype(BF)
    total = second + vecs[2:3, :]
    for part in range(4):
        block = slice(part * D, (part + 1) * D)
        part_bias = jnp.concatenate([bias[4 + i : 5 + i, lanes(part)] for i in range(4)], axis=1)
        for copy in copies[part]:
            copy.wait()
        pre = mm(low[...], weight[0, part]) + part_bias
        value, slope = gelu_parts(pre)
        hidden[:, block] = value.astype(BF)
        slopes[:, block] = slope
        total = total + mm(hidden[:, block], weight[1, part])
    normed3, inverse3 = norm_parts(total)
    output[...] = (normed3 * vecs[5:6, :] + vecs[8:9, :]).astype(BF)
    for copy in late:
        copy.wait()
    row = pl.multiple_of((1 - half) * 2 * TQ, 2 * TQ)
    output_send[...] = output[pl.ds(row, 2 * TQ), :]
    incoming = cot[...].astype(F32)
    sums[0:1, :] = col_sum(incoming * normed3)
    sums[1:2, :] = col_sum(incoming)
    third_grad = norm_backward(incoming, normed3, inverse3, vecs[5:6, :])
    branch = third_grad.astype(BF)
    sums[2:3, :] = col_sum(branch)
    total = third_grad
    for part in range(4):
        block = slice(part * D, (part + 1) * D)
        pre_grad = (slopes[:, block] * mm_cols(branch, weight[1, part])).astype(BF)
        sums[8 + part : 9 + part, :] = col_sum(pre_grad)
        grads[part, 0:D, :] = mm_rows(low[...], pre_grad).astype(BF)
        grads[part, D : 2 * D, :] = mm_rows(hidden[:, block], branch).astype(BF)
        if part == 3:
            moves = grad_copies(grads, mine, theirs, sem)
            for copy in moves:
                copy.start()
        total = total + mm_cols(pre_grad, weight[0, part])
    sums[3:4, :] = col_sum(total * normed2)
    sums[4:5, :] = col_sum(total)
    second_grad = norm_backward(total, normed2, inverse2, vecs[4:5, :])
    sums[5:6, :] = col_sum(second_grad.astype(BF))
    back[...] = second_grad
    for copy in moves:
        copy.wait()


def store_grad(grads, matrix, value):
    low = value.astype(BF)
    for pair in range(PAIRS):
        grads[pair, matrix * D : (matrix + 1) * D, :] = low[:, lanes(pair)]


def projection_grads(grads, x, low, matrix):
    store_grad(grads, matrix, mm_rows(x[...], low[...]))


def input_grads(dk, dv, weight, out):
    step = min(dk.shape[0], 1024)
    for part in range(dk.shape[0] // step):
        rows = slice(part * step, (part + 1) * step)
        out[rows, :] = (
            mm_cols(dk[rows, :], weight[1]) + mm_cols(dv[rows, :], weight[2])
        ).astype(BF)


def load_all(sources, targets, sem):
    copies = [
        pltpu.make_async_copy(source, target, sem.at[index])
        for index, (source, target) in enumerate(zip(sources, targets))
    ]
    for copy in copies:
        copy.start()
    return copies


def store_low(dk, dv, dk_low, dv_low, low, sem):
    copies = []
    for index, (value, target) in enumerate(((dk, dk_low), (dv, dv_low))):
        for part in range(value.shape[0] // 512):
            rows = slice(part * 512, (part + 1) * 512)
            low[index, rows, :] = value[rows, :].astype(BF)
            copies.append(put(low.at[index, rows, :], target.at[rows, :], sem.at[len(copies)]))
    return copies


def cross_attention_grad_kernel(
    scal, dss2, weight_in, q_in, k_in, v_in, qaug_in, exact_in, kaug_in,
    dq, dk_low, dv_low, keep, send,
    grad_ctx, weight, enc_grad, dk, dv, dq_tile, low, q, k, v, qaug, exact, kaug, sem,
):
    first = put(weight_in, weight, sem.at[7])
    copies = load_all(
        (q_in, qaug_in, exact_in, kaug_in, k_in, v_in), (q, qaug, exact, kaug, k, v), sem
    )
    dk[...] = jnp.zeros(dk.shape, F32)
    dv[...] = jnp.zeros(dv.shape, F32)
    first.wait()
    grad_ctx[...] = mm(dss2[...].astype(BF), weight[3]).astype(BF)
    for copy in copies:
        copy.wait()
    attend_backward(scal, 1, q, k, v, kaug, qaug, None, grad_ctx, exact, dq, dk, dv, dq_tile)
    copies = store_low(dk, dv, dk_low, dv_low, low, sem)
    input_grads(low.at[0], low.at[1], weight, enc_grad)
    for copy in copies:
        copy.wait()
    send_rows(enc_grad, keep, send, sem)


def cross_projection_grad_kernel(
    dss2, s1, weight_in, self_weight, ctx, self_ctx, dq, dk_in, dv_in, encoder, vecs, sums_in,
    mine, theirs, back, grad_ctx, sums,
    grads, enc, weight, dk, dv, sem,
):
    _, _, position = mesh_place()
    rows = enc.shape[0]
    start = pl.multiple_of(position // 2 * rows, rows)
    early = [
        put(weight_in.at[0], weight.at[0], sem.at[0]),
        put(self_weight.at[3], weight.at[1], sem.at[1]),
    ]
    late = [
        put(encoder.at[pl.ds(start, rows), :], enc, sem.at[2]),
        put(dk_in, dk, sem.at[3]),
        put(dv_in, dv, sem.at[4]),
    ]
    sums[...] = sums_in[...]
    normed, inverse = norm_parts(s1[...])
    first = (normed * vecs[3:4, :] + vecs[6:7, :]).astype(BF)
    store_grad(grads, 0, mm_rows(first, dq[...]))
    store_grad(grads, 3, mm_rows(dss2[...].astype(BF), ctx[...]))
    for copy in early:
        copy.wait()
    total = dss2[...] + mm_cols(dq[...], weight[0])
    sums[6:7, :] = col_sum(total * normed)
    sums[7:8, :] = col_sum(total)
    first_grad = norm_backward(total, normed, inverse, vecs[3:4, :])
    branch = first_grad.astype(BF)
    sums[12:13, :] = col_sum(branch)
    back[...] = first_grad
    grad_ctx[...] = mm(branch, weight[1]).astype(BF)
    store_grad(grads, 4, mm_rows(branch, self_ctx[...]))
    sums[14:15, :] = col_sum(dq[...])
    for copy in late:
        copy.wait()
    projection_grads(grads, enc, dk, 1)
    projection_grads(grads, enc, dv, 2)
    sums[15:16, :] = col_sum(dv[...])
    send_grads(grads, mine, theirs, sem)


def self_attention_grad_kernel(
    scal, grad_ctx, q_in, k_in, v_in, qaug_in, exact_in, mask_in, kaug_in,
    dq, dk_low, dv_low,
    dk, dv, dq_tile, low, q, k, v, qaug, exact, mask_t, kaug, sem,
):
    copies = load_all(
        (q_in, qaug_in, exact_in, kaug_in, k_in, v_in, mask_in),
        (q, qaug, exact, kaug, k, v, mask_t),
        sem,
    )
    dk[...] = jnp.zeros(dk.shape, F32)
    dv[...] = jnp.zeros(dv.shape, F32)
    for copy in copies:
        copy.wait()
    attend_backward(scal, 0, q, k, v, kaug, qaug, mask_t, grad_ctx, exact, dq, dk, dv, dq_tile)
    for copy in store_low(dk, dv, dk_low, dv_low, low, sem):
        copy.wait()


def self_projection_grad_kernel(
    fsg, weight_in, dq, dk, dv, query, content, sums,
    mine, theirs, keep, send, query_grad,
    grads, content_grad, xq, xc, weight, sem, sem_late,
):
    _, _, position = mesh_place()
    half = position % 2
    rows = xc.shape[0]
    copies = own_tiles(query, xq, sem, 0)
    for copy in copies:
        copy.start()
    place = pl.multiple_of(position // 2 * rows, rows)
    content_copy = put(content.at[pl.ds(place, rows), :], xc, sem_late.at[0])
    weight_copy = put(weight_in, weight, sem_late.at[1])
    for copy in copies:
        copy.wait()
    store_grad(grads, 0, mm_rows(xq[...], dq[...]))
    content_copy.wait()
    projection_grads(grads, xc, dk, 1)
    projection_grads(grads, xc, dv, 2)
    bias_q = col_sum(dq[...])
    bias_v = col_sum(dv[...])
    for pair in range(PAIRS):
        parts = [bias_q[:, lanes(pair)], bias_v[:, lanes(pair)]]
        parts += [sums[14:15, lanes(pair)], sums[15:16, lanes(pair)]]
        parts += [sums[8 + pair : 9 + pair, lanes(i)] for i in range(4)]
        for index in (0, 1, 2, 3, 4, 5, 6, 7, 12):
            parts += [sums[index : index + 1, lanes(i)] for i in range(4)]
        parts += [jnp.zeros((SUB * EXT - len(parts), PAIR), F32)]
        grads[pair, 3 * D : 3 * D + SUB * EXT, :] = jnp.concatenate(parts, axis=0).astype(BF)
    moves = grad_copies(grads, mine, theirs, sem)
    for copy in moves:
        copy.start()
    weight_copy.wait()
    input_grads(dk, dv, weight, content_grad)
    query_grad[...] = (fsg[...] + mm_cols(dq[...], weight[0])).astype(BF)
    mid = rows // 2
    keep[...] = content_grad[pl.ds(pl.multiple_of(half * mid, mid), mid), :]
    send[0:mid, :] = content_grad[pl.ds(pl.multiple_of((1 - half) * mid, mid), mid), :]
    row = pl.multiple_of((1 - half) * 2 * TQ, 2 * TQ)
    send[mid:, :] = query_grad[pl.ds(row, 2 * TQ), :]
    for copy in moves:
        copy.wait()


def add_split_kernel(mine, theirs, *outs):
    for index, out in enumerate(outs):
        out[...] = (mine[index].astype(F32) + theirs[index].astype(F32)).astype(BF)


def sum_split_kernel(own, first, second, third, *outs):
    for index, out in enumerate(outs):
        out[...] = (
            (own[index].astype(F32) + first[index].astype(F32))
            + (second[index].astype(F32) + third[index].astype(F32))
        ).astype(BF)


def sum_merge_kernel(a0, a1, a2, a3, b0, b1, b2, b3, *outs):
    rows = a0.shape[1]
    for index, out in enumerate(outs):
        for group, spot in (((a0, a1, a2, a3), slice(0, rows)), ((b0, b1, b2, b3), slice(rows, None))):
            own, first, second, third = [part[index].astype(F32) for part in group]
            out[spot, :] = ((own + first) + (second + third)).astype(BF)


def sum_kernel(own, first, second, third, out):
    out[...] = (
        (own[...].astype(F32) + first[...].astype(F32))
        + (second[...].astype(F32) + third[...].astype(F32))
    ).astype(out.dtype)


def finish_ffn_kernel(line, other, ffn_in, ffn_out, wide):
    core, place, _ = mesh_place()
    for side, source in ((core, line), (1 - core, other)):
        for shift in range(4):
            row = pl.multiple_of((4 * side + jnp.bitwise_xor(place, shift)) * 128, 128)
            wide[pl.ds(row, 128), :] = source[shift].astype(F32)
    ffn_in[...] = wide[0:D, :]
    ffn_out[...] = wide[D:, :]


def finish_rows_kernel(output_own, output_got, query_own, keep, got, output, query, content):
    _, _, position = mesh_place()
    half = position % 2
    mid = keep.shape[0]
    for own, theirs, skip, target in (
        (output_own, output_got, 0, output), (query_own, got, mid, query)
    ):
        for index in range(2):
            row = pl.multiple_of((2 * half + index) * TQ, TQ)
            place_own = pl.multiple_of((half + 2 * index) * TQ, TQ)
            place_got = pl.multiple_of((1 - half + 2 * index) * TQ, TQ)
            first = skip + index * TQ
            target[pl.ds(place_own, TQ), :] = own[pl.ds(row, TQ), :]
            target[pl.ds(place_got, TQ), :] = theirs[first : first + TQ, :]
    content[...] = (keep[...].astype(F32) + got[0:mid, :].astype(F32)).astype(BF)


def finish_kernel(
    line, other,
    self_proj, self_bias, self_out, cross_proj, cross_bias, cross_out, ffn_bias,
    out_bias, gain, moved, flat, flat_self,
):
    core, place, _ = mesh_place()
    cross_rows, self_rows = flat.shape[0] // SUB, flat_self.shape[0] // SUB
    for side, source in ((core, line), (1 - core, other)):
        for shift in range(4):
            spot = 4 * side + jnp.bitwise_xor(place, shift)
            row = pl.multiple_of(spot * cross_rows, 8)
            flat[pl.ds(row, cross_rows), :] = source[shift, 0:cross_rows, :].astype(F32)
            row = pl.multiple_of(spot * self_rows, 8)
            flat_self[pl.ds(row, self_rows), :] = source[shift, cross_rows:, :].astype(F32)
    for matrix in range(3):
        cross_proj[matrix] = flat[matrix * D : (matrix + 1) * D, :]
        self_proj[matrix] = flat_self[matrix * D : (matrix + 1) * D, :]
    cross_out[...] = flat[3 * D : 4 * D, :].T
    self_out[...] = flat[4 * D : 5 * D, :].T
    start = 3 * D
    self_bias[...] = flat_self[start : start + 2, :]
    cross_bias[...] = flat_self[start + 2 : start + 4, :]
    for block in range(4):
        ffn_bias[:, lanes(block)] = flat_self[start + 4 + block : start + 5 + block, :]
    for target, order in ((out_bias, (8, 5, 2)), (gain, (6, 3, 0)), (moved, (7, 4, 1))):
        for index, number in enumerate(order):
            for block in range(4):
                row = start + 8 + number * 4 + block
                target[index : index + 1, lanes(block)] = flat_self[row : row + 1, :]


def call(kernel, outs, inputs, scratch=(), smem_in=(), any_in=(), any_out=(), smem_out=(), long=False):
    def space(index, smem, hbm):
        return pltpu.SMEM if index in smem else pl.ANY if index in hbm else pltpu.VMEM

    return pl.pallas_call(
        kernel,
        out_shape=[jax.ShapeDtypeStruct(shape, dtype) for shape, dtype in outs],
        in_specs=[
            pl.BlockSpec(memory_space=space(index, smem_in, any_in)) for index in range(len(inputs))
        ],
        out_specs=[
            pl.BlockSpec(memory_space=space(index, smem_out, any_out)) for index in range(len(outs))
        ],
        scratch_shapes=list(scratch),
        compiler_params=pltpu.CompilerParams(vmem_limit_bytes=VMEM_LIMIT),
        cost_estimate=pl.CostEstimate(
            flops=10**13 if long else 10**6, bytes_accessed=1 << (30 if long else 14),
            transcendentals=0,
        ),
    )(*inputs)


def after(value, *others):
    flat, tree = jax.tree.flatten(value)
    tied = lax.optimization_barrier(tuple(flat) + tuple(others))
    return jax.tree.unflatten(tree, tied[: len(flat)])


def body(
    query_stream, content_stream, encoder, dec_segments, enc_segments, key_rank, observe_limit,
    padding, self_proj, self_bias, self_out, cross_proj, cross_bias, cross_out, ffn_in,
    ffn_in_bias, ffn_out, out_bias, norm_gain, norm_bias, cotangent,
):
    members = lax.axis_size("mp")
    groups = lax.axis_size("dp")
    length = dec_segments.shape[1]
    sources = enc_segments.shape[1]
    DMA = pltpu.SemaphoreType.DMA

    def swap(value, axis, mask):
        size = members if axis == "mp" else groups
        return lax.ppermute(value, axis, [(i, i ^ mask) for i in range(size)])

    def along(values):
        return [swap(value, "mp", shift + 1) for shift, value in enumerate(values)]

    def across(values):
        return [swap(value, "dp", 2 * shift + 2) for shift, value in enumerate(values)]

    own12, own3, cot_send, small = call(
        pack_kernel,
        [
            ((512 + EXT, PAIR), BF), ((2 * D // SUB, D), BF), ((2 * TQ, D), BF),
            ((EXT, PAIR), BF),
        ],
        (
            self_proj, self_out, cross_proj, cross_out, ffn_in, ffn_out, self_bias, cross_bias,
            ffn_in_bias.reshape(1, D), cotangent,
        ),
    )
    line12 = along([own12] * 3)
    scal, mask, mask_t, hot, kaug_dec, kaug_enc, vecs = call(
        prep_kernel,
        [
            ((2 + 4 * TILES,), jnp.int32), ((OWN, length), F32), ((length, OWN), F32),
            ((OWN, PAIR), BF), ((length, PAIR), BF), ((sources, PAIR), BF), ((EXT, D), F32),
        ],
        (
            dec_segments, enc_segments, key_rank, observe_limit, padding, out_bias, norm_gain,
            norm_bias,
        ),
        [pltpu.VMEM((8, length), F32)],
        smem_out=(0,),
    )
    line12, hot = after((line12, hot))
    line1 = jnp.stack([value[: 256 + EXT] for value in line12])
    line2 = jnp.stack([value[256 + EXT :] for value in line12])
    plane1, line3 = after((across([line1] * 3), along([after(own3, line1)] * 3)))
    plane1 = jnp.stack([line1] + plane1)
    line3 = jnp.stack(line3)
    other1 = swap(plane1, "dp", 1)
    cot_got = swap(after(cot_send, line1), "mp", 1)
    plane2 = across([after(line2, plane1)] * 3)

    def attention_outs(keys):
        return [
            ((OWN, D), BF), ((keys, D), BF), ((keys, D), BF), ((2 * PAIRS, OWN, PAIR), BF),
            ((OWN, D), BF), ((OWN, D), F32), ((OWN, D), F32), ((4, D, D), BF),
        ]

    def attention_scratch(keys):
        return [
            pltpu.VMEM((PAIRS, 2 * TQ, keys), F32), pltpu.VMEM((PAIRS, 2 * TQ, PAIR), F32),
            pltpu.VMEM((PAIRS, 2 * TQ, 2 * PAIR), F32),
        ]

    def backward_scratch(keys, masked=False):
        shapes = [
            pltpu.VMEM((keys, D), F32), pltpu.VMEM((keys, D), F32),
            pltpu.VMEM((PAIRS, 2 * TQ, PAIR), F32), pltpu.VMEM((2, keys, D), BF),
            pltpu.VMEM((OWN, D), BF), pltpu.VMEM((keys, D), BF), pltpu.VMEM((keys, D), BF),
            pltpu.VMEM((2 * PAIRS, OWN, PAIR), BF), pltpu.VMEM((OWN, D), F32),
        ]
        if masked:
            shapes.append(pltpu.VMEM((keys, OWN), F32))
        return shapes + [pltpu.VMEM((keys, PAIR), BF), DMA((8,))]

    q1, k1, v1, qaug1, ctx1, exact1, s1, weight1, bias = call(
        self_forward_kernel,
        attention_outs(length) + [((EXT, D), F32)],
        (
            scal, query_stream, content_stream, mask, hot, kaug_dec, vecs, small, self_proj,
            self_out, plane1, other1,
        ),
        attention_scratch(length)
        + [
            pltpu.VMEM((PAIRS - 1, EXT, PAIR), BF), pltpu.VMEM((OWN, D), BF),
            pltpu.VMEM((length, D), BF), pltpu.VMEM((length, D), BF), pltpu.VMEM((length, D), BF),
            pltpu.VMEM((4, D, D), BF), pltpu.VMEM((OWN, length), F32), DMA((41,)), DMA((3,)),
        ],
        smem_in=(0,), any_in=(1, 2, 3, 8, 10, 11), any_out=(1, 2, 7),
    )
    plane2, s1, cot_got = after((plane2, s1, cot_got))
    plane2 = jnp.stack([line2] + plane2)
    plane3 = across([after(line3, plane2)] * 3)
    other2 = swap(plane2, "dp", 1)
    q2, k2, v2, qaug2, ctx2, exact2, s2, weight2 = call(
        cross_forward_kernel,
        attention_outs(sources),
        (
            scal, s1, encoder, hot, kaug_enc, vecs, bias, cross_proj, cross_out, plane2, other2,
        ),
        attention_scratch(sources)
        + [
            pltpu.VMEM((sources, D), BF), pltpu.VMEM((sources, D), BF), pltpu.VMEM((sources, D), BF),
            pltpu.VMEM((4, D, D), BF), DMA((33,)), DMA((3,)),
        ],
        smem_in=(0,), any_in=(2, 7, 9, 10), any_out=(1, 2, 7),
    )
    plane3, s2 = after((plane3, s2))
    plane3 = jnp.stack([line3] + plane3)
    other3 = swap(plane3, "dp", 1)

    def group_outs(rows, width):
        return [((4, 4, rows // SUB, width), BF)] * 2

    output_own, mine3, theirs3, dss2, sums, output_send = call(
        ffn_kernel,
        [((OWN, D), BF)]
        + group_outs(2 * D, D)
        + [((OWN, D), F32), ((EXT, D), F32), ((2 * TQ, D), BF)],
        (s2, cotangent, cot_got, bias, vecs, ffn_in, ffn_out, plane3, other3),
        [
            pltpu.VMEM((2, 4, D, D), BF), pltpu.VMEM((OWN, 4 * D), BF),
            pltpu.VMEM((OWN, 4 * D), F32), pltpu.VMEM((OWN, D), BF), pltpu.VMEM((4, 2 * D, D), BF),
            pltpu.VMEM((OWN, D), BF), DMA((26,)), DMA((3,)),
        ],
        any_in=(1, 2, 5, 6, 7, 8), any_out=(1, 2),
    )

    def low_sum(*values):
        total = values[0].astype(F32)
        for value in values[1:]:
            total = total + value.astype(F32)
        return total.astype(BF)

    def add_split(mine, theirs):
        return [low_sum(mine[index], theirs[index]) for index in range(4)]

    def sum_split(parts):
        return [low_sum(*[part[index] for part in parts]) for index in range(4)]

    def sum_parts(parts):
        piece = parts[0].astype(F32)
        for part in parts[1:]:
            piece = piece + part.astype(F32)
        bit = SUB
        while bit < groups:
            piece = piece + swap(piece, "dp", bit)
            bit *= 2
        return piece.astype(BF)

    theirs3 = swap(theirs3, "dp", 1)
    dq2, dk2, dv2, enc_keep, enc_send = call(
        cross_attention_grad_kernel,
        [((OWN, D), BF), ((sources, D), BF), ((sources, D), BF)] + [((sources // 2, D), BF)] * 2,
        (scal, dss2, weight2, q2, k2, v2, qaug2, exact2, kaug_enc),
        [pltpu.VMEM((OWN, D), BF), pltpu.VMEM((4, D, D), BF), pltpu.VMEM((sources, D), BF)]
        + backward_scratch(sources),
        smem_in=(0,), any_in=(2, 3, 4, 5, 6, 7, 8), any_out=(1, 2, 3, 4), long=True,
    )
    output_got = swap(output_send, "mp", 1)
    theirs3, dq2, output_got = after((theirs3, dq2, output_got))
    parts3 = add_split(mine3, theirs3)
    dq2 = after(dq2, parts3[0])
    moved3 = across(parts3[1:])
    enc_theirs = swap(enc_send, "mp", 1)
    mine2, theirs2, fsg, grad_ctx1, sums = call(
        cross_projection_grad_kernel,
        group_outs(5 * D, PAIR) + [((OWN, D), F32), ((OWN, D), BF), ((EXT, D), F32)],
        (dss2, s1, weight2, weight1, ctx2, ctx1, dq2, dk2, dv2, encoder, vecs, sums),
        [
            pltpu.VMEM((PAIRS, 5 * D, PAIR), BF), pltpu.VMEM((sources, D), BF),
            pltpu.VMEM((2, D, D), BF), pltpu.VMEM((sources, D), BF), pltpu.VMEM((sources, D), BF),
            DMA((8,)),
        ],
        any_in=(2, 3, 7, 8, 9), any_out=(0, 1), long=True,
    )
    theirs2 = swap(theirs2, "dp", 1)
    dq1, dk1, dv1 = call(
        self_attention_grad_kernel,
        [((OWN, D), BF), ((length, D), BF), ((length, D), BF)],
        (scal, grad_ctx1, q1, k1, v1, qaug1, exact1, mask_t, kaug_dec),
        backward_scratch(length, True),
        smem_in=(0,), any_in=(2, 3, 4, 5, 6, 7, 8), any_out=(1, 2), long=True,
    )
    moved3, theirs2, enc_theirs, dq1 = after((moved3, theirs2, enc_theirs, dq1))
    slots3 = sum_split([parts3[0]] + moved3)
    parts2 = add_split(mine2, theirs2)
    dq1 = after(dq1, slots3[0], parts2[0])
    moved_slots3 = along(slots3[1:])
    moved2 = across(parts2[1:])
    mine1, theirs1, content_keep, rows_send, query_own = call(
        self_projection_grad_kernel,
        group_outs(3 * D + SUB * EXT, PAIR)
        + [((length // 2, D), BF), ((length // 2 + 2 * TQ, D), BF), ((OWN, D), BF)],
        (fsg, weight1, dq1, dk1, dv1, query_stream, content_stream, sums),
        [
            pltpu.VMEM((PAIRS, 3 * D + SUB * EXT, PAIR), BF), pltpu.VMEM((length, D), BF),
            pltpu.VMEM((OWN, D), BF), pltpu.VMEM((length, D), BF), pltpu.VMEM((4, D, D), BF),
            DMA((8,)), DMA((2,)),
        ],
        any_in=(1, 5, 6), any_out=(0, 1), long=True,
    )
    theirs1, moved_slots3, moved2 = after((theirs1, moved_slots3, moved2))
    theirs1 = swap(theirs1, "dp", 1)
    rows_got = swap(rows_send, "mp", 1)
    parts1 = add_split(mine1, theirs1)
    moved1 = across(parts1[1:])
    piece3 = sum_parts([slots3[0]] + moved_slots3)
    encoder_grad = (enc_keep.astype(F32) + enc_theirs.astype(F32)).astype(BF)
    ffn_line = across([piece3] * 3)
    ffn_line, moved1, encoder_grad, rows_got = after((ffn_line, moved1, encoder_grad, rows_got))
    slots = [
        jnp.concatenate(both, axis=0)
        for both in zip(sum_split([parts2[0]] + moved2), sum_split([parts1[0]] + moved1))
    ]
    moved_slots = along(slots[1:])
    piece = sum_parts([slots[0]] + moved_slots)
    ffn_line = jnp.stack([piece3] + ffn_line)
    ffn_other = swap(ffn_line, "dp", 1)
    output, query_grad, content_grad = call(
        finish_rows_kernel,
        [((OWN, D), BF), ((OWN, D), BF), ((length // 2, D), BF)],
        (output_own, output_got, query_own, content_keep, rows_got),
    )
    line, ffn_other, content_grad = after((across([piece] * 3), ffn_other, content_grad))
    line = jnp.stack([piece] + line)
    other = swap(line, "dp", 1)
    ffn_in_grad, ffn_out_grad = call(
        finish_ffn_kernel,
        [((D, D), F32), ((D, D), F32)],
        (ffn_line, ffn_other),
        [pltpu.VMEM((2 * D, D), F32)],
    )

    (
        self_proj_grad, self_bias_grad, self_out_grad, cross_proj_grad, cross_bias_grad,
        cross_out_grad, ffn_bias_grad, out_bias_grad,
        gain_grad, shift_grad,
    ) = call(
        finish_kernel,
        [
            ((3, D, PAIR), F32), ((2, PAIR), F32), ((PAIR, D), F32), ((3, D, PAIR), F32),
            ((2, PAIR), F32), ((PAIR, D), F32), ((1, D), F32),
            ((3, D), F32), ((3, D), F32), ((3, D), F32),
        ],
        (line, other),
        [
            pltpu.VMEM((5 * D, PAIR), F32), pltpu.VMEM((3 * D + SUB * EXT, PAIR), F32),
        ],
    )
    return (
        output,
        query_grad,
        content_grad,
        encoder_grad,
        self_proj_grad,
        self_bias_grad,
        self_out_grad,
        cross_proj_grad,
        cross_bias_grad,
        cross_out_grad,
        ffn_in_grad,
        ffn_bias_grad.reshape(D),
        ffn_out_grad,
        out_bias_grad,
        gain_grad,
        shift_grad,
    )


def solution(mesh):
    return jax.shard_map(
        body,
        mesh=mesh,
        in_specs=(
            P("dp", None), P("dp", None), P("dp", None), P("dp", None), P("dp", None),
            P("dp", None), P("dp", None), P("dp", None), P(None, None, "mp"), P(None, "mp"),
            P("mp", None), P(None, None, "mp"), P(None, "mp"), P("mp", None), P(None, "mp"),
            P("mp"), P("mp", None), P(), P(), P(), P(("dp", "mp"), None),
        ),
        out_specs=(
            P(("dp", "mp"), None), P(("dp", "mp"), None), P(("dp", "mp"), None),
            P(("dp", "mp"), None), P(None, None, "mp"), P(None, "mp"), P("mp", None),
            P(None, None, "mp"), P(None, "mp"), P("mp", None), P(None, "mp"), P("mp"),
            P("mp", None), P(), P(), P(),
        ),
        check_vma=False,
    )
```

```python
import math

import jax
import jax.numpy as jnp
from jax import lax
from jax.experimental import pallas as pl
from jax.experimental.pallas import tpu as pltpu
from jax.sharding import PartitionSpec as P

HEAD = 64
EPSILON = 1e-05
MASKED = -1000000000.0
LOG2E = math.log2(math.e)
D = 512
PAIR = 128
PAIRS = 4
OWN = 512
TQ = 128
ROW_TILES = 8
TK = 256
TILES = OWN // TQ
SUB = 8
EXT = 16
BF = jnp.bfloat16
F32 = jnp.float32
VMEM_LIMIT = 56 * 1024 * 1024


def mm(left, right):
    return jnp.dot(left, right, preferred_element_type=F32)


def mm_rows(left, right):
    return lax.dot_general(left, right, (((0,), (0,)), ((), ())), preferred_element_type=F32)


def mm_cols(left, right):
    return lax.dot_general(left, right, (((1,), (1,)), ((), ())), preferred_element_type=F32)


def norm_parts(summed):
    average = jnp.mean(summed, axis=-1, keepdims=True)
    centred = summed - average
    inverse = lax.rsqrt(jnp.mean(centred * centred, axis=-1, keepdims=True) + EPSILON)
    return centred * inverse, inverse


def norm_backward(incoming, normed, inverse, gain):
    scaled = incoming * gain
    inner = (
        scaled
        - jnp.mean(scaled, axis=-1, keepdims=True)
        - normed * jnp.mean(scaled * normed, axis=-1, keepdims=True)
    )
    return inner * inverse


def col_sum(values):
    return jnp.sum(values.astype(F32), axis=0, keepdims=True)


def half_lanes(rows):
    return lax.broadcasted_iota(jnp.int32, (rows, PAIR), 1) < HEAD


def stack_heads(values):
    keep = half_lanes(values.shape[0])
    zero = jnp.zeros_like(values)
    return jnp.concatenate([jnp.where(keep, values, zero), jnp.where(keep, zero, values)], axis=0)


def pieces_of(value, first_lane, base):
    lane = lax.broadcasted_iota(jnp.int32, value.shape, 1)
    high = value.astype(BF)
    rest = value - high.astype(F32)
    middle = rest.astype(BF)
    low = (rest - middle.astype(F32)).astype(BF)
    out = jnp.where(lane == first_lane, high, base)
    out = jnp.where(lane == first_lane + 1, middle, out)
    return jnp.where(lane == first_lane + 2, low, out)


def lanes(pair):
    return slice(pair * PAIR, (pair + 1) * PAIR)


def key_range(scal, which, tile):
    base = pl.multiple_of(scal[2 + which * 2 * TILES + tile], PAIR)
    count = scal[2 + which * 2 * TILES + TILES + tile]
    return base, count


def over_keys(count, block):
    done = 0
    for wide in (4, 2, 1):
        whole = (count - done) // wide

        def step(index, carry, done=done, wide=wide):
            block((done + index * wide) * TK, wide * TK)
            return carry

        lax.fori_loop(0, whole, step, 0)
        done = done + whole * wide


def attend_forward(scal, which, q, k, v, kaug, hot, mask, score, peak, mixed, qaug, ctx, exact):
    def tile_body(tile, carry):
        base, count = key_range(scal, which, tile)
        rows = pl.ds(pl.multiple_of(tile * TQ, TQ), TQ)
        extra = hot[rows, :]
        extra2 = jnp.concatenate([extra, extra], axis=0)
        peak[...] = jnp.full(peak.shape, -jnp.inf, F32)
        mixed[...] = jnp.zeros(mixed.shape, F32)

        def scores(begin, size):
            off = pl.multiple_of(base + begin, PAIR)
            here = pl.ds(pl.multiple_of(begin, TK), size)
            ka = kaug[pl.ds(off, size), :]
            if mask is not None:
                block = mask[rows, pl.ds(off, size)]
                block = jnp.concatenate([block, block], axis=0)
            for pair in range(PAIRS):
                q2 = jnp.concatenate([stack_heads(q[rows, lanes(pair)]), extra2], axis=1)
                kk = jnp.concatenate([k[pl.ds(off, size), lanes(pair)], ka], axis=1)
                s = mm_cols(q2, kk)
                if mask is not None:
                    s = s + block
                score[pair, :, here] = s
                top = peak[pair]
                for part in range(size // PAIR):
                    top = jnp.maximum(top, s[:, part * PAIR : (part + 1) * PAIR])
                peak[pair] = top

        over_keys(count, scores)
        for pair in range(PAIRS):
            peak[pair] = jnp.broadcast_to(
                jnp.max(peak[pair], axis=1, keepdims=True), (2 * TQ, PAIR)
            )

        def weights(begin, size):
            off = pl.multiple_of(base + begin, PAIR)
            here = pl.ds(pl.multiple_of(begin, TK), size)
            minus = jnp.full((size, PAIR), -1.0, BF)
            for pair in range(PAIRS):
                top = jnp.concatenate([peak[pair]] * (size // PAIR), axis=1)
                p = jnp.exp2((score[pair, :, here] - top) * LOG2E).astype(BF)
                vv = jnp.concatenate([v[pl.ds(off, size), lanes(pair)], minus], axis=1)
                mixed[pair] += mm(p, vv)

        over_keys(count, weights)
        keep = half_lanes(TQ)
        for pair in range(PAIRS):
            both = mixed[pair]
            total = -both[:, PAIR:]
            normal = both[:, :PAIR] / total
            out = jnp.where(keep, normal[:TQ], normal[TQ:])
            exact[rows, lanes(pair)] = out
            ctx[rows, lanes(pair)] = out.astype(BF)
            logsum = peak[pair] + jnp.log(total)
            for head in range(2):
                part = logsum[head * TQ : (head + 1) * TQ]
                qaug[2 * pair + head, rows, :] = pieces_of(part, 4, extra)
        return carry

    lax.fori_loop(0, TILES, tile_body, 0)


def attend_backward(scal, which, q, k, v, kaug, qaug, mask_t, grad, exact, dq, dk, dv, dq_tile):
    def tile_body(tile, carry):
        base, count = key_range(scal, which, tile)
        start = pl.multiple_of(tile * TQ, TQ)
        rows = pl.ds(start, TQ)
        dq_tile[...] = jnp.zeros(dq_tile.shape, F32)
        keep = half_lanes(TQ)
        grads, queries, grad_aug, query_aug = [], [], [], []
        for pair in range(PAIRS):
            g = grad[rows, lanes(pair)]
            inner = g.astype(F32) * exact[rows, lanes(pair)]
            first = jnp.sum(jnp.where(keep, inner, 0.0), axis=1, keepdims=True)
            second = jnp.sum(jnp.where(keep, 0.0, inner), axis=1, keepdims=True)
            delta = jnp.broadcast_to(jnp.concatenate([first, second], axis=0), (2 * TQ, PAIR))
            aug = pieces_of(delta, 0, jnp.zeros((2 * TQ, PAIR), BF))
            g2 = stack_heads(g)
            q2 = stack_heads(q[rows, lanes(pair)])
            grads.append(g2)
            queries.append(q2)
            grad_aug.append(jnp.concatenate([g2, aug], axis=1))
            qa = jnp.concatenate([qaug[2 * pair, rows, :], qaug[2 * pair + 1, rows, :]], axis=0)
            query_aug.append(jnp.concatenate([q2, qa], axis=1))

        def keys(begin, size):
            off = pl.multiple_of(base + begin, PAIR)
            here = pl.ds(off, size)
            ka = kaug[here, :]
            minus = jnp.full((size, PAIR), -1.0, BF)
            if mask_t is not None:
                block = mask_t[here, rows]
                block = jnp.concatenate([block, block], axis=1)

            def raw(pair):
                kp = k[here, lanes(pair)]
                vp = jnp.concatenate([v[here, lanes(pair)], minus], axis=1)
                s = mm_cols(jnp.concatenate([kp, ka], axis=1), query_aug[pair])
                return kp, s, mm_cols(vp, grad_aug[pair])

            ready = raw(0)
            for pair in range(PAIRS):
                kp, s, dp = ready
                if pair + 1 < PAIRS:
                    ready = raw(pair + 1)
                if mask_t is not None:
                    s = s + block
                p = jnp.exp2(s * LOG2E)
                ds = (p * dp).astype(BF)
                dv[here, lanes(pair)] += mm(p.astype(BF), grads[pair])
                dk[here, lanes(pair)] += mm(ds, queries[pair])
                dq_tile[pair] += mm_rows(ds, kp)

        over_keys(count, keys)
        for pair in range(PAIRS):
            both = dq_tile[pair] * HEAD ** (-0.5)
            dq[rows, lanes(pair)] = jnp.where(keep, both[:TQ], both[TQ:]).astype(BF)
        return carry

    lax.fori_loop(0, TILES, tile_body, 0)


def mesh_place():
    group = lax.axis_index("dp")
    return group % 2, (group // 2) % 4, lax.axis_index("mp")


def run_copies(copies):
    for copy in copies:
        copy.start()
    for copy in copies:
        copy.wait()


def load_weights(proj, out, mine, other, weight, sem):
    core, place, _ = mesh_place()
    copies = []
    for matrix in range(3):
        copies.append(
            pltpu.make_async_copy(
                proj.at[matrix], weight.at[matrix, :, lanes(0)], sem.at[len(copies)]
            )
        )
    for side, source in ((core, mine), (1 - core, other)):
        for shift in range(4):
            spot = jnp.bitwise_xor(place, shift)
            matrix = 2 * side + spot // 2
            row = pl.multiple_of((spot % 2) * 256, 256)
            for pair in range(1, PAIRS):
                copies.append(
                    pltpu.make_async_copy(
                        source.at[shift, pair - 1, pl.ds(0, 256), :],
                        weight.at[matrix, pl.ds(row, 256), lanes(pair)],
                        sem.at[len(copies)],
                    )
                )
    weight[3, :, lanes(0)] = out[...].astype(F32).T.astype(BF)
    return copies


def put(source, target, sem):
    copy = pltpu.make_async_copy(source, target, sem)
    copy.start()
    return copy


def own_tiles(source, target, sem, first):
    _, _, position = mesh_place()
    copies = []
    for tile in range(TILES):
        row = pl.multiple_of((position // 2 * ROW_TILES + 2 * tile + position % 2) * TQ, TQ)
        copies.append(
            pltpu.make_async_copy(
                source.at[pl.ds(row, TQ), :], target.at[tile * TQ : (tile + 1) * TQ, :],
                sem.at[first + tile],
            )
        )
    return copies


def grad_copies(buffer, mine, theirs, sem):
    core, place, _ = mesh_place()
    chunk = buffer.shape[1] // SUB
    copies = []
    for side, target in ((core, mine), (1 - core, theirs)):
        for shift in range(4):
            row = pl.multiple_of((4 * side + jnp.bitwise_xor(place, shift)) * chunk, 16)
            copies.append(
                pltpu.make_async_copy(
                    buffer.at[:, pl.ds(row, chunk), :], target.at[shift], sem.at[len(copies)]
                )
            )
    return copies


def send_grads(buffer, mine, theirs, sem):
    run_copies(grad_copies(buffer, mine, theirs, sem))


def send_rows(buffer, keep, theirs, sem):
    part = lax.axis_index("mp") % 2
    rows = buffer.shape[0] // 2
    copies = []
    for side, target in ((part, keep), (1 - part, theirs)):
        row = pl.multiple_of(side * rows, 16)
        copies.append(
            pltpu.make_async_copy(buffer.at[pl.ds(row, rows), :], target, sem.at[len(copies)])
        )
    run_copies(copies)


def pack_kernel(
    self_proj, self_out, cross_proj, cross_out, ffn_in, ffn_out, self_bias, cross_bias, ffn_bias, cot,
    own, own3, cot_send, small,
):
    core, place, position = mesh_place()
    for index in range(2):
        row = pl.multiple_of((1 - position % 2 + 2 * index) * TQ, TQ)
        cot_send[index * TQ : (index + 1) * TQ, :] = cot[pl.ds(row, TQ), :]
    chunk = 4 * core + place
    matrix, half = chunk // 2, chunk % 2
    for proj, out, base in ((self_proj, self_out, 0), (cross_proj, cross_out, 256 + EXT)):

        @pl.when(matrix < 3)
        def _(proj=proj, base=base):
            own[base : base + 256, :] = proj[matrix, pl.ds(pl.multiple_of(half * 256, 256), 256), :]

        @pl.when(matrix == 3)
        def _(out=out, base=base):
            block = out[:, pl.ds(pl.multiple_of(half * 256, 256), 256)]
            own[base : base + 256, :] = block.astype(F32).T.astype(BF)

    rows = [self_bias[...].astype(F32), cross_bias[...].astype(F32)]
    rows += [ffn_bias[lanes(block)].astype(F32).reshape(1, PAIR) for block in range(4)]
    rows += [jnp.zeros((8, PAIR), F32)]
    small[...] = jnp.concatenate(rows, axis=0).astype(BF)
    own[256 : 256 + EXT, :] = small[...]
    rows = own3.shape[0]
    row = chunk * rows

    @pl.when(row < D)
    def _():
        own3[...] = ffn_in[pl.ds(pl.multiple_of(row, rows), rows), :]

    @pl.when(row >= D)
    def _():
        own3[...] = ffn_out[pl.ds(pl.multiple_of(row - D, rows), rows), :]


def prep_kernel(
    dec, enc, ranks, limits, padded, out_bias, gain, shift,
    scal, mask, mask_t, hot, kaug_dec, kaug_enc, vecs, table,
):
    _, _, position = mesh_place()
    row, part = position // 2, position % 2
    length, sources = dec.shape[1], enc.shape[1]
    seg = dec[pl.ds(row, 1), :]
    seg_enc = enc[pl.ds(row, 1), :]
    place = lax.broadcasted_iota(jnp.int32, (1, length), 1)
    begins = (place == 0) | (seg != pltpu.roll(seg, 1, 1))
    rank = jnp.where(padded[pl.ds(row, 1), :] == 0, ranks[pl.ds(row, 1), :], length)
    table[...] = jnp.zeros(table.shape, F32)
    table[0:1, :] = seg.astype(F32)
    table[1:2, :] = rank.astype(F32)
    table[2:3, :] = begins.astype(F32)
    table[3:4, :] = limits[pl.ds(row, 1), :].astype(F32)
    table[4:5, :] = place.astype(F32)
    own = jnp.concatenate(
        [
            table[:, pl.ds(pl.multiple_of((2 * tile + part) * TQ, TQ), TQ)]
            for tile in range(TILES)
        ],
        axis=1,
    )
    own_t = own.T
    every = table[...]
    every_t = every.T

    def visible(seg_q, limit_q, place_q, seg_k, rank_k, start_k, place_k):
        chosen = (rank_k < limit_q) & (place_q != place_k)
        return jnp.where((seg_q == seg_k) & ((start_k > 0.5) | chosen), 0.0, MASKED)

    mask[...] = visible(
        own_t[:, 0:1], own_t[:, 3:4], own_t[:, 4:5],
        every[0:1], every[1:2], every[2:3], every[4:5],
    )
    mask_t[...] = visible(
        own[0:1], own[3:4], own[4:5],
        every_t[:, 0:1], every_t[:, 1:2], every_t[:, 2:3], every_t[:, 4:5],
    )

    def key_aug(column):
        lane = lax.broadcasted_iota(jnp.int32, (column.shape[0], PAIR), 1)
        different = (lane < 4) & (column != lane.astype(F32))
        minus = (lane >= 4) & (lane < 7)
        return jnp.where(different, MASKED, jnp.where(minus, -1.0, 0.0)).astype(BF)

    kaug_dec[...] = key_aug(every_t[:, 0:1])
    seg_enc_f = jnp.broadcast_to(seg_enc.astype(F32), (8, sources))
    kaug_enc[...] = key_aug(seg_enc_f.T[:, 0:1])
    lane = lax.broadcasted_iota(jnp.int32, (OWN, PAIR), 1)
    hot[...] = (own_t[:, 0:1] == lane.astype(F32)).astype(F32).astype(BF)
    vecs[...] = jnp.zeros(vecs.shape, F32)
    for index, source in enumerate((out_bias, gain, shift)):
        vecs[3 * index : 3 * index + 3, :] = source[...].astype(F32)
    scal[0] = 0
    scal[1] = 0
    for which, keys in ((0, every[0:1]), (1, seg_enc_f[0:1])):
        size = keys.shape[1]
        for tile in range(TILES):
            block = own[0:1, tile * TQ : (tile + 1) * TQ]
            low, high = jnp.min(block), jnp.max(block)
            begin = jnp.sum((keys < low).astype(F32)).astype(jnp.int32)
            end = jnp.sum((keys <= high).astype(F32)).astype(jnp.int32)
            base = begin // PAIR * PAIR
            count = (end - base + TK - 1) // TK
            scal[2 + which * 2 * TILES + tile] = jnp.minimum(base, size - count * TK)
            scal[2 + which * 2 * TILES + TILES + tile] = count


def fetch(source, target, start, sem):
    return pltpu.make_async_copy(
        source.at[pl.ds(pl.multiple_of(start, target.shape[0]), target.shape[0]), :], target, sem
    )


def project(x, weight, bias, target):
    step = min(x.shape[0], 1024)
    for part in range(x.shape[0] // step):
        rows = slice(part * step, (part + 1) * step)
        value = mm(x[rows, :], weight)
        target[rows, :] = (value if bias is None else value + bias).astype(BF)


def self_forward_kernel(
    scal, query, content, mask_in, hot, kaug, vecs, small, proj, out, mine, other,
    q, k_out, v_out, qaug, ctx, exact, s1, weight_out, bias,
    score, peak, mixed, got, xq, xc, k, v, weight, mask, sem, sem_out,
):
    _, _, position = mesh_place()
    rows = xc.shape[0]
    copies = own_tiles(query, xq, sem, 32)
    copies.append(
        pltpu.make_async_copy(
            content.at[pl.ds(pl.multiple_of(position // 2 * rows, rows), rows), :], xc, sem.at[36]
        )
    )
    for pair in range(1, PAIRS):
        copies.append(
            pltpu.make_async_copy(
                mine.at[0, pair - 1, pl.ds(256, EXT), :], got.at[pair - 1], sem.at[36 + pair]
            )
        )
    late = pltpu.make_async_copy(mask_in, mask, sem.at[40])
    for copy in copies:
        copy.start()
    moves = load_weights(proj, out, mine, other, weight, sem)
    for copy in moves:
        copy.start()
    late.start()
    for copy in copies + moves:
        copy.wait()
    outs = [put(weight, weight_out, sem_out.at[0])]
    bias[:, lanes(0)] = small[...].astype(F32)
    for pair in range(1, PAIRS):
        bias[:, lanes(pair)] = got[pair - 1].astype(F32)
    q[...] = ((mm(xq[...], weight[0]) + bias[0:1, :]).astype(BF) * BF(HEAD ** (-0.5))).astype(BF)
    project(xc, weight[1], None, k)
    outs.append(put(k, k_out, sem_out.at[1]))
    project(xc, weight[2], bias[1:2, :], v)
    outs.append(put(v, v_out, sem_out.at[2]))
    late.wait()
    attend_forward(scal, 0, q, k, v, kaug, hot, mask, score, peak, mixed, qaug, ctx, exact)
    s1[...] = xq[...].astype(F32) + mm_cols(ctx[...], weight[3]) + vecs[0:1, :]
    for copy in outs:
        copy.wait()


def cross_forward_kernel(
    scal, s1, encoder, hot, kaug, vecs, bias, proj, out, mine, other,
    q, k_out, v_out, qaug, ctx, exact, s2, weight_out,
    score, peak, mixed, enc, k, v, weight, sem, sem_out,
):
    _, _, position = mesh_place()
    moves = load_weights(proj, out, mine, other, weight, sem)
    rows = enc.shape[0]
    late = pltpu.make_async_copy(
        encoder.at[pl.ds(pl.multiple_of(position // 2 * rows, rows), rows), :], enc, sem.at[32]
    )
    for copy in moves:
        copy.start()
    late.start()
    normed, _ = norm_parts(s1[...])
    first = normed * vecs[3:4, :] + vecs[6:7, :]
    for copy in moves:
        copy.wait()
    outs = [put(weight, weight_out, sem_out.at[0])]
    q[...] = (
        (mm(first.astype(BF), weight[0]) + bias[2:3, :]).astype(BF) * BF(HEAD ** (-0.5))
    ).astype(BF)
    late.wait()
    project(enc, weight[1], None, k)
    outs.append(put(k, k_out, sem_out.at[1]))
    project(enc, weight[2], bias[3:4, :], v)
    outs.append(put(v, v_out, sem_out.at[2]))
    attend_forward(scal, 1, q, k, v, kaug, hot, None, score, peak, mixed, qaug, ctx, exact)
    s2[...] = first + mm_cols(ctx[...], weight[3]) + vecs[1:2, :]
    for copy in outs:
        copy.wait()


def gelu_parts(v):
    c = math.sqrt(2.0 / math.pi)
    square = v * v
    t = jnp.tanh(c * (v + 0.044715 * square * v))
    value = 0.5 * v * (1.0 + t)
    slope = 0.5 * (1.0 + t) + 0.5 * v * (1.0 - t * t) * (c + (3.0 * 0.044715 * c) * square)
    return value, slope


def ffn_kernel(
    s2, cot_own, cot_got, bias, vecs, ffn_in, ffn_out, first_core, second_core,
    output, mine, theirs, back, sums, output_send,
    weight, hidden, slopes, low, grads, cot, sem, sem_cot,
):
    core, place, position = mesh_place()
    half = position % 2
    late = []
    for index in range(2):
        row = pl.multiple_of((half + 2 * index) * TQ, TQ)
        target = pl.multiple_of((2 * half + index) * TQ, TQ)
        late.append(
            put(cot_own.at[pl.ds(row, TQ), :], cot.at[pl.ds(target, TQ), :], sem_cot.at[index])
        )
    target = pl.multiple_of((1 - half) * 2 * TQ, 2 * TQ)
    late.append(put(cot_got, cot.at[pl.ds(target, 2 * TQ), :], sem_cot.at[2]))
    copies = [[] for _ in range(4)]
    for side, source in enumerate((ffn_in, ffn_out)):
        copies[0].append(put(source, weight.at[side, 0], sem.at[side]))
    for part in range(1, 4):
        for side, source in ((core, first_core), (1 - core, second_core)):
            for shift in range(4):
                row = pl.multiple_of(jnp.bitwise_xor(place, shift) * 128, 128)
                number = 2 + sum(len(group) for group in copies[1:])
                copies[part].append(
                    put(
                        source.at[shift, part - 1], weight.at[side, part, pl.ds(row, 128), :],
                        sem.at[number],
                    )
                )
    sums[...] = jnp.zeros(sums.shape, F32)
    normed2, inverse2 = norm_parts(s2[...])
    second = normed2 * vecs[4:5, :] + vecs[7:8, :]
    low[...] = second.astype(BF)
    total = second + vecs[2:3, :]
    def before_gelu(part):
        part_bias = jnp.concatenate([bias[4 + i : 5 + i, lanes(part)] for i in range(4)], axis=1)
        for copy in copies[part]:
            copy.wait()
        return mm(low[...], weight[0, part]) + part_bias

    ready = before_gelu(0)
    for part in range(4):
        block = slice(part * D, (part + 1) * D)
        pre = ready
        if part < 3:
            ready = before_gelu(part + 1)
        value, slope = gelu_parts(pre)
        hidden[:, block] = value.astype(BF)
        slopes[:, block] = slope
        total = total + mm(hidden[:, block], weight[1, part])
    normed3, inverse3 = norm_parts(total)
    output[...] = (normed3 * vecs[5:6, :] + vecs[8:9, :]).astype(BF)
    for copy in late:
        copy.wait()
    row = pl.multiple_of((1 - half) * 2 * TQ, 2 * TQ)
    output_send[...] = output[pl.ds(row, 2 * TQ), :]
    incoming = cot[...].astype(F32)
    sums[0:1, :] = col_sum(incoming * normed3)
    sums[1:2, :] = col_sum(incoming)
    third_grad = norm_backward(incoming, normed3, inverse3, vecs[5:6, :])
    branch = third_grad.astype(BF)
    sums[2:3, :] = col_sum(branch)
    total = third_grad
    ready = mm_cols(branch, weight[1, 0])
    for part in range(4):
        block = slice(part * D, (part + 1) * D)
        pre_grad = (slopes[:, block] * ready).astype(BF)
        if part < 3:
            ready = mm_cols(branch, weight[1, part + 1])
        sums[8 + part : 9 + part, :] = col_sum(pre_grad)
        grads[part, 0:D, :] = mm_rows(low[...], pre_grad).astype(BF)
        grads[part, D : 2 * D, :] = mm_rows(hidden[:, block], branch).astype(BF)
        if part == 3:
            moves = grad_copies(grads, mine, theirs, sem)
            for copy in moves:
                copy.start()
        total = total + mm_cols(pre_grad, weight[0, part])
    sums[3:4, :] = col_sum(total * normed2)
    sums[4:5, :] = col_sum(total)
    second_grad = norm_backward(total, normed2, inverse2, vecs[4:5, :])
    sums[5:6, :] = col_sum(second_grad.astype(BF))
    back[...] = second_grad
    for copy in moves:
        copy.wait()


def store_grad(grads, matrix, value):
    low = value.astype(BF)
    for pair in range(PAIRS):
        grads[pair, matrix * D : (matrix + 1) * D, :] = low[:, lanes(pair)]


def projection_grads(grads, x, low, matrix):
    store_grad(grads, matrix, mm_rows(x[...], low[...]))


def input_grads(dk, dv, weight, out):
    step = min(dk.shape[0], 1024)
    for part in range(dk.shape[0] // step):
        rows = slice(part * step, (part + 1) * step)
        out[rows, :] = (
            mm_cols(dk[rows, :], weight[1]) + mm_cols(dv[rows, :], weight[2])
        ).astype(BF)


def load_all(sources, targets, sem):
    copies = [
        pltpu.make_async_copy(source, target, sem.at[index])
        for index, (source, target) in enumerate(zip(sources, targets))
    ]
    for copy in copies:
        copy.start()
    return copies


def store_low(dk, dv, dk_low, dv_low, low, sem):
    copies = []
    for index, (value, target) in enumerate(((dk, dk_low), (dv, dv_low))):
        for part in range(value.shape[0] // 512):
            rows = slice(part * 512, (part + 1) * 512)
            low[index, rows, :] = value[rows, :].astype(BF)
            copies.append(put(low.at[index, rows, :], target.at[rows, :], sem.at[len(copies)]))
    return copies


def cross_attention_grad_kernel(
    scal, dss2, weight_in, q_in, k_in, v_in, qaug_in, exact_in, kaug_in,
    dq, dk_low, dv_low, keep, send,
    grad_ctx, weight, enc_grad, dk, dv, dq_tile, low, q, k, v, qaug, exact, kaug, sem,
):
    first = put(weight_in, weight, sem.at[7])
    copies = load_all(
        (q_in, qaug_in, exact_in, kaug_in, k_in, v_in), (q, qaug, exact, kaug, k, v), sem
    )
    dk[...] = jnp.zeros(dk.shape, F32)
    dv[...] = jnp.zeros(dv.shape, F32)
    first.wait()
    grad_ctx[...] = mm(dss2[...].astype(BF), weight[3]).astype(BF)
    for copy in copies:
        copy.wait()
    attend_backward(scal, 1, q, k, v, kaug, qaug, None, grad_ctx, exact, dq, dk, dv, dq_tile)
    copies = store_low(dk, dv, dk_low, dv_low, low, sem)
    input_grads(low.at[0], low.at[1], weight, enc_grad)
    for copy in copies:
        copy.wait()
    send_rows(enc_grad, keep, send, sem)


def cross_projection_grad_kernel(
    dss2, s1, weight_in, self_weight, ctx, self_ctx, dq, dk_in, dv_in, encoder, vecs, sums_in,
    mine, theirs, back, grad_ctx, sums,
    grads, enc, weight, dk, dv, sem,
):
    _, _, position = mesh_place()
    rows = enc.shape[0]
    start = pl.multiple_of(position // 2 * rows, rows)
    early = [
        put(weight_in.at[0], weight.at[0], sem.at[0]),
        put(self_weight.at[3], weight.at[1], sem.at[1]),
    ]
    late = [
        put(encoder.at[pl.ds(start, rows), :], enc, sem.at[2]),
        put(dk_in, dk, sem.at[3]),
        put(dv_in, dv, sem.at[4]),
    ]
    sums[...] = sums_in[...]
    normed, inverse = norm_parts(s1[...])
    first = (normed * vecs[3:4, :] + vecs[6:7, :]).astype(BF)
    store_grad(grads, 0, mm_rows(first, dq[...]))
    store_grad(grads, 3, mm_rows(dss2[...].astype(BF), ctx[...]))
    for copy in early:
        copy.wait()
    total = dss2[...] + mm_cols(dq[...], weight[0])
    sums[6:7, :] = col_sum(total * normed)
    sums[7:8, :] = col_sum(total)
    first_grad = norm_backward(total, normed, inverse, vecs[3:4, :])
    branch = first_grad.astype(BF)
    sums[12:13, :] = col_sum(branch)
    back[...] = first_grad
    grad_ctx[...] = mm(branch, weight[1]).astype(BF)
    store_grad(grads, 4, mm_rows(branch, self_ctx[...]))
    sums[14:15, :] = col_sum(dq[...])
    for copy in late:
        copy.wait()
    projection_grads(grads, enc, dk, 1)
    projection_grads(grads, enc, dv, 2)
    sums[15:16, :] = col_sum(dv[...])
    send_grads(grads, mine, theirs, sem)


def self_attention_grad_kernel(
    scal, grad_ctx, q_in, k_in, v_in, qaug_in, exact_in, mask_in, kaug_in, weight_in,
    dq, dk_low, dv_low, keep, send,
    dk, dv, dq_tile, low, q, k, v, qaug, exact, mask_t, kaug, sem, weight, content_grad,
):
    late = put(weight_in.at[1:3], weight.at[1:3], sem.at[7])
    copies = load_all(
        (q_in, qaug_in, exact_in, kaug_in, k_in, v_in, mask_in),
        (q, qaug, exact, kaug, k, v, mask_t),
        sem,
    )
    dk[...] = jnp.zeros(dk.shape, F32)
    dv[...] = jnp.zeros(dv.shape, F32)
    for copy in copies:
        copy.wait()
    attend_backward(scal, 0, q, k, v, kaug, qaug, mask_t, grad_ctx, exact, dq, dk, dv, dq_tile)
    late.wait()
    copies = store_low(dk, dv, dk_low, dv_low, low, sem)
    input_grads(low.at[0], low.at[1], weight, content_grad)
    half = lax.axis_index("mp") % 2
    mid = content_grad.shape[0] // 2
    keep[...] = content_grad[pl.ds(pl.multiple_of(half * mid, mid), mid), :]
    send[...] = content_grad[pl.ds(pl.multiple_of((1 - half) * mid, mid), mid), :]
    for copy in copies:
        copy.wait()


def self_projection_grad_kernel(
    fsg, weight_in, dq, dk, dv, query, content, sums,
    mine, theirs, send, query_grad,
    grads, xq, xc, weight, sem, sem_late,
):
    _, _, position = mesh_place()
    half = position % 2
    rows = xc.shape[0]
    copies = own_tiles(query, xq, sem, 0)
    for copy in copies:
        copy.start()
    place = pl.multiple_of(position // 2 * rows, rows)
    content_copy = put(content.at[pl.ds(place, rows), :], xc, sem_late.at[0])
    weight_copy = put(weight_in.at[0], weight, sem_late.at[1])
    for copy in copies:
        copy.wait()
    store_grad(grads, 0, mm_rows(xq[...], dq[...]))
    content_copy.wait()
    projection_grads(grads, xc, dk, 1)
    projection_grads(grads, xc, dv, 2)
    bias_q = col_sum(dq[...])
    bias_v = col_sum(dv[...])
    for pair in range(PAIRS):
        parts = [bias_q[:, lanes(pair)], bias_v[:, lanes(pair)]]
        parts += [sums[14:15, lanes(pair)], sums[15:16, lanes(pair)]]
        parts += [sums[8 + pair : 9 + pair, lanes(i)] for i in range(4)]
        for index in (0, 1, 2, 3, 4, 5, 6, 7, 12):
            parts += [sums[index : index + 1, lanes(i)] for i in range(4)]
        parts += [jnp.zeros((SUB * EXT - len(parts), PAIR), F32)]
        grads[pair, 3 * D : 3 * D + SUB * EXT, :] = jnp.concatenate(parts, axis=0).astype(BF)
    moves = grad_copies(grads, mine, theirs, sem)
    for copy in moves:
        copy.start()
    weight_copy.wait()
    query_grad[...] = (fsg[...] + mm_cols(dq[...], weight[...])).astype(BF)
    row = pl.multiple_of((1 - half) * 2 * TQ, 2 * TQ)
    send[...] = query_grad[pl.ds(row, 2 * TQ), :]
    for copy in moves:
        copy.wait()


def add_split_kernel(mine, theirs, *outs):
    for index, out in enumerate(outs):
        out[...] = (mine[index].astype(F32) + theirs[index].astype(F32)).astype(BF)


def sum_split_kernel(own, first, second, third, *outs):
    for index, out in enumerate(outs):
        out[...] = (
            (own[index].astype(F32) + first[index].astype(F32))
            + (second[index].astype(F32) + third[index].astype(F32))
        ).astype(BF)


def sum_merge_kernel(a0, a1, a2, a3, b0, b1, b2, b3, *outs):
    rows = a0.shape[1]
    for index, out in enumerate(outs):
        for group, spot in (((a0, a1, a2, a3), slice(0, rows)), ((b0, b1, b2, b3), slice(rows, None))):
            own, first, second, third = [part[index].astype(F32) for part in group]
            out[spot, :] = ((own + first) + (second + third)).astype(BF)


def sum_kernel(own, first, second, third, out):
    out[...] = (
        (own[...].astype(F32) + first[...].astype(F32))
        + (second[...].astype(F32) + third[...].astype(F32))
    ).astype(out.dtype)


def finish_ffn_kernel(line, other, ffn_in, ffn_out, wide):
    core, place, _ = mesh_place()
    for side, source in ((core, line), (1 - core, other)):
        for shift in range(4):
            row = pl.multiple_of((4 * side + jnp.bitwise_xor(place, shift)) * 128, 128)
            wide[pl.ds(row, 128), :] = source[shift].astype(F32)
    ffn_in[...] = wide[0:D, :]
    ffn_out[...] = wide[D:, :]


def finish_rows_kernel(
    output_own, output_got, query_own, query_got, keep, got, output, query, content
):
    _, _, position = mesh_place()
    half = position % 2
    for own, theirs, target in (
        (output_own, output_got, output), (query_own, query_got, query)
    ):
        for index in range(2):
            row = pl.multiple_of((2 * half + index) * TQ, TQ)
            place_own = pl.multiple_of((half + 2 * index) * TQ, TQ)
            place_got = pl.multiple_of((1 - half + 2 * index) * TQ, TQ)
            first = index * TQ
            target[pl.ds(place_own, TQ), :] = own[pl.ds(row, TQ), :]
            target[pl.ds(place_got, TQ), :] = theirs[first : first + TQ, :]
    content[...] = (keep[...].astype(F32) + got[...].astype(F32)).astype(BF)


def finish_kernel(
    line, other,
    self_proj, self_bias, self_out, cross_proj, cross_bias, cross_out, ffn_bias,
    out_bias, gain, moved, flat, flat_self,
):
    core, place, _ = mesh_place()
    cross_rows, self_rows = flat.shape[0] // SUB, flat_self.shape[0] // SUB
    for side, source in ((core, line), (1 - core, other)):
        for shift in range(4):
            spot = 4 * side + jnp.bitwise_xor(place, shift)
            row = pl.multiple_of(spot * cross_rows, 8)
            flat[pl.ds(row, cross_rows), :] = source[shift, 0:cross_rows, :].astype(F32)
            row = pl.multiple_of(spot * self_rows, 8)
            flat_self[pl.ds(row, self_rows), :] = source[shift, cross_rows:, :].astype(F32)
    for matrix in range(3):
        cross_proj[matrix] = flat[matrix * D : (matrix + 1) * D, :]
        self_proj[matrix] = flat_self[matrix * D : (matrix + 1) * D, :]
    cross_out[...] = flat[3 * D : 4 * D, :].T
    self_out[...] = flat[4 * D : 5 * D, :].T
    start = 3 * D
    self_bias[...] = flat_self[start : start + 2, :]
    cross_bias[...] = flat_self[start + 2 : start + 4, :]
    for block in range(4):
        ffn_bias[:, lanes(block)] = flat_self[start + 4 + block : start + 5 + block, :]
    for target, order in ((out_bias, (8, 5, 2)), (gain, (6, 3, 0)), (moved, (7, 4, 1))):
        for index, number in enumerate(order):
            for block in range(4):
                row = start + 8 + number * 4 + block
                target[index : index + 1, lanes(block)] = flat_self[row : row + 1, :]


def call(kernel, outs, inputs, scratch=(), smem_in=(), any_in=(), any_out=(), smem_out=(), long=False):
    def space(index, smem, hbm):
        return pltpu.SMEM if index in smem else pl.ANY if index in hbm else pltpu.VMEM

    return pl.pallas_call(
        kernel,
        out_shape=[jax.ShapeDtypeStruct(shape, dtype) for shape, dtype in outs],
        in_specs=[
            pl.BlockSpec(memory_space=space(index, smem_in, any_in)) for index in range(len(inputs))
        ],
        out_specs=[
            pl.BlockSpec(memory_space=space(index, smem_out, any_out)) for index in range(len(outs))
        ],
        scratch_shapes=list(scratch),
        compiler_params=pltpu.CompilerParams(vmem_limit_bytes=VMEM_LIMIT),
        cost_estimate=pl.CostEstimate(
            flops=10**13 if long else 10**6, bytes_accessed=1 << (30 if long else 14),
            transcendentals=0,
        ),
    )(*inputs)


def after(value, *others):
    flat, tree = jax.tree.flatten(value)
    tied = lax.optimization_barrier(tuple(flat) + tuple(others))
    return jax.tree.unflatten(tree, tied[: len(flat)])


def body(
    query_stream, content_stream, encoder, dec_segments, enc_segments, key_rank, observe_limit,
    padding, self_proj, self_bias, self_out, cross_proj, cross_bias, cross_out, ffn_in,
    ffn_in_bias, ffn_out, out_bias, norm_gain, norm_bias, cotangent,
):
    members = lax.axis_size("mp")
    groups = lax.axis_size("dp")
    length = dec_segments.shape[1]
    sources = enc_segments.shape[1]
    DMA = pltpu.SemaphoreType.DMA

    def swap(value, axis, mask):
        size = members if axis == "mp" else groups
        return lax.ppermute(value, axis, [(i, i ^ mask) for i in range(size)])

    def along(values):
        return [swap(value, "mp", shift + 1) for shift, value in enumerate(values)]

    def across(values):
        return [swap(value, "dp", 2 * shift + 2) for shift, value in enumerate(values)]

    own12, own3, cot_send, small = call(
        pack_kernel,
        [
            ((512 + EXT, PAIR), BF), ((2 * D // SUB, D), BF), ((2 * TQ, D), BF),
            ((EXT, PAIR), BF),
        ],
        (
            self_proj, self_out, cross_proj, cross_out, ffn_in, ffn_out, self_bias, cross_bias,
            ffn_in_bias, cotangent,
        ),
    )
    line12 = along([own12] * 3)
    scal, mask, mask_t, hot, kaug_dec, kaug_enc, vecs = call(
        prep_kernel,
        [
            ((2 + 4 * TILES,), jnp.int32), ((OWN, length), F32), ((length, OWN), F32),
            ((OWN, PAIR), BF), ((length, PAIR), BF), ((sources, PAIR), BF), ((EXT, D), F32),
        ],
        (
            dec_segments, enc_segments, key_rank, observe_limit, padding, out_bias, norm_gain,
            norm_bias,
        ),
        [pltpu.VMEM((8, length), F32)],
        smem_out=(0,),
    )
    line12, hot = after((line12, hot))
    line1 = jnp.stack([value[: 256 + EXT] for value in line12])
    line2 = jnp.stack([value[256 + EXT :] for value in line12])
    plane1, line3 = after((across([line1] * 3), along([after(own3, line1)] * 3)))
    plane1 = jnp.stack([line1] + plane1)
    line3 = jnp.stack(line3)
    other1 = swap(plane1, "dp", 1)
    cot_got = swap(after(cot_send, line1), "mp", 1)
    plane2 = across([after(line2, plane1)] * 3)

    def attention_outs(keys):
        return [
            ((OWN, D), BF), ((keys, D), BF), ((keys, D), BF), ((2 * PAIRS, OWN, PAIR), BF),
            ((OWN, D), BF), ((OWN, D), F32), ((OWN, D), F32), ((4, D, D), BF),
        ]

    def attention_scratch(keys):
        return [
            pltpu.VMEM((PAIRS, 2 * TQ, keys), F32), pltpu.VMEM((PAIRS, 2 * TQ, PAIR), F32),
            pltpu.VMEM((PAIRS, 2 * TQ, 2 * PAIR), F32),
        ]

    def backward_scratch(keys, masked=False):
        shapes = [
            pltpu.VMEM((keys, D), F32), pltpu.VMEM((keys, D), F32),
            pltpu.VMEM((PAIRS, 2 * TQ, PAIR), F32), pltpu.VMEM((2, keys, D), BF),
            pltpu.VMEM((OWN, D), BF), pltpu.VMEM((keys, D), BF), pltpu.VMEM((keys, D), BF),
            pltpu.VMEM((2 * PAIRS, OWN, PAIR), BF), pltpu.VMEM((OWN, D), F32),
        ]
        if masked:
            shapes.append(pltpu.VMEM((keys, OWN), F32))
        return shapes + [pltpu.VMEM((keys, PAIR), BF), DMA((8,))]

    q1, k1, v1, qaug1, ctx1, exact1, s1, weight1, bias = call(
        self_forward_kernel,
        attention_outs(length) + [((EXT, D), F32)],
        (
            scal, query_stream, content_stream, mask, hot, kaug_dec, vecs, small, self_proj,
            self_out, plane1, other1,
        ),
        attention_scratch(length)
        + [
            pltpu.VMEM((PAIRS - 1, EXT, PAIR), BF), pltpu.VMEM((OWN, D), BF),
            pltpu.VMEM((length, D), BF), pltpu.VMEM((length, D), BF), pltpu.VMEM((length, D), BF),
            pltpu.VMEM((4, D, D), BF), pltpu.VMEM((OWN, length), F32), DMA((41,)), DMA((3,)),
        ],
        smem_in=(0,), any_in=(1, 2, 3, 8, 10, 11), any_out=(1, 2, 7),
    )
    plane2, s1, cot_got = after((plane2, s1, cot_got))
    plane2 = jnp.stack([line2] + plane2)
    plane3 = across([after(line3, plane2)] * 3)
    other2 = swap(plane2, "dp", 1)
    q2, k2, v2, qaug2, ctx2, exact2, s2, weight2 = call(
        cross_forward_kernel,
        attention_outs(sources),
        (
            scal, s1, encoder, hot, kaug_enc, vecs, bias, cross_proj, cross_out, plane2, other2,
        ),
        attention_scratch(sources)
        + [
            pltpu.VMEM((sources, D), BF), pltpu.VMEM((sources, D), BF), pltpu.VMEM((sources, D), BF),
            pltpu.VMEM((4, D, D), BF), DMA((33,)), DMA((3,)),
        ],
        smem_in=(0,), any_in=(2, 7, 9, 10), any_out=(1, 2, 7),
    )
    plane3, s2 = after((plane3, s2))
    plane3 = jnp.stack([line3] + plane3)
    other3 = swap(plane3, "dp", 1)

    def group_outs(rows, width):
        return [((4, 4, rows // SUB, width), BF)] * 2

    output_own, mine3, theirs3, dss2, sums, output_send = call(
        ffn_kernel,
        [((OWN, D), BF)]
        + group_outs(2 * D, D)
        + [((OWN, D), F32), ((EXT, D), F32), ((2 * TQ, D), BF)],
        (s2, cotangent, cot_got, bias, vecs, ffn_in, ffn_out, plane3, other3),
        [
            pltpu.VMEM((2, 4, D, D), BF), pltpu.VMEM((OWN, 4 * D), BF),
            pltpu.VMEM((OWN, 4 * D), F32), pltpu.VMEM((OWN, D), BF), pltpu.VMEM((4, 2 * D, D), BF),
            pltpu.VMEM((OWN, D), BF), DMA((26,)), DMA((3,)),
        ],
        any_in=(1, 2, 5, 6, 7, 8), any_out=(1, 2),
    )

    def low_sum(*values):
        total = values[0].astype(F32)
        for value in values[1:]:
            total = total + value.astype(F32)
        return total.astype(BF)

    def add_split(mine, theirs):
        return [low_sum(mine[index], theirs[index]) for index in range(4)]

    def sum_split(parts):
        return [low_sum(*[part[index] for part in parts]) for index in range(4)]

    def sum_parts(parts):
        piece = parts[0].astype(F32)
        for part in parts[1:]:
            piece = piece + part.astype(F32)
        bit = SUB
        while bit < groups:
            piece = piece + swap(piece, "dp", bit)
            bit *= 2
        return piece.astype(BF)

    theirs3 = swap(theirs3, "dp", 1)
    dq2, dk2, dv2, enc_keep, enc_send = call(
        cross_attention_grad_kernel,
        [((OWN, D), BF), ((sources, D), BF), ((sources, D), BF)] + [((sources // 2, D), BF)] * 2,
        (scal, dss2, weight2, q2, k2, v2, qaug2, exact2, kaug_enc),
        [pltpu.VMEM((OWN, D), BF), pltpu.VMEM((4, D, D), BF), pltpu.VMEM((sources, D), BF)]
        + backward_scratch(sources),
        smem_in=(0,), any_in=(2, 3, 4, 5, 6, 7, 8), any_out=(1, 2, 3, 4), long=True,
    )
    output_got = swap(output_send, "mp", 1)
    theirs3, dq2, output_got = after((theirs3, dq2, output_got))
    parts3 = add_split(mine3, theirs3)
    dq2 = after(dq2, parts3[0])
    moved3 = across(parts3[1:])
    enc_theirs = swap(enc_send, "mp", 1)
    mine2, theirs2, fsg, grad_ctx1, sums = call(
        cross_projection_grad_kernel,
        group_outs(5 * D, PAIR) + [((OWN, D), F32), ((OWN, D), BF), ((EXT, D), F32)],
        (dss2, s1, weight2, weight1, ctx2, ctx1, dq2, dk2, dv2, encoder, vecs, sums),
        [
            pltpu.VMEM((PAIRS, 5 * D, PAIR), BF), pltpu.VMEM((sources, D), BF),
            pltpu.VMEM((2, D, D), BF), pltpu.VMEM((sources, D), BF), pltpu.VMEM((sources, D), BF),
            DMA((8,)),
        ],
        any_in=(2, 3, 7, 8, 9), any_out=(0, 1), long=True,
    )
    theirs2 = swap(theirs2, "dp", 1)
    dq1, dk1, dv1, content_keep, content_send = call(
        self_attention_grad_kernel,
        [((OWN, D), BF), ((length, D), BF), ((length, D), BF)] + [((length // 2, D), BF)] * 2,
        (scal, grad_ctx1, q1, k1, v1, qaug1, exact1, mask_t, kaug_dec, weight1),
        backward_scratch(length, True)
        + [pltpu.VMEM((4, D, D), BF), pltpu.VMEM((length, D), BF)],
        smem_in=(0,), any_in=(2, 3, 4, 5, 6, 7, 8, 9), any_out=(1, 2), long=True,
    )
    content_got = swap(content_send, "mp", 1)
    moved3, theirs2, enc_theirs, dq1 = after((moved3, theirs2, enc_theirs, dq1))
    slots3 = sum_split([parts3[0]] + moved3)
    parts2 = add_split(mine2, theirs2)
    dq1 = after(dq1, slots3[0], parts2[0])
    moved_slots3 = along(slots3[1:])
    moved2 = across(parts2[1:])
    mine1, theirs1, rows_send, query_own = call(
        self_projection_grad_kernel,
        group_outs(3 * D + SUB * EXT, PAIR)
        + [((2 * TQ, D), BF), ((OWN, D), BF)],
        (fsg, weight1, dq1, dk1, dv1, query_stream, content_stream, sums),
        [
            pltpu.VMEM((PAIRS, 3 * D + SUB * EXT, PAIR), BF),
            pltpu.VMEM((OWN, D), BF), pltpu.VMEM((length, D), BF), pltpu.VMEM((D, D), BF),
            DMA((8,)), DMA((2,)),
        ],
        any_in=(1, 5, 6), any_out=(0, 1), long=True,
    )
    theirs1, moved_slots3, moved2 = after((theirs1, moved_slots3, moved2))
    theirs1 = swap(theirs1, "dp", 1)
    rows_got = swap(rows_send, "mp", 1)
    parts1 = add_split(mine1, theirs1)
    moved1 = across(parts1[1:])
    piece3 = sum_parts([slots3[0]] + moved_slots3)
    encoder_grad = (enc_keep.astype(F32) + enc_theirs.astype(F32)).astype(BF)
    moved1, content_got = after((moved1, content_got))
    slots = [
        jnp.concatenate(both, axis=0)
        for both in zip(sum_split([parts2[0]] + moved2), sum_split([parts1[0]] + moved1))
    ]
    moved_slots = along(slots[1:])
    ffn_line = across([after(piece3, slots[0])] * 3)
    moved_slots, ffn_line, encoder_grad, rows_got = after(
        (moved_slots, ffn_line, encoder_grad, rows_got)
    )
    piece = sum_parts([slots[0]] + moved_slots)
    ffn_line = jnp.stack([piece3] + ffn_line)
    ffn_other = swap(ffn_line, "dp", 1)
    output, query_grad, content_grad = call(
        finish_rows_kernel,
        [((OWN, D), BF), ((OWN, D), BF), ((length // 2, D), BF)],
        (output_own, output_got, query_own, rows_got, content_keep, content_got),
    )
    line, ffn_other, content_grad = after((across([piece] * 3), ffn_other, content_grad))
    line = jnp.stack([piece] + line)
    other = swap(line, "dp", 1)
    ffn_in_grad, ffn_out_grad = call(
        finish_ffn_kernel,
        [((D, D), F32), ((D, D), F32)],
        (ffn_line, ffn_other),
        [pltpu.VMEM((2 * D, D), F32)],
    )

    (
        self_proj_grad, self_bias_grad, self_out_grad, cross_proj_grad, cross_bias_grad,
        cross_out_grad, ffn_bias_grad, out_bias_grad,
        gain_grad, shift_grad,
    ) = call(
        finish_kernel,
        [
            ((3, D, PAIR), F32), ((2, PAIR), F32), ((PAIR, D), F32), ((3, D, PAIR), F32),
            ((2, PAIR), F32), ((PAIR, D), F32), ((1, D), F32),
            ((3, D), F32), ((3, D), F32), ((3, D), F32),
        ],
        (line, other),
        [
            pltpu.VMEM((5 * D, PAIR), F32), pltpu.VMEM((3 * D + SUB * EXT, PAIR), F32),
        ],
    )
    return (
        output,
        query_grad,
        content_grad,
        encoder_grad,
        self_proj_grad,
        self_bias_grad,
        self_out_grad,
        cross_proj_grad,
        cross_bias_grad,
        cross_out_grad,
        ffn_in_grad,
        ffn_bias_grad.reshape(D),
        ffn_out_grad,
        out_bias_grad,
        gain_grad,
        shift_grad,
    )


def solution(mesh):
    return jax.shard_map(
        body,
        mesh=mesh,
        in_specs=(
            P("dp", None), P("dp", None), P("dp", None), P("dp", None), P("dp", None),
            P("dp", None), P("dp", None), P("dp", None), P(None, None, "mp"), P(None, "mp"),
            P("mp", None), P(None, None, "mp"), P(None, "mp"), P("mp", None), P(None, "mp"),
            P("mp"), P("mp", None), P(), P(), P(), P(("dp", "mp"), None),
        ),
        out_specs=(
            P(("dp", "mp"), None), P(("dp", "mp"), None), P(("dp", "mp"), None),
            P(("dp", "mp"), None), P(None, None, "mp"), P(None, "mp"), P("mp", None),
            P(None, None, "mp"), P(None, "mp"), P("mp", None), P(None, "mp"), P("mp"),
            P("mp", None), P(), P(), P(),
        ),
        check_vma=False,
    )
```

```python
import math

import jax
import jax.numpy as jnp
from jax import lax
from jax.experimental import pallas as pl
from jax.experimental.pallas import tpu as pltpu
from jax.sharding import PartitionSpec as P

HEAD = 64
EPSILON = 1e-05
MASKED = -1000000000.0
LOG2E = math.log2(math.e)
D = 512
PAIR = 128
ROWS = 16
PAIRS = 4
OWN = 512
TQ = 128
ROW_TILES = 8
TK = 256
TILES = OWN // TQ
SUB = 8
EXT = 16
BF = jnp.bfloat16
F32 = jnp.float32
VMEM_LIMIT = 56 * 1024 * 1024


def mm(left, right):
    return jnp.dot(left, right, preferred_element_type=F32)


def mm_rows(left, right):
    return lax.dot_general(left, right, (((0,), (0,)), ((), ())), preferred_element_type=F32)


def mm_cols(left, right):
    return lax.dot_general(left, right, (((1,), (1,)), ((), ())), preferred_element_type=F32)


def norm_parts(summed):
    average = jnp.mean(summed, axis=-1, keepdims=True)
    centred = summed - average
    inverse = lax.rsqrt(jnp.mean(centred * centred, axis=-1, keepdims=True) + EPSILON)
    return centred * inverse, inverse


def norm_backward(incoming, normed, inverse, gain):
    scaled = incoming * gain
    inner = (
        scaled
        - jnp.mean(scaled, axis=-1, keepdims=True)
        - normed * jnp.mean(scaled * normed, axis=-1, keepdims=True)
    )
    return inner * inverse


def col_sum(values):
    return jnp.sum(values.astype(F32), axis=0, keepdims=True)


def half_lanes(rows):
    return lax.broadcasted_iota(jnp.int32, (rows, PAIR), 1) < HEAD


def stack_heads(values):
    keep = half_lanes(values.shape[0])
    zero = jnp.zeros_like(values)
    return jnp.concatenate([jnp.where(keep, values, zero), jnp.where(keep, zero, values)], axis=0)


def pieces_of(value, first_lane, base):
    lane = lax.broadcasted_iota(jnp.int32, value.shape, 1)
    high = value.astype(BF)
    rest = value - high.astype(F32)
    middle = rest.astype(BF)
    low = (rest - middle.astype(F32)).astype(BF)
    out = jnp.where(lane == first_lane, high, base)
    out = jnp.where(lane == first_lane + 1, middle, out)
    return jnp.where(lane == first_lane + 2, low, out)


def lanes(pair):
    return slice(pair * PAIR, (pair + 1) * PAIR)


def key_range(scal, which, tile, align):
    base = pl.multiple_of(scal[which * 2 * TILES + tile], align)
    count = scal[which * 2 * TILES + TILES + tile]
    return base, count


def over_keys(count, block):
    done = 0
    for wide in (4, 3, 2, 1):
        whole = (count - done) // wide

        def step(index, carry, done=done, wide=wide):
            block((done + index * wide) * TK, wide * TK)
            return carry

        lax.fori_loop(0, whole, step, 0)
        done = done + whole * wide


def attend_forward(scal, which, q, k, v, kaug, hot, mask, score, peak, mixed, qaug, ctx, exact):
    align = ROWS if mask is None else PAIR

    def tile_body(tile, carry):
        base, count = key_range(scal, which, tile, align)
        rows = pl.ds(pl.multiple_of(tile * TQ, TQ), TQ)
        extra = hot[rows, :]
        extra2 = jnp.concatenate([extra, extra], axis=0)
        peak[...] = jnp.full(peak.shape, -jnp.inf, F32)
        mixed[...] = jnp.zeros(mixed.shape, F32)

        def scores(begin, size):
            off = pl.multiple_of(base + begin, align)
            here = pl.ds(pl.multiple_of(begin, TK), size)
            ka = kaug[pl.ds(off, size), :]
            if mask is not None:
                block = mask[rows, pl.ds(off, size)]
                block = jnp.concatenate([block, block], axis=0)
            for pair in range(PAIRS):
                q2 = jnp.concatenate([stack_heads(q[rows, lanes(pair)]), extra2], axis=1)
                kk = jnp.concatenate([k[pl.ds(off, size), lanes(pair)], ka], axis=1)
                s = mm_cols(q2, kk)
                if mask is not None:
                    s = s + block
                score[pair, :, here] = s
                top = peak[pair]
                for part in range(size // PAIR):
                    top = jnp.maximum(top, s[:, part * PAIR : (part + 1) * PAIR])
                peak[pair] = top

        over_keys(count, scores)
        for pair in range(PAIRS):
            peak[pair] = jnp.broadcast_to(
                jnp.max(peak[pair], axis=1, keepdims=True), (2 * TQ, PAIR)
            )

        def weights(begin, size):
            off = pl.multiple_of(base + begin, align)
            here = pl.ds(pl.multiple_of(begin, TK), size)
            minus = jnp.full((size, PAIR), -1.0, BF)
            for pair in range(PAIRS):
                top = jnp.concatenate([peak[pair]] * (size // PAIR), axis=1)
                p = jnp.exp2((score[pair, :, here] - top) * LOG2E).astype(BF)
                vv = jnp.concatenate([v[pl.ds(off, size), lanes(pair)], minus], axis=1)
                mixed[pair] += mm(p, vv)

        over_keys(count, weights)
        keep = half_lanes(TQ)
        for pair in range(PAIRS):
            both = mixed[pair]
            total = -both[:, PAIR:]
            normal = both[:, :PAIR] / total
            out = jnp.where(keep, normal[:TQ], normal[TQ:])
            exact[rows, lanes(pair)] = out
            ctx[rows, lanes(pair)] = out.astype(BF)
            logsum = peak[pair] + jnp.log(total)
            for head in range(2):
                part = logsum[head * TQ : (head + 1) * TQ]
                qaug[2 * pair + head, rows, :] = pieces_of(part, 4, extra)
        return carry

    lax.fori_loop(0, TILES, tile_body, 0)


def attend_backward(scal, which, q, k, v, kaug, qaug, mask_t, grad, exact, dq, dk, dv, dq_tile):
    def tile_body(tile, carry):
        base, count = key_range(scal, which, tile, ROWS)
        start = pl.multiple_of(tile * TQ, TQ)
        rows = pl.ds(start, TQ)
        dq_tile[...] = jnp.zeros(dq_tile.shape, F32)
        keep = half_lanes(TQ)
        grads, queries, grad_aug, query_aug = [], [], [], []
        for pair in range(PAIRS):
            g = grad[rows, lanes(pair)]
            inner = g.astype(F32) * exact[rows, lanes(pair)]
            first = jnp.sum(jnp.where(keep, inner, 0.0), axis=1, keepdims=True)
            second = jnp.sum(jnp.where(keep, 0.0, inner), axis=1, keepdims=True)
            delta = jnp.broadcast_to(jnp.concatenate([first, second], axis=0), (2 * TQ, PAIR))
            aug = pieces_of(delta, 0, jnp.zeros((2 * TQ, PAIR), BF))
            g2 = stack_heads(g)
            q2 = stack_heads(q[rows, lanes(pair)])
            grads.append(g2)
            queries.append(q2)
            grad_aug.append(jnp.concatenate([g2, aug], axis=1))
            qa = jnp.concatenate([qaug[2 * pair, rows, :], qaug[2 * pair + 1, rows, :]], axis=0)
            query_aug.append(jnp.concatenate([q2, qa], axis=1))

        def keys(begin, size):
            off = pl.multiple_of(base + begin, ROWS)
            here = pl.ds(off, size)
            ka = kaug[here, :]
            minus = jnp.full((size, PAIR), -1.0, BF)
            if mask_t is not None:
                block = mask_t[here, rows]
                block = jnp.concatenate([block, block], axis=1)

            def raw(pair):
                kp = k[here, lanes(pair)]
                vp = jnp.concatenate([v[here, lanes(pair)], minus], axis=1)
                s = mm_cols(jnp.concatenate([kp, ka], axis=1), query_aug[pair])
                return kp, s, mm_cols(vp, grad_aug[pair])

            ready = raw(0)
            for pair in range(PAIRS):
                kp, s, dp = ready
                if pair + 1 < PAIRS:
                    ready = raw(pair + 1)
                if mask_t is not None:
                    s = s + block
                p = jnp.exp2(s * LOG2E)
                ds = (p * dp).astype(BF)
                dv[here, lanes(pair)] += mm(p.astype(BF), grads[pair])
                dk[here, lanes(pair)] += mm(ds, queries[pair])
                dq_tile[pair] += mm_rows(ds, kp)

        over_keys(count, keys)
        for pair in range(PAIRS):
            both = dq_tile[pair] * HEAD ** (-0.5)
            dq[rows, lanes(pair)] = jnp.where(keep, both[:TQ], both[TQ:]).astype(BF)
        return carry

    lax.fori_loop(0, TILES, tile_body, 0)


def mesh_place():
    group = lax.axis_index("dp")
    return group % 2, (group // 2) % 4, lax.axis_index("mp")


def run_copies(copies):
    for copy in copies:
        copy.start()
    for copy in copies:
        copy.wait()


def load_weights(proj, out, mine, other, weight, sem):
    core, place, _ = mesh_place()
    copies = []
    for matrix in range(3):
        copies.append(
            pltpu.make_async_copy(
                proj.at[matrix], weight.at[matrix, :, lanes(0)], sem.at[len(copies)]
            )
        )
    for side, source in ((core, mine), (1 - core, other)):
        for shift in range(4):
            spot = jnp.bitwise_xor(place, shift)
            matrix = 2 * side + spot // 2
            row = pl.multiple_of((spot % 2) * 256, 256)
            for pair in range(1, PAIRS):
                copies.append(
                    pltpu.make_async_copy(
                        source.at[shift, pair - 1, pl.ds(0, 256), :],
                        weight.at[matrix, pl.ds(row, 256), lanes(pair)],
                        sem.at[len(copies)],
                    )
                )
    weight[3, :, lanes(0)] = out[...].astype(F32).T.astype(BF)
    return copies


def put(source, target, sem):
    copy = pltpu.make_async_copy(source, target, sem)
    copy.start()
    return copy


def own_tiles(source, target, sem, first):
    _, _, position = mesh_place()
    copies = []
    for tile in range(TILES):
        row = pl.multiple_of((position // 2 * ROW_TILES + 2 * tile + position % 2) * TQ, TQ)
        copies.append(
            pltpu.make_async_copy(
                source.at[pl.ds(row, TQ), :], target.at[tile * TQ : (tile + 1) * TQ, :],
                sem.at[first + tile],
            )
        )
    return copies


def grad_copies(buffer, mine, theirs, sem):
    core, place, _ = mesh_place()
    chunk = buffer.shape[1] // SUB
    copies = []
    for side, target in ((core, mine), (1 - core, theirs)):
        for shift in range(4):
            row = pl.multiple_of((4 * side + jnp.bitwise_xor(place, shift)) * chunk, 16)
            copies.append(
                pltpu.make_async_copy(
                    buffer.at[:, pl.ds(row, chunk), :], target.at[shift], sem.at[len(copies)]
                )
            )
    return copies


def send_grads(buffer, mine, theirs, sem):
    run_copies(grad_copies(buffer, mine, theirs, sem))


def send_rows(buffer, keep, theirs, sem):
    part = lax.axis_index("mp") % 2
    rows = buffer.shape[0] // 2
    copies = []
    for side, target in ((part, keep), (1 - part, theirs)):
        row = pl.multiple_of(side * rows, 16)
        copies.append(
            pltpu.make_async_copy(buffer.at[pl.ds(row, rows), :], target, sem.at[len(copies)])
        )
    run_copies(copies)


def pack_kernel(
    self_proj, self_out, cross_proj, cross_out, ffn_in, ffn_out, self_bias, cross_bias, ffn_bias, cot,
    own, own3, cot_send, small,
):
    core, place, position = mesh_place()
    for index in range(2):
        row = pl.multiple_of((1 - position % 2 + 2 * index) * TQ, TQ)
        cot_send[index * TQ : (index + 1) * TQ, :] = cot[pl.ds(row, TQ), :]
    chunk = 4 * core + place
    matrix, half = chunk // 2, chunk % 2
    for proj, out, base in ((self_proj, self_out, 0), (cross_proj, cross_out, 256 + EXT)):

        @pl.when(matrix < 3)
        def _(proj=proj, base=base):
            own[base : base + 256, :] = proj[matrix, pl.ds(pl.multiple_of(half * 256, 256), 256), :]

        @pl.when(matrix == 3)
        def _(out=out, base=base):
            block = out[:, pl.ds(pl.multiple_of(half * 256, 256), 256)]
            own[base : base + 256, :] = block.astype(F32).T.astype(BF)

    rows = [self_bias[...].astype(F32), cross_bias[...].astype(F32)]
    rows += [ffn_bias[lanes(block)].astype(F32).reshape(1, PAIR) for block in range(4)]
    rows += [jnp.zeros((8, PAIR), F32)]
    small[...] = jnp.concatenate(rows, axis=0).astype(BF)
    own[256 : 256 + EXT, :] = small[...]
    rows = own3.shape[0]
    row = chunk * rows

    @pl.when(row < D)
    def _():
        own3[...] = ffn_in[pl.ds(pl.multiple_of(row, rows), rows), :]

    @pl.when(row >= D)
    def _():
        own3[...] = ffn_out[pl.ds(pl.multiple_of(row - D, rows), rows), :]


def prep_kernel(
    dec, enc, ranks, limits, padded, out_bias, gain, shift,
    scal, mask, mask_t, hot, kaug_dec, kaug_enc, vecs, table,
):
    _, _, position = mesh_place()
    row, part = position // 2, position % 2
    length, sources = dec.shape[1], enc.shape[1]
    seg = dec[pl.ds(row, 1), :]
    seg_enc = enc[pl.ds(row, 1), :]
    place = lax.broadcasted_iota(jnp.int32, (1, length), 1)
    begins = (place == 0) | (seg != pltpu.roll(seg, 1, 1))
    rank = jnp.where(padded[pl.ds(row, 1), :] == 0, ranks[pl.ds(row, 1), :], length)
    table[...] = jnp.zeros(table.shape, F32)
    table[0:1, :] = seg.astype(F32)
    table[1:2, :] = rank.astype(F32)
    table[2:3, :] = begins.astype(F32)
    table[3:4, :] = limits[pl.ds(row, 1), :].astype(F32)
    table[4:5, :] = place.astype(F32)
    own = jnp.concatenate(
        [
            table[:, pl.ds(pl.multiple_of((2 * tile + part) * TQ, TQ), TQ)]
            for tile in range(TILES)
        ],
        axis=1,
    )
    own_t = own.T
    every = table[...]
    every_t = every.T

    def visible(seg_q, limit_q, place_q, seg_k, rank_k, start_k, place_k):
        chosen = (rank_k < limit_q) & (place_q != place_k)
        return jnp.where((seg_q == seg_k) & ((start_k > 0.5) | chosen), 0.0, MASKED)

    mask[...] = visible(
        own_t[:, 0:1], own_t[:, 3:4], own_t[:, 4:5],
        every[0:1], every[1:2], every[2:3], every[4:5],
    )
    mask_t[...] = visible(
        own[0:1], own[3:4], own[4:5],
        every_t[:, 0:1], every_t[:, 1:2], every_t[:, 2:3], every_t[:, 4:5],
    )

    def key_aug(column):
        lane = lax.broadcasted_iota(jnp.int32, (column.shape[0], PAIR), 1)
        different = (lane < 4) & (column != lane.astype(F32))
        minus = (lane >= 4) & (lane < 7)
        return jnp.where(different, MASKED, jnp.where(minus, -1.0, 0.0)).astype(BF)

    kaug_dec[...] = key_aug(every_t[:, 0:1])
    seg_enc_f = jnp.broadcast_to(seg_enc.astype(F32), (8, sources))
    kaug_enc[...] = key_aug(seg_enc_f.T[:, 0:1])
    lane = lax.broadcasted_iota(jnp.int32, (OWN, PAIR), 1)
    hot[...] = (own_t[:, 0:1] == lane.astype(F32)).astype(F32).astype(BF)
    vecs[...] = jnp.zeros(vecs.shape, F32)
    for index, source in enumerate((out_bias, gain, shift)):
        vecs[3 * index : 3 * index + 3, :] = source[...].astype(F32)
    for which, keys, align in (
        (0, every[0:1], PAIR), (1, seg_enc_f[0:1], ROWS), (2, every[0:1], ROWS)
    ):
        size = keys.shape[1]
        for tile in range(TILES):
            block = own[0:1, tile * TQ : (tile + 1) * TQ]
            low, high = jnp.min(block), jnp.max(block)
            begin = jnp.sum((keys < low).astype(F32)).astype(jnp.int32)
            end = jnp.sum((keys <= high).astype(F32)).astype(jnp.int32)
            base = begin // align * align
            count = (end - base + TK - 1) // TK
            scal[which * 2 * TILES + tile] = jnp.minimum(base, size - count * TK)
            scal[which * 2 * TILES + TILES + tile] = count


def fetch(source, target, start, sem):
    return pltpu.make_async_copy(
        source.at[pl.ds(pl.multiple_of(start, target.shape[0]), target.shape[0]), :], target, sem
    )


def project(x, weight, bias, target):
    step = min(x.shape[0], 1024)
    for part in range(x.shape[0] // step):
        rows = slice(part * step, (part + 1) * step)
        value = mm(x[rows, :], weight)
        target[rows, :] = (value if bias is None else value + bias).astype(BF)


def self_forward_kernel(
    scal, query, content, mask_in, hot, kaug, vecs, small, proj, out, mine, other,
    q, k_out, v_out, qaug, ctx, exact, s1, weight_out, bias,
    score, peak, mixed, got, xq, xc, k, v, weight, mask, sem, sem_out,
):
    _, _, position = mesh_place()
    rows = xc.shape[0]
    copies = own_tiles(query, xq, sem, 32)
    copies.append(
        pltpu.make_async_copy(
            content.at[pl.ds(pl.multiple_of(position // 2 * rows, rows), rows), :], xc, sem.at[36]
        )
    )
    for pair in range(1, PAIRS):
        copies.append(
            pltpu.make_async_copy(
                mine.at[0, pair - 1, pl.ds(256, EXT), :], got.at[pair - 1], sem.at[36 + pair]
            )
        )
    late = pltpu.make_async_copy(mask_in, mask, sem.at[40])
    for copy in copies:
        copy.start()
    moves = load_weights(proj, out, mine, other, weight, sem)
    for copy in moves:
        copy.start()
    late.start()
    for copy in copies + moves:
        copy.wait()
    outs = [put(weight, weight_out, sem_out.at[0])]
    bias[:, lanes(0)] = small[...].astype(F32)
    for pair in range(1, PAIRS):
        bias[:, lanes(pair)] = got[pair - 1].astype(F32)
    q[...] = ((mm(xq[...], weight[0]) + bias[0:1, :]).astype(BF) * BF(HEAD ** (-0.5))).astype(BF)
    project(xc, weight[1], None, k)
    outs.append(put(k, k_out, sem_out.at[1]))
    project(xc, weight[2], bias[1:2, :], v)
    outs.append(put(v, v_out, sem_out.at[2]))
    late.wait()
    attend_forward(scal, 0, q, k, v, kaug, hot, mask, score, peak, mixed, qaug, ctx, exact)
    s1[...] = xq[...].astype(F32) + mm_cols(ctx[...], weight[3]) + vecs[0:1, :]
    for copy in outs:
        copy.wait()


def cross_forward_kernel(
    scal, s1, encoder, hot, kaug, vecs, bias, proj, out, mine, other,
    q, k_out, v_out, qaug, ctx, exact, s2, weight_out,
    score, peak, mixed, enc, k, v, weight, sem, sem_out,
):
    _, _, position = mesh_place()
    moves = load_weights(proj, out, mine, other, weight, sem)
    rows = enc.shape[0]
    late = pltpu.make_async_copy(
        encoder.at[pl.ds(pl.multiple_of(position // 2 * rows, rows), rows), :], enc, sem.at[32]
    )
    for copy in moves:
        copy.start()
    late.start()
    normed, _ = norm_parts(s1[...])
    first = normed * vecs[3:4, :] + vecs[6:7, :]
    for copy in moves:
        copy.wait()
    outs = [put(weight, weight_out, sem_out.at[0])]
    q[...] = (
        (mm(first.astype(BF), weight[0]) + bias[2:3, :]).astype(BF) * BF(HEAD ** (-0.5))
    ).astype(BF)
    late.wait()
    project(enc, weight[1], None, k)
    outs.append(put(k, k_out, sem_out.at[1]))
    project(enc, weight[2], bias[3:4, :], v)
    outs.append(put(v, v_out, sem_out.at[2]))
    attend_forward(scal, 1, q, k, v, kaug, hot, None, score, peak, mixed, qaug, ctx, exact)
    s2[...] = first + mm_cols(ctx[...], weight[3]) + vecs[1:2, :]
    for copy in outs:
        copy.wait()


def gelu_parts(v):
    c = math.sqrt(2.0 / math.pi)
    square = v * v
    t = jnp.tanh(c * (v + 0.044715 * square * v))
    value = 0.5 * v * (1.0 + t)
    slope = 0.5 * (1.0 + t) + 0.5 * v * (1.0 - t * t) * (c + (3.0 * 0.044715 * c) * square)
    return value, slope


def ffn_kernel(
    s2, cot_own, cot_got, bias, vecs, ffn_in, ffn_out, first_core, second_core,
    output, mine, theirs, back, sums, output_send,
    weight, hidden, slopes, low, grads, cot, sem, sem_cot,
):
    core, place, position = mesh_place()
    half = position % 2
    late = []
    for index in range(2):
        row = pl.multiple_of((half + 2 * index) * TQ, TQ)
        target = pl.multiple_of((2 * half + index) * TQ, TQ)
        late.append(
            put(cot_own.at[pl.ds(row, TQ), :], cot.at[pl.ds(target, TQ), :], sem_cot.at[index])
        )
    target = pl.multiple_of((1 - half) * 2 * TQ, 2 * TQ)
    late.append(put(cot_got, cot.at[pl.ds(target, 2 * TQ), :], sem_cot.at[2]))
    copies = [[] for _ in range(4)]
    for side, source in enumerate((ffn_in, ffn_out)):
        copies[0].append(put(source, weight.at[side, 0], sem.at[side]))
    for part in range(1, 4):
        for side, source in ((core, first_core), (1 - core, second_core)):
            for shift in range(4):
                row = pl.multiple_of(jnp.bitwise_xor(place, shift) * 128, 128)
                number = 2 + sum(len(group) for group in copies[1:])
                copies[part].append(
                    put(
                        source.at[shift, part - 1], weight.at[side, part, pl.ds(row, 128), :],
                        sem.at[number],
                    )
                )
    sums[...] = jnp.zeros(sums.shape, F32)
    normed2, inverse2 = norm_parts(s2[...])
    second = normed2 * vecs[4:5, :] + vecs[7:8, :]
    low[...] = second.astype(BF)
    total = second + vecs[2:3, :]
    def before_gelu(part):
        part_bias = jnp.concatenate([bias[4 + i : 5 + i, lanes(part)] for i in range(4)], axis=1)
        for copy in copies[part]:
            copy.wait()
        return mm(low[...], weight[0, part]) + part_bias

    ready = before_gelu(0)
    for part in range(4):
        block = slice(part * D, (part + 1) * D)
        pre = ready
        if part < 3:
            ready = before_gelu(part + 1)
        value, slope = gelu_parts(pre)
        hidden[:, block] = value.astype(BF)
        slopes[:, block] = slope
        total = total + mm(hidden[:, block], weight[1, part])
    normed3, inverse3 = norm_parts(total)
    output[...] = (normed3 * vecs[5:6, :] + vecs[8:9, :]).astype(BF)
    for copy in late:
        copy.wait()
    row = pl.multiple_of((1 - half) * 2 * TQ, 2 * TQ)
    output_send[...] = output[pl.ds(row, 2 * TQ), :]
    incoming = cot[...].astype(F32)
    sums[0:1, :] = col_sum(incoming * normed3)
    sums[1:2, :] = col_sum(incoming)
    third_grad = norm_backward(incoming, normed3, inverse3, vecs[5:6, :])
    branch = third_grad.astype(BF)
    sums[2:3, :] = col_sum(branch)
    total = third_grad
    ready = mm_cols(branch, weight[1, 0])
    for part in range(4):
        block = slice(part * D, (part + 1) * D)
        pre_grad = (slopes[:, block] * ready).astype(BF)
        if part < 3:
            ready = mm_cols(branch, weight[1, part + 1])
        sums[8 + part : 9 + part, :] = col_sum(pre_grad)
        grads[part, 0:D, :] = mm_rows(low[...], pre_grad).astype(BF)
        grads[part, D : 2 * D, :] = mm_rows(hidden[:, block], branch).astype(BF)
        if part == 3:
            moves = grad_copies(grads, mine, theirs, sem)
            for copy in moves:
                copy.start()
        total = total + mm_cols(pre_grad, weight[0, part])
    sums[3:4, :] = col_sum(total * normed2)
    sums[4:5, :] = col_sum(total)
    second_grad = norm_backward(total, normed2, inverse2, vecs[4:5, :])
    sums[5:6, :] = col_sum(second_grad.astype(BF))
    back[...] = second_grad
    for copy in moves:
        copy.wait()


def store_grad(grads, matrix, value):
    low = value.astype(BF)
    for pair in range(PAIRS):
        grads[pair, matrix * D : (matrix + 1) * D, :] = low[:, lanes(pair)]


def projection_grads(grads, x, low, matrix):
    store_grad(grads, matrix, mm_rows(x[...], low[...]))


def input_grads(dk, dv, weight, out):
    step = min(dk.shape[0], 1024)
    for part in range(dk.shape[0] // step):
        rows = slice(part * step, (part + 1) * step)
        out[rows, :] = (
            mm_cols(dk[rows, :], weight[1]) + mm_cols(dv[rows, :], weight[2])
        ).astype(BF)


def load_all(sources, targets, sem):
    copies = [
        pltpu.make_async_copy(source, target, sem.at[index])
        for index, (source, target) in enumerate(zip(sources, targets))
    ]
    for copy in copies:
        copy.start()
    return copies


def store_low(dk, dv, dk_low, dv_low, low, sem):
    copies = []
    for index, (value, target) in enumerate(((dk, dk_low), (dv, dv_low))):
        for part in range(value.shape[0] // 512):
            rows = slice(part * 512, (part + 1) * 512)
            low[index, rows, :] = value[rows, :].astype(BF)
            copies.append(put(low.at[index, rows, :], target.at[rows, :], sem.at[len(copies)]))
    return copies


def cross_attention_grad_kernel(
    scal, dss2, weight_in, q_in, k_in, v_in, qaug_in, exact_in, kaug_in,
    dq, dk_low, dv_low, keep, send,
    grad_ctx, weight, enc_grad, dk, dv, dq_tile, low, q, k, v, qaug, exact, kaug, sem,
):
    first = put(weight_in, weight, sem.at[7])
    copies = load_all(
        (q_in, qaug_in, exact_in, kaug_in, k_in, v_in), (q, qaug, exact, kaug, k, v), sem
    )
    dk[...] = jnp.zeros(dk.shape, F32)
    dv[...] = jnp.zeros(dv.shape, F32)
    first.wait()
    grad_ctx[...] = mm(dss2[...].astype(BF), weight[3]).astype(BF)
    for copy in copies:
        copy.wait()
    attend_backward(scal, 1, q, k, v, kaug, qaug, None, grad_ctx, exact, dq, dk, dv, dq_tile)
    copies = store_low(dk, dv, dk_low, dv_low, low, sem)
    input_grads(low.at[0], low.at[1], weight, enc_grad)
    for copy in copies:
        copy.wait()
    send_rows(enc_grad, keep, send, sem)


def cross_projection_grad_kernel(
    dss2, s1, weight_in, self_weight, ctx, self_ctx, dq, dk_in, dv_in, encoder, vecs, sums_in,
    mine, theirs, back, grad_ctx, sums,
    grads, enc, weight, dk, dv, sem,
):
    _, _, position = mesh_place()
    rows = enc.shape[0]
    start = pl.multiple_of(position // 2 * rows, rows)
    early = [
        put(weight_in.at[0], weight.at[0], sem.at[0]),
        put(self_weight.at[3], weight.at[1], sem.at[1]),
    ]
    late = [
        put(encoder.at[pl.ds(start, rows), :], enc, sem.at[2]),
        put(dk_in, dk, sem.at[3]),
        put(dv_in, dv, sem.at[4]),
    ]
    sums[...] = sums_in[...]
    normed, inverse = norm_parts(s1[...])
    first = (normed * vecs[3:4, :] + vecs[6:7, :]).astype(BF)
    store_grad(grads, 0, mm_rows(first, dq[...]))
    store_grad(grads, 3, mm_rows(dss2[...].astype(BF), ctx[...]))
    for copy in early:
        copy.wait()
    total = dss2[...] + mm_cols(dq[...], weight[0])
    sums[6:7, :] = col_sum(total * normed)
    sums[7:8, :] = col_sum(total)
    first_grad = norm_backward(total, normed, inverse, vecs[3:4, :])
    branch = first_grad.astype(BF)
    sums[12:13, :] = col_sum(branch)
    back[...] = first_grad
    grad_ctx[...] = mm(branch, weight[1]).astype(BF)
    store_grad(grads, 4, mm_rows(branch, self_ctx[...]))
    sums[14:15, :] = col_sum(dq[...])
    for copy in late:
        copy.wait()
    projection_grads(grads, enc, dk, 1)
    projection_grads(grads, enc, dv, 2)
    sums[15:16, :] = col_sum(dv[...])
    send_grads(grads, mine, theirs, sem)


def self_attention_grad_kernel(
    scal, grad_ctx, q_in, k_in, v_in, qaug_in, exact_in, mask_in, kaug_in, weight_in,
    dq, dk_low, dv_low, keep, send,
    dk, dv, dq_tile, low, q, k, v, qaug, exact, mask_t, kaug, sem, weight, content_grad,
):
    late = put(weight_in.at[1:3], weight.at[1:3], sem.at[7])
    copies = load_all(
        (q_in, qaug_in, exact_in, kaug_in, k_in, v_in, mask_in),
        (q, qaug, exact, kaug, k, v, mask_t),
        sem,
    )
    dk[...] = jnp.zeros(dk.shape, F32)
    dv[...] = jnp.zeros(dv.shape, F32)
    for copy in copies:
        copy.wait()
    attend_backward(scal, 2, q, k, v, kaug, qaug, mask_t, grad_ctx, exact, dq, dk, dv, dq_tile)
    late.wait()
    copies = store_low(dk, dv, dk_low, dv_low, low, sem)
    input_grads(low.at[0], low.at[1], weight, content_grad)
    half = lax.axis_index("mp") % 2
    mid = content_grad.shape[0] // 2
    keep[...] = content_grad[pl.ds(pl.multiple_of(half * mid, mid), mid), :]
    send[...] = content_grad[pl.ds(pl.multiple_of((1 - half) * mid, mid), mid), :]
    for copy in copies:
        copy.wait()


def self_projection_grad_kernel(
    fsg, weight_in, dq, dk, dv, query, content, sums,
    mine, theirs, send, query_grad,
    grads, xq, xc, weight, sem, sem_late,
):
    _, _, position = mesh_place()
    half = position % 2
    rows = xc.shape[0]
    copies = own_tiles(query, xq, sem, 0)
    for copy in copies:
        copy.start()
    place = pl.multiple_of(position // 2 * rows, rows)
    content_copy = put(content.at[pl.ds(place, rows), :], xc, sem_late.at[0])
    weight_copy = put(weight_in.at[0], weight, sem_late.at[1])
    for copy in copies:
        copy.wait()
    store_grad(grads, 0, mm_rows(xq[...], dq[...]))
    content_copy.wait()
    projection_grads(grads, xc, dk, 1)
    projection_grads(grads, xc, dv, 2)
    bias_q = col_sum(dq[...])
    bias_v = col_sum(dv[...])
    for pair in range(PAIRS):
        parts = [bias_q[:, lanes(pair)], bias_v[:, lanes(pair)]]
        parts += [sums[14:15, lanes(pair)], sums[15:16, lanes(pair)]]
        parts += [sums[8 + pair : 9 + pair, lanes(i)] for i in range(4)]
        for index in (0, 1, 2, 3, 4, 5, 6, 7, 12):
            parts += [sums[index : index + 1, lanes(i)] for i in range(4)]
        parts += [jnp.zeros((SUB * EXT - len(parts), PAIR), F32)]
        grads[pair, 3 * D : 3 * D + SUB * EXT, :] = jnp.concatenate(parts, axis=0).astype(BF)
    moves = grad_copies(grads, mine, theirs, sem)
    for copy in moves:
        copy.start()
    weight_copy.wait()
    query_grad[...] = (fsg[...] + mm_cols(dq[...], weight[...])).astype(BF)
    row = pl.multiple_of((1 - half) * 2 * TQ, 2 * TQ)
    send[...] = query_grad[pl.ds(row, 2 * TQ), :]
    for copy in moves:
        copy.wait()


def add_split_kernel(mine, theirs, *outs):
    for index, out in enumerate(outs):
        out[...] = (mine[index].astype(F32) + theirs[index].astype(F32)).astype(BF)


def sum_split_kernel(own, first, second, third, *outs):
    for index, out in enumerate(outs):
        out[...] = (
            (own[index].astype(F32) + first[index].astype(F32))
            + (second[index].astype(F32) + third[index].astype(F32))
        ).astype(BF)


def sum_merge_kernel(a0, a1, a2, a3, b0, b1, b2, b3, *outs):
    rows = a0.shape[1]
    for index, out in enumerate(outs):
        for group, spot in (((a0, a1, a2, a3), slice(0, rows)), ((b0, b1, b2, b3), slice(rows, None))):
            own, first, second, third = [part[index].astype(F32) for part in group]
            out[spot, :] = ((own + first) + (second + third)).astype(BF)


def sum_kernel(own, first, second, third, out):
    out[...] = (
        (own[...].astype(F32) + first[...].astype(F32))
        + (second[...].astype(F32) + third[...].astype(F32))
    ).astype(out.dtype)


def finish_ffn_kernel(line, other, ffn_in, ffn_out, wide):
    core, place, _ = mesh_place()
    for side, source in ((core, line), (1 - core, other)):
        for shift in range(4):
            row = pl.multiple_of((4 * side + jnp.bitwise_xor(place, shift)) * 128, 128)
            wide[pl.ds(row, 128), :] = source[shift].astype(F32)
    ffn_in[...] = wide[0:D, :]
    ffn_out[...] = wide[D:, :]


def finish_rows_kernel(
    output_own, output_got, query_own, query_got, keep, got, output, query, content
):
    _, _, position = mesh_place()
    half = position % 2
    for own, theirs, target in (
        (output_own, output_got, output), (query_own, query_got, query)
    ):
        for index in range(2):
            row = pl.multiple_of((2 * half + index) * TQ, TQ)
            place_own = pl.multiple_of((half + 2 * index) * TQ, TQ)
            place_got = pl.multiple_of((1 - half + 2 * index) * TQ, TQ)
            first = index * TQ
            target[pl.ds(place_own, TQ), :] = own[pl.ds(row, TQ), :]
            target[pl.ds(place_got, TQ), :] = theirs[first : first + TQ, :]
    content[...] = (keep[...].astype(F32) + got[...].astype(F32)).astype(BF)


def finish_kernel(
    line, other,
    self_proj, self_bias, self_out, cross_proj, cross_bias, cross_out, ffn_bias,
    out_bias, gain, moved, flat, flat_self,
):
    core, place, _ = mesh_place()
    cross_rows, self_rows = flat.shape[0] // SUB, flat_self.shape[0] // SUB
    for side, source in ((core, line), (1 - core, other)):
        for shift in range(4):
            spot = 4 * side + jnp.bitwise_xor(place, shift)
            row = pl.multiple_of(spot * cross_rows, 8)
            flat[pl.ds(row, cross_rows), :] = source[shift, 0:cross_rows, :].astype(F32)
            row = pl.multiple_of(spot * self_rows, 8)
            flat_self[pl.ds(row, self_rows), :] = source[shift, cross_rows:, :].astype(F32)
    for matrix in range(3):
        cross_proj[matrix] = flat[matrix * D : (matrix + 1) * D, :]
        self_proj[matrix] = flat_self[matrix * D : (matrix + 1) * D, :]
    cross_out[...] = flat[3 * D : 4 * D, :].T
    self_out[...] = flat[4 * D : 5 * D, :].T
    start = 3 * D
    self_bias[...] = flat_self[start : start + 2, :]
    cross_bias[...] = flat_self[start + 2 : start + 4, :]
    for block in range(4):
        ffn_bias[:, lanes(block)] = flat_self[start + 4 + block : start + 5 + block, :]
    for target, order in ((out_bias, (8, 5, 2)), (gain, (6, 3, 0)), (moved, (7, 4, 1))):
        for index, number in enumerate(order):
            for block in range(4):
                row = start + 8 + number * 4 + block
                target[index : index + 1, lanes(block)] = flat_self[row : row + 1, :]


def call(kernel, outs, inputs, scratch=(), smem_in=(), any_in=(), any_out=(), smem_out=(), long=False):
    def space(index, smem, hbm):
        return pltpu.SMEM if index in smem else pl.ANY if index in hbm else pltpu.VMEM

    return pl.pallas_call(
        kernel,
        out_shape=[jax.ShapeDtypeStruct(shape, dtype) for shape, dtype in outs],
        in_specs=[
            pl.BlockSpec(memory_space=space(index, smem_in, any_in)) for index in range(len(inputs))
        ],
        out_specs=[
            pl.BlockSpec(memory_space=space(index, smem_out, any_out)) for index in range(len(outs))
        ],
        scratch_shapes=list(scratch),
        compiler_params=pltpu.CompilerParams(vmem_limit_bytes=VMEM_LIMIT),
        cost_estimate=pl.CostEstimate(
            flops=10**13 if long else 10**6, bytes_accessed=1 << (30 if long else 14),
            transcendentals=0,
        ),
    )(*inputs)


def after(value, *others):
    flat, tree = jax.tree.flatten(value)
    tied = lax.optimization_barrier(tuple(flat) + tuple(others))
    return jax.tree.unflatten(tree, tied[: len(flat)])


def body(
    query_stream, content_stream, encoder, dec_segments, enc_segments, key_rank, observe_limit,
    padding, self_proj, self_bias, self_out, cross_proj, cross_bias, cross_out, ffn_in,
    ffn_in_bias, ffn_out, out_bias, norm_gain, norm_bias, cotangent,
):
    members = lax.axis_size("mp")
    groups = lax.axis_size("dp")
    length = dec_segments.shape[1]
    sources = enc_segments.shape[1]
    DMA = pltpu.SemaphoreType.DMA

    def swap(value, axis, mask):
        size = members if axis == "mp" else groups
        return lax.ppermute(value, axis, [(i, i ^ mask) for i in range(size)])

    def along(values):
        return [swap(value, "mp", shift + 1) for shift, value in enumerate(values)]

    def across(values):
        return [swap(value, "dp", 2 * shift + 2) for shift, value in enumerate(values)]

    own12, own3, cot_send, small = call(
        pack_kernel,
        [
            ((512 + EXT, PAIR), BF), ((2 * D // SUB, D), BF), ((2 * TQ, D), BF),
            ((EXT, PAIR), BF),
        ],
        (
            self_proj, self_out, cross_proj, cross_out, ffn_in, ffn_out, self_bias, cross_bias,
            ffn_in_bias, cotangent,
        ),
    )
    line12 = along([own12] * 3)
    scal, mask, mask_t, hot, kaug_dec, kaug_enc, vecs = call(
        prep_kernel,
        [
            ((6 * TILES,), jnp.int32), ((OWN, length), F32), ((length, OWN), F32),
            ((OWN, PAIR), BF), ((length, PAIR), BF), ((sources, PAIR), BF), ((EXT, D), F32),
        ],
        (
            dec_segments, enc_segments, key_rank, observe_limit, padding, out_bias, norm_gain,
            norm_bias,
        ),
        [pltpu.VMEM((8, length), F32)],
        smem_out=(0,),
    )
    line12, hot = after((line12, hot))
    line1 = jnp.stack([value[: 256 + EXT] for value in line12])
    line2 = jnp.stack([value[256 + EXT :] for value in line12])
    plane1, line3 = after((across([line1] * 3), along([after(own3, line1)] * 3)))
    plane1 = jnp.stack([line1] + plane1)
    line3 = jnp.stack(line3)
    other1 = swap(plane1, "dp", 1)
    cot_got = swap(after(cot_send, line1), "mp", 1)
    plane2 = across([after(line2, plane1)] * 3)

    def attention_outs(keys):
        return [
            ((OWN, D), BF), ((keys, D), BF), ((keys, D), BF), ((2 * PAIRS, OWN, PAIR), BF),
            ((OWN, D), BF), ((OWN, D), F32), ((OWN, D), F32), ((4, D, D), BF),
        ]

    def attention_scratch(keys):
        return [
            pltpu.VMEM((PAIRS, 2 * TQ, keys), F32), pltpu.VMEM((PAIRS, 2 * TQ, PAIR), F32),
            pltpu.VMEM((PAIRS, 2 * TQ, 2 * PAIR), F32),
        ]

    def backward_scratch(keys, masked=False):
        shapes = [
            pltpu.VMEM((keys, D), F32), pltpu.VMEM((keys, D), F32),
            pltpu.VMEM((PAIRS, 2 * TQ, PAIR), F32), pltpu.VMEM((2, keys, D), BF),
            pltpu.VMEM((OWN, D), BF), pltpu.VMEM((keys, D), BF), pltpu.VMEM((keys, D), BF),
            pltpu.VMEM((2 * PAIRS, OWN, PAIR), BF), pltpu.VMEM((OWN, D), F32),
        ]
        if masked:
            shapes.append(pltpu.VMEM((keys, OWN), F32))
        return shapes + [pltpu.VMEM((keys, PAIR), BF), DMA((8,))]

    q1, k1, v1, qaug1, ctx1, exact1, s1, weight1, bias = call(
        self_forward_kernel,
        attention_outs(length) + [((EXT, D), F32)],
        (
            scal, query_stream, content_stream, mask, hot, kaug_dec, vecs, small, self_proj,
            self_out, plane1, other1,
        ),
        attention_scratch(length)
        + [
            pltpu.VMEM((PAIRS - 1, EXT, PAIR), BF), pltpu.VMEM((OWN, D), BF),
            pltpu.VMEM((length, D), BF), pltpu.VMEM((length, D), BF), pltpu.VMEM((length, D), BF),
            pltpu.VMEM((4, D, D), BF), pltpu.VMEM((OWN, length), F32), DMA((41,)), DMA((3,)),
        ],
        smem_in=(0,), any_in=(1, 2, 3, 8, 10, 11), any_out=(1, 2, 7),
    )
    plane2, s1, cot_got = after((plane2, s1, cot_got))
    plane2 = jnp.stack([line2] + plane2)
    plane3 = across([after(line3, plane2)] * 3)
    other2 = swap(plane2, "dp", 1)
    q2, k2, v2, qaug2, ctx2, exact2, s2, weight2 = call(
        cross_forward_kernel,
        attention_outs(sources),
        (
            scal, s1, encoder, hot, kaug_enc, vecs, bias, cross_proj, cross_out, plane2, other2,
        ),
        attention_scratch(sources)
        + [
            pltpu.VMEM((sources, D), BF), pltpu.VMEM((sources, D), BF), pltpu.VMEM((sources, D), BF),
            pltpu.VMEM((4, D, D), BF), DMA((33,)), DMA((3,)),
        ],
        smem_in=(0,), any_in=(2, 7, 9, 10), any_out=(1, 2, 7),
    )
    plane3, s2 = after((plane3, s2))
    plane3 = jnp.stack([line3] + plane3)
    other3 = swap(plane3, "dp", 1)

    def group_outs(rows, width):
        return [((4, 4, rows // SUB, width), BF)] * 2

    output_own, mine3, theirs3, dss2, sums, output_send = call(
        ffn_kernel,
        [((OWN, D), BF)]
        + group_outs(2 * D, D)
        + [((OWN, D), F32), ((EXT, D), F32), ((2 * TQ, D), BF)],
        (s2, cotangent, cot_got, bias, vecs, ffn_in, ffn_out, plane3, other3),
        [
            pltpu.VMEM((2, 4, D, D), BF), pltpu.VMEM((OWN, 4 * D), BF),
            pltpu.VMEM((OWN, 4 * D), F32), pltpu.VMEM((OWN, D), BF), pltpu.VMEM((4, 2 * D, D), BF),
            pltpu.VMEM((OWN, D), BF), DMA((26,)), DMA((3,)),
        ],
        any_in=(1, 2, 5, 6, 7, 8), any_out=(1, 2),
    )

    def low_sum(*values):
        total = values[0].astype(F32)
        for value in values[1:]:
            total = total + value.astype(F32)
        return total.astype(BF)

    def add_split(mine, theirs):
        return [low_sum(mine[index], theirs[index]) for index in range(4)]

    def sum_split(parts):
        return [low_sum(*[part[index] for part in parts]) for index in range(4)]

    def sum_parts(parts):
        piece = parts[0].astype(F32)
        for part in parts[1:]:
            piece = piece + part.astype(F32)
        bit = SUB
        while bit < groups:
            piece = piece + swap(piece, "dp", bit)
            bit *= 2
        return piece.astype(BF)

    theirs3 = swap(theirs3, "dp", 1)
    dq2, dk2, dv2, enc_keep, enc_send = call(
        cross_attention_grad_kernel,
        [((OWN, D), BF), ((sources, D), BF), ((sources, D), BF)] + [((sources // 2, D), BF)] * 2,
        (scal, dss2, weight2, q2, k2, v2, qaug2, exact2, kaug_enc),
        [pltpu.VMEM((OWN, D), BF), pltpu.VMEM((4, D, D), BF), pltpu.VMEM((sources, D), BF)]
        + backward_scratch(sources),
        smem_in=(0,), any_in=(2, 3, 4, 5, 6, 7, 8), any_out=(1, 2, 3, 4), long=True,
    )
    output_got = swap(output_send, "mp", 1)
    theirs3, dq2, output_got = after((theirs3, dq2, output_got))
    parts3 = add_split(mine3, theirs3)
    dq2 = after(dq2, parts3[0])
    moved3 = across(parts3[1:])
    enc_theirs = swap(enc_send, "mp", 1)
    mine2, theirs2, fsg, grad_ctx1, sums = call(
        cross_projection_grad_kernel,
        group_outs(5 * D, PAIR) + [((OWN, D), F32), ((OWN, D), BF), ((EXT, D), F32)],
        (dss2, s1, weight2, weight1, ctx2, ctx1, dq2, dk2, dv2, encoder, vecs, sums),
        [
            pltpu.VMEM((PAIRS, 5 * D, PAIR), BF), pltpu.VMEM((sources, D), BF),
            pltpu.VMEM((2, D, D), BF), pltpu.VMEM((sources, D), BF), pltpu.VMEM((sources, D), BF),
            DMA((8,)),
        ],
        any_in=(2, 3, 7, 8, 9), any_out=(0, 1), long=True,
    )
    theirs2 = swap(theirs2, "dp", 1)
    dq1, dk1, dv1, content_keep, content_send = call(
        self_attention_grad_kernel,
        [((OWN, D), BF), ((length, D), BF), ((length, D), BF)] + [((length // 2, D), BF)] * 2,
        (scal, grad_ctx1, q1, k1, v1, qaug1, exact1, mask_t, kaug_dec, weight1),
        backward_scratch(length, True)
        + [pltpu.VMEM((4, D, D), BF), pltpu.VMEM((length, D), BF)],
        smem_in=(0,), any_in=(2, 3, 4, 5, 6, 7, 8, 9), any_out=(1, 2), long=True,
    )
    content_got = swap(content_send, "mp", 1)
    moved3, theirs2, enc_theirs, dq1 = after((moved3, theirs2, enc_theirs, dq1))
    slots3 = sum_split([parts3[0]] + moved3)
    parts2 = add_split(mine2, theirs2)
    dq1 = after(dq1, slots3[0], parts2[0])
    moved_slots3 = along(slots3[1:])
    moved2 = across(parts2[1:])
    mine1, theirs1, rows_send, query_own = call(
        self_projection_grad_kernel,
        group_outs(3 * D + SUB * EXT, PAIR)
        + [((2 * TQ, D), BF), ((OWN, D), BF)],
        (fsg, weight1, dq1, dk1, dv1, query_stream, content_stream, sums),
        [
            pltpu.VMEM((PAIRS, 3 * D + SUB * EXT, PAIR), BF),
            pltpu.VMEM((OWN, D), BF), pltpu.VMEM((length, D), BF), pltpu.VMEM((D, D), BF),
            DMA((8,)), DMA((2,)),
        ],
        any_in=(1, 5, 6), any_out=(0, 1), long=True,
    )
    theirs1, moved_slots3, moved2 = after((theirs1, moved_slots3, moved2))
    theirs1 = swap(theirs1, "dp", 1)
    rows_got = swap(rows_send, "mp", 1)
    parts1 = add_split(mine1, theirs1)
    moved1 = across(parts1[1:])
    piece3 = sum_parts([slots3[0]] + moved_slots3)
    encoder_grad = (enc_keep.astype(F32) + enc_theirs.astype(F32)).astype(BF)
    moved1, content_got = after((moved1, content_got))
    slots = [
        jnp.concatenate(both, axis=0)
        for both in zip(sum_split([parts2[0]] + moved2), sum_split([parts1[0]] + moved1))
    ]
    moved_slots = along(slots[1:])
    ffn_line = across([after(piece3, slots[0])] * 3)
    moved_slots, ffn_line, encoder_grad, rows_got = after(
        (moved_slots, ffn_line, encoder_grad, rows_got)
    )
    piece = sum_parts([slots[0]] + moved_slots)
    ffn_line = jnp.stack([piece3] + ffn_line)
    ffn_other = swap(ffn_line, "dp", 1)
    output, query_grad, content_grad = call(
        finish_rows_kernel,
        [((OWN, D), BF), ((OWN, D), BF), ((length // 2, D), BF)],
        (output_own, output_got, query_own, rows_got, content_keep, content_got),
    )
    line, ffn_other, content_grad = after((across([piece] * 3), ffn_other, content_grad))
    line = jnp.stack([piece] + line)
    other = swap(line, "dp", 1)
    ffn_in_grad, ffn_out_grad = call(
        finish_ffn_kernel,
        [((D, D), F32), ((D, D), F32)],
        (ffn_line, ffn_other),
        [pltpu.VMEM((2 * D, D), F32)],
    )

    (
        self_proj_grad, self_bias_grad, self_out_grad, cross_proj_grad, cross_bias_grad,
        cross_out_grad, ffn_bias_grad, out_bias_grad,
        gain_grad, shift_grad,
    ) = call(
        finish_kernel,
        [
            ((3, D, PAIR), F32), ((2, PAIR), F32), ((PAIR, D), F32), ((3, D, PAIR), F32),
            ((2, PAIR), F32), ((PAIR, D), F32), ((1, D), F32),
            ((3, D), F32), ((3, D), F32), ((3, D), F32),
        ],
        (line, other),
        [
            pltpu.VMEM((5 * D, PAIR), F32), pltpu.VMEM((3 * D + SUB * EXT, PAIR), F32),
        ],
    )
    return (
        output,
        query_grad,
        content_grad,
        encoder_grad,
        self_proj_grad,
        self_bias_grad,
        self_out_grad,
        cross_proj_grad,
        cross_bias_grad,
        cross_out_grad,
        ffn_in_grad,
        ffn_bias_grad.reshape(D),
        ffn_out_grad,
        out_bias_grad,
        gain_grad,
        shift_grad,
    )


def solution(mesh):
    return jax.shard_map(
        body,
        mesh=mesh,
        in_specs=(
            P("dp", None), P("dp", None), P("dp", None), P("dp", None), P("dp", None),
            P("dp", None), P("dp", None), P("dp", None), P(None, None, "mp"), P(None, "mp"),
            P("mp", None), P(None, None, "mp"), P(None, "mp"), P("mp", None), P(None, "mp"),
            P("mp"), P("mp", None), P(), P(), P(), P(("dp", "mp"), None),
        ),
        out_specs=(
            P(("dp", "mp"), None), P(("dp", "mp"), None), P(("dp", "mp"), None),
            P(("dp", "mp"), None), P(None, None, "mp"), P(None, "mp"), P("mp", None),
            P(None, None, "mp"), P(None, "mp"), P("mp", None), P(None, "mp"), P("mp"),
            P("mp", None), P(), P(), P(),
        ),
        check_vma=False,
    )
```

```python
import math

import jax
import jax.numpy as jnp
from jax import lax
from jax.experimental import pallas as pl
from jax.experimental.pallas import tpu as pltpu
from jax.sharding import PartitionSpec as P

HEAD = 64
EPSILON = 1e-05
MASKED = -1000000000.0
LOG2E = math.log2(math.e)
D = 512
PAIR = 128
ROWS = 16
PAIRS = 4
OWN = 512
TQ = 128
ROW_TILES = 8
TK = 256
TILES = OWN // TQ
SUB = 8
EXT = 16
BF = jnp.bfloat16
F32 = jnp.float32
VMEM_LIMIT = 56 * 1024 * 1024


def mm(left, right):
    return jnp.dot(left, right, preferred_element_type=F32)


def mm_rows(left, right):
    return lax.dot_general(left, right, (((0,), (0,)), ((), ())), preferred_element_type=F32)


def mm_cols(left, right):
    return lax.dot_general(left, right, (((1,), (1,)), ((), ())), preferred_element_type=F32)


def norm_parts(summed):
    average = jnp.mean(summed, axis=-1, keepdims=True)
    centred = summed - average
    inverse = lax.rsqrt(jnp.mean(centred * centred, axis=-1, keepdims=True) + EPSILON)
    return centred * inverse, inverse


def norm_backward(incoming, normed, inverse, gain):
    scaled = incoming * gain
    inner = (
        scaled
        - jnp.mean(scaled, axis=-1, keepdims=True)
        - normed * jnp.mean(scaled * normed, axis=-1, keepdims=True)
    )
    return inner * inverse


def col_sum(values):
    return jnp.sum(values.astype(F32), axis=0, keepdims=True)


def half_lanes(rows):
    return lax.broadcasted_iota(jnp.int32, (rows, PAIR), 1) < HEAD


def stack_heads(values):
    keep = half_lanes(values.shape[0])
    zero = jnp.zeros_like(values)
    return jnp.concatenate([jnp.where(keep, values, zero), jnp.where(keep, zero, values)], axis=0)


def pieces_of(value, first_lane, base):
    lane = lax.broadcasted_iota(jnp.int32, value.shape, 1)
    high = value.astype(BF)
    rest = value - high.astype(F32)
    middle = rest.astype(BF)
    low = (rest - middle.astype(F32)).astype(BF)
    out = jnp.where(lane == first_lane, high, base)
    out = jnp.where(lane == first_lane + 1, middle, out)
    return jnp.where(lane == first_lane + 2, low, out)


def lanes(pair):
    return slice(pair * PAIR, (pair + 1) * PAIR)


def key_range(scal, which, tile, align):
    base = pl.multiple_of(scal[which * 2 * TILES + tile], align)
    count = scal[which * 2 * TILES + TILES + tile]
    return base, count


def over_keys(count, block):
    done = 0
    for wide in (4, 3, 2, 1):
        whole = (count - done) // wide

        def step(index, carry, done=done, wide=wide):
            block((done + index * wide) * TK, wide * TK)
            return carry

        lax.fori_loop(0, whole, step, 0)
        done = done + whole * wide


def attend_forward(scal, which, q, k, v, kaug, hot, mask, score, peak, mixed, qaug, ctx, exact):
    align = ROWS if mask is None else PAIR

    def tile_body(tile, carry):
        base, count = key_range(scal, which, tile, align)
        rows = pl.ds(pl.multiple_of(tile * TQ, TQ), TQ)
        extra = hot[rows, :]
        extra2 = jnp.concatenate([extra, extra], axis=0)
        peak[...] = jnp.full(peak.shape, -jnp.inf, F32)
        mixed[...] = jnp.zeros(mixed.shape, F32)

        def scores(begin, size):
            off = pl.multiple_of(base + begin, align)
            here = pl.ds(pl.multiple_of(begin, TK), size)
            ka = kaug[pl.ds(off, size), :]
            if mask is not None:
                block = mask[rows, pl.ds(off, size)].astype(F32)
                block = jnp.concatenate([block, block], axis=0)
            for pair in range(PAIRS):
                q2 = jnp.concatenate([stack_heads(q[rows, lanes(pair)]), extra2], axis=1)
                kk = jnp.concatenate([k[pl.ds(off, size), lanes(pair)], ka], axis=1)
                s = mm_cols(q2, kk)
                if mask is not None:
                    s = s + block
                score[pair, :, here] = s
                top = peak[pair]
                for part in range(size // PAIR):
                    top = jnp.maximum(top, s[:, part * PAIR : (part + 1) * PAIR])
                peak[pair] = top

        over_keys(count, scores)
        for pair in range(PAIRS):
            peak[pair] = jnp.broadcast_to(
                jnp.max(peak[pair], axis=1, keepdims=True), (2 * TQ, PAIR)
            )

        def weights(begin, size):
            off = pl.multiple_of(base + begin, align)
            here = pl.ds(pl.multiple_of(begin, TK), size)
            minus = jnp.full((size, PAIR), -1.0, BF)
            for pair in range(PAIRS):
                top = jnp.concatenate([peak[pair]] * (size // PAIR), axis=1)
                p = jnp.exp2((score[pair, :, here] - top) * LOG2E).astype(BF)
                vv = jnp.concatenate([v[pl.ds(off, size), lanes(pair)], minus], axis=1)
                mixed[pair] += mm(p, vv)

        over_keys(count, weights)
        keep = half_lanes(TQ)
        for pair in range(PAIRS):
            both = mixed[pair]
            total = -both[:, PAIR:]
            normal = both[:, :PAIR] / total
            out = jnp.where(keep, normal[:TQ], normal[TQ:])
            exact[rows, lanes(pair)] = out
            ctx[rows, lanes(pair)] = out.astype(BF)
            logsum = peak[pair] + jnp.log(total)
            for head in range(2):
                part = logsum[head * TQ : (head + 1) * TQ]
                qaug[2 * pair + head, rows, :] = pieces_of(part, 4, extra)
        return carry

    lax.fori_loop(0, TILES, tile_body, 0)


def attend_backward(scal, which, q, k, v, kaug, qaug, mask_t, grad, exact, dq, dk, dv, dq_tile):
    def tile_body(tile, carry):
        base, count = key_range(scal, which, tile, ROWS)
        start = pl.multiple_of(tile * TQ, TQ)
        rows = pl.ds(start, TQ)
        dq_tile[...] = jnp.zeros(dq_tile.shape, F32)
        keep = half_lanes(TQ)
        grads, queries, grad_aug, query_aug = [], [], [], []
        for pair in range(PAIRS):
            g = grad[rows, lanes(pair)]
            inner = g.astype(F32) * exact[rows, lanes(pair)]
            first = jnp.sum(jnp.where(keep, inner, 0.0), axis=1, keepdims=True)
            second = jnp.sum(jnp.where(keep, 0.0, inner), axis=1, keepdims=True)
            delta = jnp.broadcast_to(jnp.concatenate([first, second], axis=0), (2 * TQ, PAIR))
            aug = pieces_of(delta, 0, jnp.zeros((2 * TQ, PAIR), BF))
            g2 = stack_heads(g)
            q2 = stack_heads(q[rows, lanes(pair)])
            grads.append(g2)
            queries.append(q2)
            grad_aug.append(jnp.concatenate([g2, aug], axis=1))
            qa = jnp.concatenate([qaug[2 * pair, rows, :], qaug[2 * pair + 1, rows, :]], axis=0)
            query_aug.append(jnp.concatenate([q2, qa], axis=1))

        def keys(begin, size):
            off = pl.multiple_of(base + begin, ROWS)
            here = pl.ds(off, size)
            ka = kaug[here, :]
            minus = jnp.full((size, PAIR), -1.0, BF)
            if mask_t is not None:
                block = mask_t[here, rows].astype(F32)
                block = jnp.concatenate([block, block], axis=1)

            def raw(pair):
                kp = k[here, lanes(pair)]
                vp = jnp.concatenate([v[here, lanes(pair)], minus], axis=1)
                s = mm_cols(jnp.concatenate([kp, ka], axis=1), query_aug[pair])
                return kp, s, mm_cols(vp, grad_aug[pair])

            ready = raw(0)
            for pair in range(PAIRS):
                kp, s, dp = ready
                if pair + 1 < PAIRS:
                    ready = raw(pair + 1)
                if mask_t is not None:
                    s = s + block
                p = jnp.exp2(s * LOG2E)
                ds = (p * dp).astype(BF)
                dv[here, lanes(pair)] += mm(p.astype(BF), grads[pair])
                dk[here, lanes(pair)] += mm(ds, queries[pair])
                dq_tile[pair] += mm_rows(ds, kp)

        over_keys(count, keys)
        for pair in range(PAIRS):
            both = dq_tile[pair] * HEAD ** (-0.5)
            dq[rows, lanes(pair)] = jnp.where(keep, both[:TQ], both[TQ:]).astype(BF)
        return carry

    lax.fori_loop(0, TILES, tile_body, 0)


def mesh_place():
    group = lax.axis_index("dp")
    return group % 2, (group // 2) % 4, lax.axis_index("mp")


def run_copies(copies):
    for copy in copies:
        copy.start()
    for copy in copies:
        copy.wait()


def load_weights(proj, out, mine, other, weight, sem):
    core, place, _ = mesh_place()
    copies = []
    for matrix in range(3):
        copies.append(
            pltpu.make_async_copy(
                proj.at[matrix], weight.at[matrix, :, lanes(0)], sem.at[len(copies)]
            )
        )
    for side, source in ((core, mine), (1 - core, other)):
        for shift in range(4):
            spot = jnp.bitwise_xor(place, shift)
            matrix = 2 * side + spot // 2
            row = pl.multiple_of((spot % 2) * 256, 256)
            for pair in range(1, PAIRS):
                copies.append(
                    pltpu.make_async_copy(
                        source.at[shift, pair - 1, pl.ds(0, 256), :],
                        weight.at[matrix, pl.ds(row, 256), lanes(pair)],
                        sem.at[len(copies)],
                    )
                )
    weight[3, :, lanes(0)] = out[...].astype(F32).T.astype(BF)
    return copies


def put(source, target, sem):
    copy = pltpu.make_async_copy(source, target, sem)
    copy.start()
    return copy


def own_tiles(source, target, sem, first):
    _, _, position = mesh_place()
    copies = []
    for tile in range(TILES):
        row = pl.multiple_of((position // 2 * ROW_TILES + 2 * tile + position % 2) * TQ, TQ)
        copies.append(
            pltpu.make_async_copy(
                source.at[pl.ds(row, TQ), :], target.at[tile * TQ : (tile + 1) * TQ, :],
                sem.at[first + tile],
            )
        )
    return copies


def grad_copies(buffer, mine, theirs, sem):
    core, place, _ = mesh_place()
    chunk = buffer.shape[1] // SUB
    copies = []
    for side, target in ((core, mine), (1 - core, theirs)):
        for shift in range(4):
            row = pl.multiple_of((4 * side + jnp.bitwise_xor(place, shift)) * chunk, 16)
            copies.append(
                pltpu.make_async_copy(
                    buffer.at[:, pl.ds(row, chunk), :], target.at[shift], sem.at[len(copies)]
                )
            )
    return copies


def send_grads(buffer, mine, theirs, sem):
    run_copies(grad_copies(buffer, mine, theirs, sem))


def send_rows(buffer, keep, theirs, sem):
    part = lax.axis_index("mp") % 2
    rows = buffer.shape[0] // 2
    copies = []
    for side, target in ((part, keep), (1 - part, theirs)):
        row = pl.multiple_of(side * rows, 16)
        copies.append(
            pltpu.make_async_copy(buffer.at[pl.ds(row, rows), :], target, sem.at[len(copies)])
        )
    run_copies(copies)


def pack_kernel(
    self_proj, self_out, cross_proj, cross_out, ffn_in, ffn_out, self_bias, cross_bias, ffn_bias, cot,
    own, own3, cot_send, small,
):
    core, place, position = mesh_place()
    for index in range(2):
        row = pl.multiple_of((1 - position % 2 + 2 * index) * TQ, TQ)
        cot_send[index * TQ : (index + 1) * TQ, :] = cot[pl.ds(row, TQ), :]
    chunk = 4 * core + place
    matrix, half = chunk // 2, chunk % 2
    for proj, out, base in ((self_proj, self_out, 0), (cross_proj, cross_out, 256 + EXT)):

        @pl.when(matrix < 3)
        def _(proj=proj, base=base):
            own[base : base + 256, :] = proj[matrix, pl.ds(pl.multiple_of(half * 256, 256), 256), :]

        @pl.when(matrix == 3)
        def _(out=out, base=base):
            block = out[:, pl.ds(pl.multiple_of(half * 256, 256), 256)]
            own[base : base + 256, :] = block.astype(F32).T.astype(BF)

    rows = [self_bias[...].astype(F32), cross_bias[...].astype(F32)]
    rows += [ffn_bias[lanes(block)].astype(F32).reshape(1, PAIR) for block in range(4)]
    rows += [jnp.zeros((8, PAIR), F32)]
    small[...] = jnp.concatenate(rows, axis=0).astype(BF)
    own[256 : 256 + EXT, :] = small[...]
    rows = own3.shape[0]
    row = chunk * rows

    @pl.when(row < D)
    def _():
        own3[...] = ffn_in[pl.ds(pl.multiple_of(row, rows), rows), :]

    @pl.when(row >= D)
    def _():
        own3[...] = ffn_out[pl.ds(pl.multiple_of(row - D, rows), rows), :]


def prep_kernel(
    dec, enc, ranks, limits, padded, out_bias, gain, shift,
    scal, mask, mask_t, hot, kaug_dec, kaug_enc, vecs, table,
):
    _, _, position = mesh_place()
    row, part = position // 2, position % 2
    length, sources = dec.shape[1], enc.shape[1]
    seg = dec[pl.ds(row, 1), :]
    seg_enc = enc[pl.ds(row, 1), :]
    place = lax.broadcasted_iota(jnp.int32, (1, length), 1)
    begins = (place == 0) | (seg != pltpu.roll(seg, 1, 1))
    rank = jnp.where(padded[pl.ds(row, 1), :] == 0, ranks[pl.ds(row, 1), :], length)
    table[...] = jnp.zeros(table.shape, F32)
    table[0:1, :] = seg.astype(F32)
    table[1:2, :] = rank.astype(F32)
    table[2:3, :] = begins.astype(F32)
    table[3:4, :] = limits[pl.ds(row, 1), :].astype(F32)
    table[4:5, :] = place.astype(F32)
    own = jnp.concatenate(
        [
            table[:, pl.ds(pl.multiple_of((2 * tile + part) * TQ, TQ), TQ)]
            for tile in range(TILES)
        ],
        axis=1,
    )
    own_t = own.T
    every = table[...]
    every_t = every.T

    def visible(seg_q, limit_q, place_q, seg_k, rank_k, start_k, place_k):
        chosen = (rank_k < limit_q) & (place_q != place_k)
        seen = (seg_q == seg_k) & ((start_k > 0.5) | chosen)
        return jnp.where(seen, 0.0, MASKED).astype(BF)

    mask[...] = visible(
        own_t[:, 0:1], own_t[:, 3:4], own_t[:, 4:5],
        every[0:1], every[1:2], every[2:3], every[4:5],
    )
    mask_t[...] = visible(
        own[0:1], own[3:4], own[4:5],
        every_t[:, 0:1], every_t[:, 1:2], every_t[:, 2:3], every_t[:, 4:5],
    )

    def key_aug(column):
        lane = lax.broadcasted_iota(jnp.int32, (column.shape[0], PAIR), 1)
        different = (lane < 4) & (column != lane.astype(F32))
        minus = (lane >= 4) & (lane < 7)
        return jnp.where(different, MASKED, jnp.where(minus, -1.0, 0.0)).astype(BF)

    kaug_dec[...] = key_aug(every_t[:, 0:1])
    seg_enc_f = jnp.broadcast_to(seg_enc.astype(F32), (8, sources))
    kaug_enc[...] = key_aug(seg_enc_f.T[:, 0:1])
    lane = lax.broadcasted_iota(jnp.int32, (OWN, PAIR), 1)
    hot[...] = (own_t[:, 0:1] == lane.astype(F32)).astype(F32).astype(BF)
    vecs[...] = jnp.zeros(vecs.shape, F32)
    for index, source in enumerate((out_bias, gain, shift)):
        vecs[3 * index : 3 * index + 3, :] = source[...].astype(F32)
    for which, keys, align in (
        (0, every[0:1], PAIR), (1, seg_enc_f[0:1], ROWS), (2, every[0:1], ROWS)
    ):
        size = keys.shape[1]
        for tile in range(TILES):
            block = own[0:1, tile * TQ : (tile + 1) * TQ]
            low, high = jnp.min(block), jnp.max(block)
            begin = jnp.sum((keys < low).astype(F32)).astype(jnp.int32)
            end = jnp.sum((keys <= high).astype(F32)).astype(jnp.int32)
            base = begin // align * align
            count = (end - base + TK - 1) // TK
            scal[which * 2 * TILES + tile] = jnp.minimum(base, size - count * TK)
            scal[which * 2 * TILES + TILES + tile] = count


def fetch(source, target, start, sem):
    return pltpu.make_async_copy(
        source.at[pl.ds(pl.multiple_of(start, target.shape[0]), target.shape[0]), :], target, sem
    )


def project(x, weight, bias, target):
    step = min(x.shape[0], 1024)
    for part in range(x.shape[0] // step):
        rows = slice(part * step, (part + 1) * step)
        value = mm(x[rows, :], weight)
        target[rows, :] = (value if bias is None else value + bias).astype(BF)


def self_forward_kernel(
    scal, query, content, mask_in, hot, kaug, vecs, small, proj, out, mine, other,
    q, k_out, v_out, qaug, ctx, exact, s1, weight_out, bias,
    score, peak, mixed, got, xq, xc, k, v, weight, mask, sem, sem_out,
):
    _, _, position = mesh_place()
    rows = xc.shape[0]
    copies = own_tiles(query, xq, sem, 32)
    copies.append(
        pltpu.make_async_copy(
            content.at[pl.ds(pl.multiple_of(position // 2 * rows, rows), rows), :], xc, sem.at[36]
        )
    )
    for pair in range(1, PAIRS):
        copies.append(
            pltpu.make_async_copy(
                mine.at[0, pair - 1, pl.ds(256, EXT), :], got.at[pair - 1], sem.at[36 + pair]
            )
        )
    late = pltpu.make_async_copy(mask_in, mask, sem.at[40])
    for copy in copies:
        copy.start()
    moves = load_weights(proj, out, mine, other, weight, sem)
    for copy in moves:
        copy.start()
    late.start()
    for copy in copies + moves:
        copy.wait()
    outs = [put(weight, weight_out, sem_out.at[0])]
    bias[:, lanes(0)] = small[...].astype(F32)
    for pair in range(1, PAIRS):
        bias[:, lanes(pair)] = got[pair - 1].astype(F32)
    q[...] = ((mm(xq[...], weight[0]) + bias[0:1, :]).astype(BF) * BF(HEAD ** (-0.5))).astype(BF)
    project(xc, weight[1], None, k)
    outs.append(put(k, k_out, sem_out.at[1]))
    project(xc, weight[2], bias[1:2, :], v)
    outs.append(put(v, v_out, sem_out.at[2]))
    late.wait()
    attend_forward(scal, 0, q, k, v, kaug, hot, mask, score, peak, mixed, qaug, ctx, exact)
    s1[...] = xq[...].astype(F32) + mm_cols(ctx[...], weight[3]) + vecs[0:1, :]
    for copy in outs:
        copy.wait()


def cross_forward_kernel(
    scal, s1, encoder, hot, kaug, vecs, bias, proj, out, mine, other,
    q, k_out, v_out, qaug, ctx, exact, s2, weight_out,
    score, peak, mixed, enc, k, v, weight, sem, sem_out,
):
    _, _, position = mesh_place()
    moves = load_weights(proj, out, mine, other, weight, sem)
    rows = enc.shape[0]
    late = pltpu.make_async_copy(
        encoder.at[pl.ds(pl.multiple_of(position // 2 * rows, rows), rows), :], enc, sem.at[32]
    )
    for copy in moves:
        copy.start()
    late.start()
    normed, _ = norm_parts(s1[...])
    first = normed * vecs[3:4, :] + vecs[6:7, :]
    for copy in moves:
        copy.wait()
    outs = [put(weight, weight_out, sem_out.at[0])]
    q[...] = (
        (mm(first.astype(BF), weight[0]) + bias[2:3, :]).astype(BF) * BF(HEAD ** (-0.5))
    ).astype(BF)
    late.wait()
    project(enc, weight[1], None, k)
    outs.append(put(k, k_out, sem_out.at[1]))
    project(enc, weight[2], bias[3:4, :], v)
    outs.append(put(v, v_out, sem_out.at[2]))
    attend_forward(scal, 1, q, k, v, kaug, hot, None, score, peak, mixed, qaug, ctx, exact)
    s2[...] = first + mm_cols(ctx[...], weight[3]) + vecs[1:2, :]
    for copy in outs:
        copy.wait()


def gelu_parts(v):
    c = math.sqrt(2.0 / math.pi)
    square = v * v
    t = jnp.tanh(c * (v + 0.044715 * square * v))
    value = 0.5 * v * (1.0 + t)
    slope = 0.5 * (1.0 + t) + 0.5 * v * (1.0 - t * t) * (c + (3.0 * 0.044715 * c) * square)
    return value, slope


def ffn_kernel(
    s2, cot_own, cot_got, bias, vecs, ffn_in, ffn_out, first_core, second_core,
    output, mine, theirs, back, sums, output_send,
    weight, hidden, slopes, low, grads, cot, sem, sem_cot,
):
    core, place, position = mesh_place()
    half = position % 2
    late = []
    for index in range(2):
        row = pl.multiple_of((half + 2 * index) * TQ, TQ)
        target = pl.multiple_of((2 * half + index) * TQ, TQ)
        late.append(
            put(cot_own.at[pl.ds(row, TQ), :], cot.at[pl.ds(target, TQ), :], sem_cot.at[index])
        )
    target = pl.multiple_of((1 - half) * 2 * TQ, 2 * TQ)
    late.append(put(cot_got, cot.at[pl.ds(target, 2 * TQ), :], sem_cot.at[2]))
    copies = [[] for _ in range(4)]
    for side, source in enumerate((ffn_in, ffn_out)):
        copies[0].append(put(source, weight.at[side, 0], sem.at[side]))
    for part in range(1, 4):
        for side, source in ((core, first_core), (1 - core, second_core)):
            for shift in range(4):
                row = pl.multiple_of(jnp.bitwise_xor(place, shift) * 128, 128)
                number = 2 + sum(len(group) for group in copies[1:])
                copies[part].append(
                    put(
                        source.at[shift, part - 1], weight.at[side, part, pl.ds(row, 128), :],
                        sem.at[number],
                    )
                )
    sums[...] = jnp.zeros(sums.shape, F32)
    normed2, inverse2 = norm_parts(s2[...])
    second = normed2 * vecs[4:5, :] + vecs[7:8, :]
    low[...] = second.astype(BF)
    total = second + vecs[2:3, :]
    def before_gelu(part):
        part_bias = jnp.concatenate([bias[4 + i : 5 + i, lanes(part)] for i in range(4)], axis=1)
        for copy in copies[part]:
            copy.wait()
        return mm(low[...], weight[0, part]) + part_bias

    ready = before_gelu(0)
    for part in range(4):
        block = slice(part * D, (part + 1) * D)
        pre = ready
        if part < 3:
            ready = before_gelu(part + 1)
        value, slope = gelu_parts(pre)
        hidden[:, block] = value.astype(BF)
        slopes[:, block] = slope
        total = total + mm(hidden[:, block], weight[1, part])
    normed3, inverse3 = norm_parts(total)
    output[...] = (normed3 * vecs[5:6, :] + vecs[8:9, :]).astype(BF)
    for copy in late:
        copy.wait()
    row = pl.multiple_of((1 - half) * 2 * TQ, 2 * TQ)
    output_send[...] = output[pl.ds(row, 2 * TQ), :]
    incoming = cot[...].astype(F32)
    sums[0:1, :] = col_sum(incoming * normed3)
    sums[1:2, :] = col_sum(incoming)
    third_grad = norm_backward(incoming, normed3, inverse3, vecs[5:6, :])
    branch = third_grad.astype(BF)
    sums[2:3, :] = col_sum(branch)
    total = third_grad
    ready = mm_cols(branch, weight[1, 0])
    for part in range(4):
        block = slice(part * D, (part + 1) * D)
        pre_grad = (slopes[:, block] * ready).astype(BF)
        if part < 3:
            ready = mm_cols(branch, weight[1, part + 1])
        sums[8 + part : 9 + part, :] = col_sum(pre_grad)
        grads[part, 0:D, :] = mm_rows(low[...], pre_grad).astype(BF)
        grads[part, D : 2 * D, :] = mm_rows(hidden[:, block], branch).astype(BF)
        if part == 3:
            moves = grad_copies(grads, mine, theirs, sem)
            for copy in moves:
                copy.start()
        total = total + mm_cols(pre_grad, weight[0, part])
    sums[3:4, :] = col_sum(total * normed2)
    sums[4:5, :] = col_sum(total)
    second_grad = norm_backward(total, normed2, inverse2, vecs[4:5, :])
    sums[5:6, :] = col_sum(second_grad.astype(BF))
    back[...] = second_grad
    for copy in moves:
        copy.wait()


def store_grad(grads, matrix, value):
    low = value.astype(BF)
    for pair in range(PAIRS):
        grads[pair, matrix * D : (matrix + 1) * D, :] = low[:, lanes(pair)]


def projection_grads(grads, x, low, matrix):
    store_grad(grads, matrix, mm_rows(x[...], low[...]))


def input_grads(dk, dv, weight, out):
    step = min(dk.shape[0], 1024)
    for part in range(dk.shape[0] // step):
        rows = slice(part * step, (part + 1) * step)
        out[rows, :] = (
            mm_cols(dk[rows, :], weight[1]) + mm_cols(dv[rows, :], weight[2])
        ).astype(BF)


def load_all(sources, targets, sem):
    copies = [
        pltpu.make_async_copy(source, target, sem.at[index])
        for index, (source, target) in enumerate(zip(sources, targets))
    ]
    for copy in copies:
        copy.start()
    return copies


def store_low(dk, dv, dk_low, dv_low, low, sem):
    copies = []
    for index, (value, target) in enumerate(((dk, dk_low), (dv, dv_low))):
        for part in range(value.shape[0] // 512):
            rows = slice(part * 512, (part + 1) * 512)
            low[index, rows, :] = value[rows, :].astype(BF)
            copies.append(put(low.at[index, rows, :], target.at[rows, :], sem.at[len(copies)]))
    return copies


def cross_attention_grad_kernel(
    scal, dss2, weight_in, q_in, k_in, v_in, qaug_in, exact_in, kaug_in,
    dq, dk_low, dv_low, keep, send,
    grad_ctx, weight, enc_grad, dk, dv, dq_tile, low, q, k, v, qaug, exact, kaug, sem,
):
    first = put(weight_in, weight, sem.at[7])
    copies = load_all(
        (q_in, qaug_in, exact_in, kaug_in, k_in, v_in), (q, qaug, exact, kaug, k, v), sem
    )
    dk[...] = jnp.zeros(dk.shape, F32)
    dv[...] = jnp.zeros(dv.shape, F32)
    first.wait()
    grad_ctx[...] = mm(dss2[...].astype(BF), weight[3]).astype(BF)
    for copy in copies:
        copy.wait()
    attend_backward(scal, 1, q, k, v, kaug, qaug, None, grad_ctx, exact, dq, dk, dv, dq_tile)
    copies = store_low(dk, dv, dk_low, dv_low, low, sem)
    input_grads(low.at[0], low.at[1], weight, enc_grad)
    for copy in copies:
        copy.wait()
    send_rows(enc_grad, keep, send, sem)


def cross_projection_grad_kernel(
    dss2, s1, weight_in, self_weight, ctx, self_ctx, dq, dk_in, dv_in, encoder, vecs, sums_in,
    mine, theirs, back, grad_ctx, sums,
    grads, enc, weight, dk, dv, sem,
):
    _, _, position = mesh_place()
    rows = enc.shape[0]
    start = pl.multiple_of(position // 2 * rows, rows)
    early = [
        put(weight_in.at[0], weight.at[0], sem.at[0]),
        put(self_weight.at[3], weight.at[1], sem.at[1]),
    ]
    late = [
        put(encoder.at[pl.ds(start, rows), :], enc, sem.at[2]),
        put(dk_in, dk, sem.at[3]),
        put(dv_in, dv, sem.at[4]),
    ]
    sums[...] = sums_in[...]
    normed, inverse = norm_parts(s1[...])
    first = (normed * vecs[3:4, :] + vecs[6:7, :]).astype(BF)
    store_grad(grads, 0, mm_rows(first, dq[...]))
    store_grad(grads, 3, mm_rows(dss2[...].astype(BF), ctx[...]))
    for copy in early:
        copy.wait()
    total = dss2[...] + mm_cols(dq[...], weight[0])
    sums[6:7, :] = col_sum(total * normed)
    sums[7:8, :] = col_sum(total)
    first_grad = norm_backward(total, normed, inverse, vecs[3:4, :])
    branch = first_grad.astype(BF)
    sums[12:13, :] = col_sum(branch)
    back[...] = first_grad
    grad_ctx[...] = mm(branch, weight[1]).astype(BF)
    store_grad(grads, 4, mm_rows(branch, self_ctx[...]))
    sums[14:15, :] = col_sum(dq[...])
    for copy in late:
        copy.wait()
    projection_grads(grads, enc, dk, 1)
    projection_grads(grads, enc, dv, 2)
    sums[15:16, :] = col_sum(dv[...])
    send_grads(grads, mine, theirs, sem)


def self_attention_grad_kernel(
    scal, grad_ctx, q_in, k_in, v_in, qaug_in, exact_in, mask_in, kaug_in, weight_in,
    dq, dk_low, dv_low, keep, send,
    dk, dv, dq_tile, low, q, k, v, qaug, exact, mask_t, kaug, sem, weight, content_grad,
):
    late = put(weight_in.at[1:3], weight.at[1:3], sem.at[7])
    copies = load_all(
        (q_in, qaug_in, exact_in, kaug_in, k_in, v_in, mask_in),
        (q, qaug, exact, kaug, k, v, mask_t),
        sem,
    )
    dk[...] = jnp.zeros(dk.shape, F32)
    dv[...] = jnp.zeros(dv.shape, F32)
    for copy in copies:
        copy.wait()
    attend_backward(scal, 2, q, k, v, kaug, qaug, mask_t, grad_ctx, exact, dq, dk, dv, dq_tile)
    late.wait()
    copies = store_low(dk, dv, dk_low, dv_low, low, sem)
    input_grads(low.at[0], low.at[1], weight, content_grad)
    half = lax.axis_index("mp") % 2
    mid = content_grad.shape[0] // 2
    keep[...] = content_grad[pl.ds(pl.multiple_of(half * mid, mid), mid), :]
    send[...] = content_grad[pl.ds(pl.multiple_of((1 - half) * mid, mid), mid), :]
    for copy in copies:
        copy.wait()


def self_projection_grad_kernel(
    fsg, weight_in, dq, dk, dv, query, content, sums,
    mine, theirs, send, query_grad,
    grads, xq, xc, weight, sem, sem_late,
):
    _, _, position = mesh_place()
    half = position % 2
    rows = xc.shape[0]
    copies = own_tiles(query, xq, sem, 0)
    for copy in copies:
        copy.start()
    place = pl.multiple_of(position // 2 * rows, rows)
    content_copy = put(content.at[pl.ds(place, rows), :], xc, sem_late.at[0])
    weight_copy = put(weight_in.at[0], weight, sem_late.at[1])
    for copy in copies:
        copy.wait()
    store_grad(grads, 0, mm_rows(xq[...], dq[...]))
    content_copy.wait()
    projection_grads(grads, xc, dk, 1)
    projection_grads(grads, xc, dv, 2)
    bias_q = col_sum(dq[...])
    bias_v = col_sum(dv[...])
    for pair in range(PAIRS):
        parts = [bias_q[:, lanes(pair)], bias_v[:, lanes(pair)]]
        parts += [sums[14:15, lanes(pair)], sums[15:16, lanes(pair)]]
        parts += [sums[8 + pair : 9 + pair, lanes(i)] for i in range(4)]
        for index in (0, 1, 2, 3, 4, 5, 6, 7, 12):
            parts += [sums[index : index + 1, lanes(i)] for i in range(4)]
        parts += [jnp.zeros((SUB * EXT - len(parts), PAIR), F32)]
        grads[pair, 3 * D : 3 * D + SUB * EXT, :] = jnp.concatenate(parts, axis=0).astype(BF)
    moves = grad_copies(grads, mine, theirs, sem)
    for copy in moves:
        copy.start()
    weight_copy.wait()
    query_grad[...] = (fsg[...] + mm_cols(dq[...], weight[...])).astype(BF)
    row = pl.multiple_of((1 - half) * 2 * TQ, 2 * TQ)
    send[...] = query_grad[pl.ds(row, 2 * TQ), :]
    for copy in moves:
        copy.wait()


def add_split_kernel(mine, theirs, *outs):
    for index, out in enumerate(outs):
        out[...] = (mine[index].astype(F32) + theirs[index].astype(F32)).astype(BF)


def sum_split_kernel(own, first, second, third, *outs):
    for index, out in enumerate(outs):
        out[...] = (
            (own[index].astype(F32) + first[index].astype(F32))
            + (second[index].astype(F32) + third[index].astype(F32))
        ).astype(BF)


def sum_merge_kernel(a0, a1, a2, a3, b0, b1, b2, b3, *outs):
    rows = a0.shape[1]
    for index, out in enumerate(outs):
        for group, spot in (((a0, a1, a2, a3), slice(0, rows)), ((b0, b1, b2, b3), slice(rows, None))):
            own, first, second, third = [part[index].astype(F32) for part in group]
            out[spot, :] = ((own + first) + (second + third)).astype(BF)


def sum_kernel(own, first, second, third, out):
    out[...] = (
        (own[...].astype(F32) + first[...].astype(F32))
        + (second[...].astype(F32) + third[...].astype(F32))
    ).astype(out.dtype)


def finish_ffn_kernel(line, other, ffn_in, ffn_out, wide):
    core, place, _ = mesh_place()
    for side, source in ((core, line), (1 - core, other)):
        for shift in range(4):
            row = pl.multiple_of((4 * side + jnp.bitwise_xor(place, shift)) * 128, 128)
            wide[pl.ds(row, 128), :] = source[shift].astype(F32)
    ffn_in[...] = wide[0:D, :]
    ffn_out[...] = wide[D:, :]


def finish_rows_kernel(
    output_own, output_got, query_own, query_got, keep, got, output, query, content
):
    _, _, position = mesh_place()
    half = position % 2
    for own, theirs, target in (
        (output_own, output_got, output), (query_own, query_got, query)
    ):
        for index in range(2):
            row = pl.multiple_of((2 * half + index) * TQ, TQ)
            place_own = pl.multiple_of((half + 2 * index) * TQ, TQ)
            place_got = pl.multiple_of((1 - half + 2 * index) * TQ, TQ)
            first = index * TQ
            target[pl.ds(place_own, TQ), :] = own[pl.ds(row, TQ), :]
            target[pl.ds(place_got, TQ), :] = theirs[first : first + TQ, :]
    content[...] = (keep[...].astype(F32) + got[...].astype(F32)).astype(BF)


def finish_kernel(
    line, other,
    self_proj, self_bias, self_out, cross_proj, cross_bias, cross_out, ffn_bias,
    out_bias, gain, moved, flat, flat_self,
):
    core, place, _ = mesh_place()
    cross_rows, self_rows = flat.shape[0] // SUB, flat_self.shape[0] // SUB
    for side, source in ((core, line), (1 - core, other)):
        for shift in range(4):
            spot = 4 * side + jnp.bitwise_xor(place, shift)
            row = pl.multiple_of(spot * cross_rows, 8)
            flat[pl.ds(row, cross_rows), :] = source[shift, 0:cross_rows, :].astype(F32)
            row = pl.multiple_of(spot * self_rows, 8)
            flat_self[pl.ds(row, self_rows), :] = source[shift, cross_rows:, :].astype(F32)
    for matrix in range(3):
        cross_proj[matrix] = flat[matrix * D : (matrix + 1) * D, :]
        self_proj[matrix] = flat_self[matrix * D : (matrix + 1) * D, :]
    cross_out[...] = flat[3 * D : 4 * D, :].T
    self_out[...] = flat[4 * D : 5 * D, :].T
    start = 3 * D
    self_bias[...] = flat_self[start : start + 2, :]
    cross_bias[...] = flat_self[start + 2 : start + 4, :]
    for block in range(4):
        ffn_bias[:, lanes(block)] = flat_self[start + 4 + block : start + 5 + block, :]
    for target, order in ((out_bias, (8, 5, 2)), (gain, (6, 3, 0)), (moved, (7, 4, 1))):
        for index, number in enumerate(order):
            for block in range(4):
                row = start + 8 + number * 4 + block
                target[index : index + 1, lanes(block)] = flat_self[row : row + 1, :]


def call(kernel, outs, inputs, scratch=(), smem_in=(), any_in=(), any_out=(), smem_out=(), long=False):
    def space(index, smem, hbm):
        return pltpu.SMEM if index in smem else pl.ANY if index in hbm else pltpu.VMEM

    return pl.pallas_call(
        kernel,
        out_shape=[jax.ShapeDtypeStruct(shape, dtype) for shape, dtype in outs],
        in_specs=[
            pl.BlockSpec(memory_space=space(index, smem_in, any_in)) for index in range(len(inputs))
        ],
        out_specs=[
            pl.BlockSpec(memory_space=space(index, smem_out, any_out)) for index in range(len(outs))
        ],
        scratch_shapes=list(scratch),
        compiler_params=pltpu.CompilerParams(vmem_limit_bytes=VMEM_LIMIT),
        cost_estimate=pl.CostEstimate(
            flops=10**13 if long else 10**6, bytes_accessed=1 << (30 if long else 14),
            transcendentals=0,
        ),
    )(*inputs)


def after(value, *others):
    flat, tree = jax.tree.flatten(value)
    tied = lax.optimization_barrier(tuple(flat) + tuple(others))
    return jax.tree.unflatten(tree, tied[: len(flat)])


def body(
    query_stream, content_stream, encoder, dec_segments, enc_segments, key_rank, observe_limit,
    padding, self_proj, self_bias, self_out, cross_proj, cross_bias, cross_out, ffn_in,
    ffn_in_bias, ffn_out, out_bias, norm_gain, norm_bias, cotangent,
):
    members = lax.axis_size("mp")
    groups = lax.axis_size("dp")
    length = dec_segments.shape[1]
    sources = enc_segments.shape[1]
    DMA = pltpu.SemaphoreType.DMA

    def swap(value, axis, mask):
        size = members if axis == "mp" else groups
        return lax.ppermute(value, axis, [(i, i ^ mask) for i in range(size)])

    def along(values):
        return [swap(value, "mp", shift + 1) for shift, value in enumerate(values)]

    def across(values):
        return [swap(value, "dp", 2 * shift + 2) for shift, value in enumerate(values)]

    own12, own3, cot_send, small = call(
        pack_kernel,
        [
            ((512 + EXT, PAIR), BF), ((2 * D // SUB, D), BF), ((2 * TQ, D), BF),
            ((EXT, PAIR), BF),
        ],
        (
            self_proj, self_out, cross_proj, cross_out, ffn_in, ffn_out, self_bias, cross_bias,
            ffn_in_bias, cotangent,
        ),
    )
    line12 = along([own12] * 3)
    scal, mask, mask_t, hot, kaug_dec, kaug_enc, vecs = call(
        prep_kernel,
        [
            ((6 * TILES,), jnp.int32), ((OWN, length), BF), ((length, OWN), BF),
            ((OWN, PAIR), BF), ((length, PAIR), BF), ((sources, PAIR), BF), ((EXT, D), F32),
        ],
        (
            dec_segments, enc_segments, key_rank, observe_limit, padding, out_bias, norm_gain,
            norm_bias,
        ),
        [pltpu.VMEM((8, length), F32)],
        smem_out=(0,),
    )
    line12, hot = after((line12, hot))
    line1 = jnp.stack([value[: 256 + EXT] for value in line12])
    line2 = jnp.stack([value[256 + EXT :] for value in line12])
    plane1, line3 = after((across([line1] * 3), along([after(own3, line1)] * 3)))
    plane1 = jnp.stack([line1] + plane1)
    line3 = jnp.stack(line3)
    other1 = swap(plane1, "dp", 1)
    cot_got = swap(after(cot_send, line1), "mp", 1)
    plane2 = across([after(line2, plane1)] * 3)

    def attention_outs(keys):
        return [
            ((OWN, D), BF), ((keys, D), BF), ((keys, D), BF), ((2 * PAIRS, OWN, PAIR), BF),
            ((OWN, D), BF), ((OWN, D), F32), ((OWN, D), F32), ((4, D, D), BF),
        ]

    def attention_scratch(keys):
        return [
            pltpu.VMEM((PAIRS, 2 * TQ, keys), F32), pltpu.VMEM((PAIRS, 2 * TQ, PAIR), F32),
            pltpu.VMEM((PAIRS, 2 * TQ, 2 * PAIR), F32),
        ]

    def backward_scratch(keys, masked=False):
        shapes = [
            pltpu.VMEM((keys, D), F32), pltpu.VMEM((keys, D), F32),
            pltpu.VMEM((PAIRS, 2 * TQ, PAIR), F32), pltpu.VMEM((2, keys, D), BF),
            pltpu.VMEM((OWN, D), BF), pltpu.VMEM((keys, D), BF), pltpu.VMEM((keys, D), BF),
            pltpu.VMEM((2 * PAIRS, OWN, PAIR), BF), pltpu.VMEM((OWN, D), F32),
        ]
        if masked:
            shapes.append(pltpu.VMEM((keys, OWN), BF))
        return shapes + [pltpu.VMEM((keys, PAIR), BF), DMA((8,))]

    q1, k1, v1, qaug1, ctx1, exact1, s1, weight1, bias = call(
        self_forward_kernel,
        attention_outs(length) + [((EXT, D), F32)],
        (
            scal, query_stream, content_stream, mask, hot, kaug_dec, vecs, small, self_proj,
            self_out, plane1, other1,
        ),
        attention_scratch(length)
        + [
            pltpu.VMEM((PAIRS - 1, EXT, PAIR), BF), pltpu.VMEM((OWN, D), BF),
            pltpu.VMEM((length, D), BF), pltpu.VMEM((length, D), BF), pltpu.VMEM((length, D), BF),
            pltpu.VMEM((4, D, D), BF), pltpu.VMEM((OWN, length), BF), DMA((41,)), DMA((3,)),
        ],
        smem_in=(0,), any_in=(1, 2, 3, 8, 10, 11), any_out=(1, 2, 7),
    )
    plane2, s1, cot_got = after((plane2, s1, cot_got))
    plane2 = jnp.stack([line2] + plane2)
    plane3 = across([after(line3, plane2)] * 3)
    other2 = swap(plane2, "dp", 1)
    q2, k2, v2, qaug2, ctx2, exact2, s2, weight2 = call(
        cross_forward_kernel,
        attention_outs(sources),
        (
            scal, s1, encoder, hot, kaug_enc, vecs, bias, cross_proj, cross_out, plane2, other2,
        ),
        attention_scratch(sources)
        + [
            pltpu.VMEM((sources, D), BF), pltpu.VMEM((sources, D), BF), pltpu.VMEM((sources, D), BF),
            pltpu.VMEM((4, D, D), BF), DMA((33,)), DMA((3,)),
        ],
        smem_in=(0,), any_in=(2, 7, 9, 10), any_out=(1, 2, 7),
    )
    plane3, s2 = after((plane3, s2))
    plane3 = jnp.stack([line3] + plane3)
    other3 = swap(plane3, "dp", 1)

    def group_outs(rows, width):
        return [((4, 4, rows // SUB, width), BF)] * 2

    output_own, mine3, theirs3, dss2, sums, output_send = call(
        ffn_kernel,
        [((OWN, D), BF)]
        + group_outs(2 * D, D)
        + [((OWN, D), F32), ((EXT, D), F32), ((2 * TQ, D), BF)],
        (s2, cotangent, cot_got, bias, vecs, ffn_in, ffn_out, plane3, other3),
        [
            pltpu.VMEM((2, 4, D, D), BF), pltpu.VMEM((OWN, 4 * D), BF),
            pltpu.VMEM((OWN, 4 * D), F32), pltpu.VMEM((OWN, D), BF), pltpu.VMEM((4, 2 * D, D), BF),
            pltpu.VMEM((OWN, D), BF), DMA((26,)), DMA((3,)),
        ],
        any_in=(1, 2, 5, 6, 7, 8), any_out=(1, 2),
    )

    def low_sum(*values):
        total = values[0].astype(F32)
        for value in values[1:]:
            total = total + value.astype(F32)
        return total.astype(BF)

    def add_split(mine, theirs):
        return [low_sum(mine[index], theirs[index]) for index in range(4)]

    def sum_split(parts):
        return [low_sum(*[part[index] for part in parts]) for index in range(4)]

    def sum_parts(parts):
        piece = parts[0].astype(F32)
        for part in parts[1:]:
            piece = piece + part.astype(F32)
        bit = SUB
        while bit < groups:
            piece = piece + swap(piece, "dp", bit)
            bit *= 2
        return piece.astype(BF)

    theirs3 = swap(theirs3, "dp", 1)
    dq2, dk2, dv2, enc_keep, enc_send = call(
        cross_attention_grad_kernel,
        [((OWN, D), BF), ((sources, D), BF), ((sources, D), BF)] + [((sources // 2, D), BF)] * 2,
        (scal, dss2, weight2, q2, k2, v2, qaug2, exact2, kaug_enc),
        [pltpu.VMEM((OWN, D), BF), pltpu.VMEM((4, D, D), BF), pltpu.VMEM((sources, D), BF)]
        + backward_scratch(sources),
        smem_in=(0,), any_in=(2, 3, 4, 5, 6, 7, 8), any_out=(1, 2, 3, 4), long=True,
    )
    output_got = swap(output_send, "mp", 1)
    theirs3, dq2, output_got = after((theirs3, dq2, output_got))
    parts3 = add_split(mine3, theirs3)
    dq2 = after(dq2, parts3[0])
    moved3 = across(parts3[1:])
    enc_theirs = swap(enc_send, "mp", 1)
    mine2, theirs2, fsg, grad_ctx1, sums = call(
        cross_projection_grad_kernel,
        group_outs(5 * D, PAIR) + [((OWN, D), F32), ((OWN, D), BF), ((EXT, D), F32)],
        (dss2, s1, weight2, weight1, ctx2, ctx1, dq2, dk2, dv2, encoder, vecs, sums),
        [
            pltpu.VMEM((PAIRS, 5 * D, PAIR), BF), pltpu.VMEM((sources, D), BF),
            pltpu.VMEM((2, D, D), BF), pltpu.VMEM((sources, D), BF), pltpu.VMEM((sources, D), BF),
            DMA((8,)),
        ],
        any_in=(2, 3, 7, 8, 9), any_out=(0, 1), long=True,
    )
    theirs2 = swap(theirs2, "dp", 1)
    dq1, dk1, dv1, content_keep, content_send = call(
        self_attention_grad_kernel,
        [((OWN, D), BF), ((length, D), BF), ((length, D), BF)] + [((length // 2, D), BF)] * 2,
        (scal, grad_ctx1, q1, k1, v1, qaug1, exact1, mask_t, kaug_dec, weight1),
        backward_scratch(length, True)
        + [pltpu.VMEM((4, D, D), BF), pltpu.VMEM((length, D), BF)],
        smem_in=(0,), any_in=(2, 3, 4, 5, 6, 7, 8, 9), any_out=(1, 2), long=True,
    )
    content_got = swap(content_send, "mp", 1)
    moved3, theirs2, enc_theirs, dq1 = after((moved3, theirs2, enc_theirs, dq1))
    slots3 = sum_split([parts3[0]] + moved3)
    parts2 = add_split(mine2, theirs2)
    dq1 = after(dq1, slots3[0], parts2[0])
    moved_slots3 = along(slots3[1:])
    moved2 = across(parts2[1:])
    mine1, theirs1, rows_send, query_own = call(
        self_projection_grad_kernel,
        group_outs(3 * D + SUB * EXT, PAIR)
        + [((2 * TQ, D), BF), ((OWN, D), BF)],
        (fsg, weight1, dq1, dk1, dv1, query_stream, content_stream, sums),
        [
            pltpu.VMEM((PAIRS, 3 * D + SUB * EXT, PAIR), BF),
            pltpu.VMEM((OWN, D), BF), pltpu.VMEM((length, D), BF), pltpu.VMEM((D, D), BF),
            DMA((8,)), DMA((2,)),
        ],
        any_in=(1, 5, 6), any_out=(0, 1), long=True,
    )
    theirs1, moved_slots3, moved2 = after((theirs1, moved_slots3, moved2))
    theirs1 = swap(theirs1, "dp", 1)
    rows_got = swap(rows_send, "mp", 1)
    parts1 = add_split(mine1, theirs1)
    moved1 = across(parts1[1:])
    piece3 = sum_parts([slots3[0]] + moved_slots3)
    encoder_grad = (enc_keep.astype(F32) + enc_theirs.astype(F32)).astype(BF)
    moved1, content_got = after((moved1, content_got))
    slots = [
        jnp.concatenate(both, axis=0)
        for both in zip(sum_split([parts2[0]] + moved2), sum_split([parts1[0]] + moved1))
    ]
    moved_slots = along(slots[1:])
    ffn_line = across([after(piece3, slots[0])] * 3)
    moved_slots, ffn_line, encoder_grad, rows_got = after(
        (moved_slots, ffn_line, encoder_grad, rows_got)
    )
    piece = sum_parts([slots[0]] + moved_slots)
    ffn_line = jnp.stack([piece3] + ffn_line)
    ffn_other = swap(ffn_line, "dp", 1)
    output, query_grad, content_grad = call(
        finish_rows_kernel,
        [((OWN, D), BF), ((OWN, D), BF), ((length // 2, D), BF)],
        (output_own, output_got, query_own, rows_got, content_keep, content_got),
    )
    line, ffn_other, content_grad = after((across([piece] * 3), ffn_other, content_grad))
    line = jnp.stack([piece] + line)
    other = swap(line, "dp", 1)
    ffn_in_grad, ffn_out_grad = call(
        finish_ffn_kernel,
        [((D, D), F32), ((D, D), F32)],
        (ffn_line, ffn_other),
        [pltpu.VMEM((2 * D, D), F32)],
    )

    (
        self_proj_grad, self_bias_grad, self_out_grad, cross_proj_grad, cross_bias_grad,
        cross_out_grad, ffn_bias_grad, out_bias_grad,
        gain_grad, shift_grad,
    ) = call(
        finish_kernel,
        [
            ((3, D, PAIR), F32), ((2, PAIR), F32), ((PAIR, D), F32), ((3, D, PAIR), F32),
            ((2, PAIR), F32), ((PAIR, D), F32), ((1, D), F32),
            ((3, D), F32), ((3, D), F32), ((3, D), F32),
        ],
        (line, other),
        [
            pltpu.VMEM((5 * D, PAIR), F32), pltpu.VMEM((3 * D + SUB * EXT, PAIR), F32),
        ],
    )
    return (
        output,
        query_grad,
        content_grad,
        encoder_grad,
        self_proj_grad,
        self_bias_grad,
        self_out_grad,
        cross_proj_grad,
        cross_bias_grad,
        cross_out_grad,
        ffn_in_grad,
        ffn_bias_grad.reshape(D),
        ffn_out_grad,
        out_bias_grad,
        gain_grad,
        shift_grad,
    )


def solution(mesh):
    return jax.shard_map(
        body,
        mesh=mesh,
        in_specs=(
            P("dp", None), P("dp", None), P("dp", None), P("dp", None), P("dp", None),
            P("dp", None), P("dp", None), P("dp", None), P(None, None, "mp"), P(None, "mp"),
            P("mp", None), P(None, None, "mp"), P(None, "mp"), P("mp", None), P(None, "mp"),
            P("mp"), P("mp", None), P(), P(), P(), P(("dp", "mp"), None),
        ),
        out_specs=(
            P(("dp", "mp"), None), P(("dp", "mp"), None), P(("dp", "mp"), None),
            P(("dp", "mp"), None), P(None, None, "mp"), P(None, "mp"), P("mp", None),
            P(None, None, "mp"), P(None, "mp"), P("mp", None), P(None, "mp"), P("mp"),
            P("mp", None), P(), P(), P(),
        ),
        check_vma=False,
    )
```
